128 devices in a mesh: bx: 8 (over z_hi, y), by: 16 (over x, z_lo, core).
Axes of the slice: x: 4, y: 4, z: 4 (z_hi: 2, z_lo: 2; z = z_hi * 2 + z_lo), core: 2. Of those that a mesh axis runs over, the one named last changes fastest.
Arguments:
- tracers: float32 [4, 60, 192, 2048], P(None, None, 'bx', 'by'), may hold values from -40 to 40
- rates: float32 [4, 60, 192, 2048], P(None, None, 'bx', 'by'), may hold values from 0.02 to 0.24
- column_order: int32 [128, 3072], P(('bx', 'by')), may hold values from 0 to 3071, as said below
- norm_gain: float32 [240], replicated, may hold values from 0.25 to 1.75
- norm_shift: float32 [240], replicated, may hold values from -3 to 3
- weight_first: bfloat16 [512, 240], replicated, may hold values from -0.375 to 0.375
- weight_hidden: bfloat16 [3, 512, 512], replicated, may hold values from -0.25 to 0.25
- weight_last: bfloat16 [240, 512], replicated, may hold values from -0.25 to 0.25
- bias_hidden: float32 [4, 512], replicated, may hold values from -3 to 3
- bias_last: float32 [240], replicated, may hold values from -3 to 3
Outputs:
- new_tracers: float32 [4, 60, 192, 2048], P(None, None, 'bx', 'by')
The draws below stay inside these ranges and needn't reach their ends.
Inputs may be any that keep to these rules, and one draw needn't show every extreme that they name: `column_order`: each row is a permutation of the block's 3072 columns.
All inputs are finite; a program needn't handle non-finite values.
Results may differ from the reference program's by a relative error of at most 0.0023.
Values may be sent and summed in bfloat16 or wider, within the bound.
No kernel may reach another device: no remote copies, remote signals or barrier semaphores. Data moves between devices by JAX's collectives and lax.ppermute only.
A program may use at most 128 MiB of HBM per device.

```python
import math
import jax
import jax.numpy as jnp
from jax import lax

F = 4
LEV = 60
WIDTH = 512
CX = 24
CY = 128
NX = 192
NY = 2048
COL_DEV = 3072
N_BX = 8
N_BY = 16
DEVICES = 128


def shared_order(key):
    order_key = jax.random.fold_in(key, 23)
    keys = jax.random.split(order_key, DEVICES)

    def one_row(row_key):
        return jax.random.permutation(row_key, COL_DEV).astype(jnp.int32)
    return jax.vmap(one_row)(keys)


def draw_column_order(key, part):
    return shared_order(key)


def draw_tracers(key, part):
    order = shared_order(key)
    key = jax.random.fold_in(key, 11)
    first, second, third, fourth, fifth = jax.random.split(key, 5)
    positions = jnp.arange(COL_DEV, dtype=jnp.int32)
    group_size = COL_DEV // DEVICES

    def batch_row(row):
        return jnp.zeros((COL_DEV,), jnp.int32).at[row].set(positions // group_size)
    batch_ids = jax.vmap(batch_row)(order)
    batch_grid = batch_ids.reshape(N_BX, N_BY, CX, CY).transpose(0, 2, 1, 3).reshape(NX, NY)
    cell_scale = jnp.exp(jax.random.uniform(second, (1, 1, NX, NY), jnp.float32, math.log(0.3), math.log(3.0)))
    field_scale = jnp.exp(jax.random.uniform(third, (F, LEV, 1, 1), jnp.float32, math.log(0.5), math.log(2.0)))
    batch_scale = jnp.exp(jax.random.uniform(fourth, (F, LEV, DEVICES), jnp.float32, math.log(0.5), math.log(2.0)))
    batch_offset = jax.random.uniform(fifth, (F, LEV, DEVICES), jnp.float32, -1.5, 1.5)
    spread_here = batch_scale[:, :, batch_grid]
    offset_here = batch_offset[:, :, batch_grid]
    base = jax.random.truncated_normal(first, -3.0, 3.0, (F, LEV, NX, NY), jnp.float32)
    return base * cell_scale * field_scale * spread_here + offset_here


def block_scale(rng, shape, cuts, least, largest):
    gain, own = 1.0, jax.random.fold_in(rng, 6)
    for axis_at, parts in cuts:
        heights = jnp.exp(jax.random.uniform(jax.random.fold_in(own, axis_at), (parts,), jnp.float32, least / len(cuts), largest / len(cuts)))
        gain = gain * jnp.repeat(heights, shape[axis_at] // parts).reshape([-1 if axis == axis_at else 1 for axis in range(len(shape))])
    return gain


def normal_values(rng, dims, width, most, held_as=jnp.bfloat16):
    drawn = width * jax.random.normal(rng, dims, jnp.float32)
    return jnp.clip(drawn, min=-most, max=most).astype(held_as)


def setup_inputs(seed: int = 0) -> dict:
    seeds = jax.random.split(jax.random.key(seed), 11)
    return {
        "tracers": draw_tracers(jax.random.fold_in(seeds[10], 71), 0),
        "rates": jnp.clip(0.02 + 0.22 * jax.random.uniform(seeds[1], (4, LEV, NX, NY), jnp.float32) ** block_scale(seeds[1], (4, LEV, NX, NY), ((2, 8), (3, 16)), -0.2, 0.2), 0.02, 0.24),
        "column_order": draw_column_order(jax.random.fold_in(seeds[10], 71), 0),
        "norm_gain": jnp.clip(1.0 + 0.15 * jax.random.normal(seeds[3], (F * LEV,), jnp.float32), 0.25, 1.75),
        "norm_shift": normal_values(seeds[4], (F * LEV,), 0.5, 3.0, jnp.float32),
        "weight_first": normal_values(seeds[5], (WIDTH, F * LEV), (F * LEV) ** -0.5, 0.375),
        "weight_hidden": normal_values(seeds[6], (3, WIDTH, WIDTH), WIDTH ** -0.5, 0.25),
        "weight_last": normal_values(seeds[7], (F * LEV, WIDTH), WIDTH ** -0.5, 0.25),
        "bias_hidden": normal_values(seeds[8], (4, WIDTH), 0.5, 3.0, jnp.float32),
        "bias_last": normal_values(seeds[9], (F * LEV,), 0.5, 3.0, jnp.float32),
    }


def advance(tracer, rates):
    eastern = jnp.roll(tracer, -1, axis=2)
    western = jnp.roll(tracer, 1, axis=2)
    northern = jnp.roll(tracer, -1, axis=3)
    southern = jnp.roll(tracer, 1, axis=3)
    return tracer + rates[0] * (eastern - tracer) + rates[1] * (western - tracer) + rates[2] * (northern - tracer) + rates[3] * (southern - tracer)

def network(features, norm_gain, norm_shift, weight_first, weight_hidden, weight_last, bias_hidden, bias_last):
    values = features.astype(jnp.float32)
    average = lax.optimization_barrier(jnp.mean(values, axis=1, keepdims=True))
    centred = values - average
    variance = lax.optimization_barrier(jnp.mean(centred * centred, axis=1, keepdims=True))
    normed = (centred * lax.rsqrt(variance + 1e-05) * norm_gain[:, None] + norm_shift[:, None]).astype(jnp.bfloat16)
    hidden = jax.nn.silu(jnp.dot(weight_first, normed, preferred_element_type=jnp.float32) + bias_hidden[0][:, None]).astype(jnp.bfloat16)
    for inner in range(3):
        hidden = jax.nn.silu(jnp.dot(weight_hidden[inner], hidden, preferred_element_type=jnp.float32) + bias_hidden[inner + 1][:, None]).astype(jnp.bfloat16)
    return (jnp.dot(weight_last, hidden, preferred_element_type=jnp.float32) + bias_last[:, None]).astype(jnp.bfloat16)

def reference(tracers, rates, column_order, norm_gain, norm_shift, weight_first, weight_hidden, weight_last, bias_hidden, bias_last):
    moved = advance(advance(tracers, rates), rates)
    flat = F * LEV
    count = N_BX * N_BY
    share = COL_DEV // count
    blocks = moved.reshape(flat, N_BX, CX, N_BY, CY).transpose(1, 3, 0, 2, 4).reshape(count, flat, COL_DEV).astype(jnp.bfloat16)
    ordered = jnp.take_along_axis(blocks, column_order[:, None, :], axis=2)
    batched = ordered.reshape(count, flat, count, share).transpose(2, 1, 0, 3).reshape(count, flat, COL_DEV)

    def apply_net(features):
        return network(features, norm_gain, norm_shift, weight_first, weight_hidden, weight_last, bias_hidden, bias_last)
    tendency = lax.map(apply_net, batched)
    returned = tendency.reshape(count, flat, count, share).transpose(2, 1, 0, 3).reshape(count, flat, COL_DEV)

    def place(values, order):
        return jnp.zeros_like(values).at[:, order].set(values)
    placed = jax.vmap(place)(returned, column_order)
    regridded = placed.reshape(N_BX, N_BY, F, LEV, CX, CY).transpose(2, 3, 0, 4, 1, 5).reshape(F, LEV, NX, NY)
    return moved + regridded.astype(jnp.float32)
```

```python
import functools

import jax
import jax.numpy as jnp
from jax import lax
from jax.experimental import pallas as pl
from jax.experimental.pallas import tpu as pltpu
from jax.sharding import PartitionSpec as P

FIELDS = 4
LEVELS = 60
CHUNKS = 8
ROWS = 24
COLS = 128
FEATS = 256
HALF = ROWS // 2
MIB = 1 << 20
NT = (((1,), (1,)), ((), ()))
NN = (((1,), (0,)), ((), ()))


def params(limit=32):
    return pltpu.CompilerParams(
        dimension_semantics=("arbitrary",), vmem_limit_bytes=limit * MIB
    )


def lanes_of(shape):
    return lax.broadcasted_iota(jnp.int32, shape, 1)


def valid_rows(chunk):
    level = chunk * 8 + lax.broadcasted_iota(jnp.int32, (8, COLS), 0)
    return level < LEVELS


class ColumnPacker:
    def __init__(self):
        self.pair = lanes_of((8, COLS)) // 2
        self.halves = [jnp.zeros((8, COLS), jnp.float32) for _ in range(2)]

    def add(self, i, f, tile):
        m = 4 * (i % HALF) + f
        moved = pltpu.roll(tile, 2 * m + 1, axis=1)
        self.halves[i // HALF] = jnp.where(self.pair == m, moved, self.halves[i // HALF])

    def store(self, ref):
        for h in range(2):
            ref[:, COLS * h : COLS * (h + 1)] = self.halves[h]


def pack_kernel(x_ref, q_ref, first_ref, last_ref, cols_ref):
    valid = valid_rows(pl.program_id(0))
    packer = ColumnPacker()
    for i in range(ROWS):
        for f in range(FIELDS):
            tile = jnp.where(valid, x_ref[f, pl.ds(i, 8, stride=ROWS), :], 0.0)
            q_ref[i, 8 * f : 8 * f + 8, :] = tile
            if i == 0:
                first_ref[8 * f : 8 * f + 8, :] = tile
            if i == ROWS - 1:
                last_ref[8 * f : 8 * f + 8, :] = tile
            packer.add(i, f, tile)
    packer.store(cols_ref)


def advance_tiles(q_ref, rates_ref, up_ref, down_ref, left_ref, right_ref, emit):
    valid = valid_rows(pl.program_id(0))
    lane = lanes_of((8, COLS))
    even = lane % 2 == 0
    ring = []
    for h in range(2):
        part = slice(COLS * h, COLS * (h + 1))
        ring.append(
            jnp.where(
                even,
                pltpu.roll(right_ref[:, part], COLS - 1, axis=1),
                pltpu.roll(left_ref[:, part], 1, axis=1),
            )
        )
    for i in range(ROWS):
        rate = [rates_ref[k, pl.ds(i, 8, stride=ROWS), :] for k in range(4)]
        for f in range(FIELDS):
            rows = slice(8 * f, 8 * f + 8)
            m = 4 * (i % HALF) + f
            here = q_ref[i, rows, :]
            above = up_ref[rows, :] if i == 0 else q_ref[i - 1, rows, :]
            below = down_ref[rows, :] if i == ROWS - 1 else q_ref[i + 1, rows, :]
            edge = pltpu.roll(ring[i // HALF], COLS - (2 * m + 1), axis=1)
            after = jnp.where(lane == COLS - 1, edge, pltpu.roll(here, COLS - 1, axis=1))
            before = jnp.where(lane == 0, edge, pltpu.roll(here, 1, axis=1))
            new = (
                here
                + rate[0] * (below - here)
                + rate[1] * (above - here)
                + rate[2] * (after - here)
                + rate[3] * (before - here)
            )
            emit(i, f, jnp.where(valid, new, 0.0))


def first_kernel(
    q_ref, rates_ref, up_ref, down_ref, left_ref, right_ref, out_ref, first_ref, last_ref, cols_ref
):
    packer = ColumnPacker()

    def emit(i, f, tile):
        out_ref[i, 8 * f : 8 * f + 8, :] = tile
        if i == 0:
            first_ref[8 * f : 8 * f + 8, :] = tile
        if i == ROWS - 1:
            last_ref[8 * f : 8 * f + 8, :] = tile
        packer.add(i, f, tile)

    advance_tiles(q_ref, rates_ref, up_ref, down_ref, left_ref, right_ref, emit)
    packer.store(cols_ref)


def second_kernel(
    share,
    q_ref,
    rates_ref,
    up_ref,
    down_ref,
    left_ref,
    right_ref,
    hot_ref,
    batch_ref,
    out_ref,
    stats_ref,
    x_ref,
    hi_ref,
    lo_ref,
):
    chunk = pl.program_id(0)
    kept = {}

    def emit(i, f, tile):
        out_ref[i, 8 * f : 8 * f + 8, :] = tile
        kept[f] = tile
        if f % 2 == 1:
            both = jnp.concatenate([kept[f - 1], tile], axis=0).astype(jnp.bfloat16)
            start = pl.multiple_of(32 * chunk + 8 * (f - 1), 16)
            x_ref[pl.ds(start, 16), COLS * i : COLS * (i + 1)] = both

    advance_tiles(q_ref, rates_ref, up_ref, down_ref, left_ref, right_ref, emit)

    @pl.when(chunk == CHUNKS - 1)
    def _():
        hot = hot_ref[...]
        sums = lax.dot_general(x_ref[...], hot, NT, preferred_element_type=jnp.float32)
        mean = sums * (1.0 / share)
        for i in range(ROWS):
            part = slice(COLS * i, COLS * (i + 1))
            index = jnp.broadcast_to(batch_ref[i : i + 1, :], (FEATS, COLS))
            own = jnp.take_along_axis(mean, index, axis=1)
            away = x_ref[:, part].astype(jnp.float32) - own
            square = away * away
            high = square.astype(jnp.bfloat16)
            hi_ref[:, part] = high
            lo_ref[:, part] = (square - high.astype(jnp.float32)).astype(jnp.bfloat16)
        spread = lax.dot_general(
            hi_ref[...], hot, NT, preferred_element_type=jnp.float32
        ) + lax.dot_general(lo_ref[...], hot, NT, preferred_element_type=jnp.float32)
        stats_ref[:, :FEATS] = mean.T
        stats_ref[:, FEATS:] = spread.T


def batch_kernel(order_ref, owner_ref, batch_ref, hot_ref):
    order = order_ref[...]
    shape = (32, order.shape[1])
    high = lax.broadcasted_iota(jnp.int32, shape, 0) == order // COLS
    left = jnp.where(high, owner_ref[...], 0.0).astype(jnp.bfloat16)
    shape = (COLS, order.shape[1])
    low = lax.broadcasted_iota(jnp.int32, shape, 0) == order % COLS
    right = jnp.where(low, 1.0, 0.0).astype(jnp.bfloat16)
    found = lax.dot_general(left, right, NT, preferred_element_type=jnp.float32)
    batch = found[:ROWS].astype(jnp.int32)
    batch_ref[...] = batch
    groups = lax.broadcasted_iota(jnp.int32, (COLS, COLS), 0)
    for i in range(ROWS):
        hot_ref[:, COLS * i : COLS * (i + 1)] = jnp.where(
            groups == batch[i : i + 1, :], 1.0, 0.0
        ).astype(jnp.bfloat16)


def merge_kernel(share, stats_ref, gain_ref, out_ref):
    count = stats_ref.shape[0]
    means = stats_ref[:, :FEATS]
    mean = jnp.sum(means, axis=0, keepdims=True) * (1.0 / count)
    away = means - mean
    total = jnp.sum(stats_ref[:, FEATS:] + share * (away * away), axis=0, keepdims=True)
    scale = lax.rsqrt(total * (1.0 / (count * share)) + 1e-05) * gain_ref[...]
    out_ref[:, :FEATS] = jnp.broadcast_to(mean, (count, FEATS))
    out_ref[:, FEATS:] = jnp.broadcast_to(scale, (count, FEATS))


def network_kernel(
    moved_ref,
    batch_ref,
    stats_ref,
    shift_ref,
    first_ref,
    inner_ref,
    last_ref,
    bias_ref,
    final_ref,
    out_ref,
    mean_ref,
    scale_ref,
):
    step = pl.program_id(0)

    @pl.when(step == 0)
    def _():
        mean_ref[...] = stats_ref[:, :FEATS].T
        scale_ref[...] = stats_ref[:, FEATS:].T

    mean = mean_ref[...]
    scale = scale_ref[...]
    shift = shift_ref[...]

    def wide(tile):
        return jnp.concatenate([tile, tile], axis=1)

    def act(product, layer):
        t = product + wide(bias_ref[layer])
        return (t + t * jnp.tanh(t)).astype(jnp.bfloat16)

    for pair in range(4):
        normed = []
        for i in (2 * pair, 2 * pair + 1):
            index = jnp.broadcast_to(batch_ref[i : i + 1, :], (FEATS, COLS))
            x = moved_ref[i].astype(jnp.bfloat16).astype(jnp.float32)
            away = x - jnp.take_along_axis(mean, index, axis=1)
            tile = away * jnp.take_along_axis(scale, index, axis=1) + shift
            normed.append(tile.astype(jnp.bfloat16))
        hidden = jnp.concatenate(normed, axis=1)
        hidden = act(
            lax.dot_general(first_ref[...], hidden, NN, preferred_element_type=jnp.float32), 0
        )
        for layer in range(3):
            hidden = act(
                lax.dot_general(
                    inner_ref[layer], hidden, NN, preferred_element_type=jnp.float32
                ),
                layer + 1,
            )
        tendency = lax.dot_general(
            last_ref[...], hidden, NN, preferred_element_type=jnp.float32
        ) + wide(final_ref[...])
        tendency = tendency.astype(jnp.bfloat16).astype(jnp.float32)
        for k in range(2):
            i = 2 * pair + k
            new = moved_ref[i] + tendency[:, COLS * k : COLS * (k + 1)]
            for chunk in range(CHUNKS):
                rows = min(8, LEVELS - 8 * chunk)
                for f in range(FIELDS):
                    row = 32 * chunk + 8 * f
                    out_ref[pl.ds((LEVELS * f + 8 * chunk) * 8 + i, rows, stride=8), :] = new[
                        row : row + rows
                    ]


def network_outer(*refs):
    (*inputs, out_ref, mean_ref, scale_ref) = refs
    network_kernel(*inputs, out_ref.reshape(FIELDS * LEVELS * 8, COLS), mean_ref, scale_ref)


def whole(shape):
    return pl.BlockSpec(shape, lambda c: (0,) * len(shape))


GRID_SPEC = pl.BlockSpec((ROWS, 32, COLS), lambda c: (0, c, 0))
NATIVE_SPEC = pl.BlockSpec((4, 8 * ROWS, COLS), lambda c: (0, c, 0))
ROW_SPEC = pl.BlockSpec((32, COLS), lambda c: (c, 0))
COL_SPEC = pl.BlockSpec((8, 2 * COLS), lambda c: (c, 0))
GRID_SHAPE = jax.ShapeDtypeStruct((ROWS, FEATS, COLS), jnp.float32)
ROW_SHAPE = jax.ShapeDtypeStruct((FEATS, COLS), jnp.float32)
COL_SHAPE = jax.ShapeDtypeStruct((64, 2 * COLS), jnp.float32)


def cost(flops, size):
    return pl.CostEstimate(flops=flops, bytes_accessed=size, transcendentals=0)


def ring(axis, by):
    count = lax.axis_size(axis)
    return [(i, (i + by) % count) for i in range(count)]


def halos(first, last, cols):
    up = lax.ppermute(last, "bx", ring("bx", 1))
    down = lax.ppermute(first, "bx", ring("bx", -1))
    left = lax.ppermute(cols, "by", ring("by", 1))
    right = lax.ppermute(cols, "by", ring("by", -1))
    return up, down, left, right


def by_row(values):
    rest = values.shape[1:]
    values = values.reshape(FIELDS, LEVELS, *rest)
    values = jnp.pad(values, ((0, 0), (0, 64 - LEVELS)) + ((0, 0),) * len(rest))
    values = values.reshape(FIELDS, CHUNKS, 8, *rest).swapaxes(0, 1)
    return values.reshape(FEATS, *rest)


def body(
    tracers,
    rates,
    column_order,
    norm_gain,
    norm_shift,
    weight_first,
    weight_hidden,
    weight_last,
    bias_hidden,
    bias_last,
):
    count = lax.axis_size("bx") * lax.axis_size("by")
    columns = ROWS * COLS
    share = columns // count
    width = weight_first.shape[0]
    x = tracers.reshape(FIELDS, LEVELS * ROWS, COLS)
    r = rates.reshape(4, LEVELS * ROWS, COLS)

    q, first, last, cols = pl.pallas_call(
        pack_kernel,
        grid=(CHUNKS,),
        in_specs=[NATIVE_SPEC],
        out_specs=[GRID_SPEC, ROW_SPEC, ROW_SPEC, COL_SPEC],
        out_shape=[GRID_SHAPE, ROW_SHAPE, ROW_SHAPE, COL_SHAPE],
        compiler_params=params(),
        cost_estimate=cost(10**6, 6 * 10**6),
        name="pack_edges",
    )(x)
    edges = halos(first, last, cols)

    owner = (jnp.arange(columns, dtype=jnp.int32) // share).astype(jnp.float32)[None, :]
    batch, hot = pl.pallas_call(
        batch_kernel,
        grid=(1,),
        in_specs=[whole((1, columns)), whole((1, columns))],
        out_specs=[whole((ROWS, COLS)), whole((COLS, columns))],
        out_shape=[
            jax.ShapeDtypeStruct((ROWS, COLS), jnp.int32),
            jax.ShapeDtypeStruct((COLS, columns), jnp.bfloat16),
        ],
        compiler_params=params(),
        cost_estimate=cost(10**9, 2 * 10**6),
        name="batch_ids",
    )(column_order, owner)

    state_specs = [GRID_SPEC, NATIVE_SPEC, ROW_SPEC, ROW_SPEC, COL_SPEC, COL_SPEC]
    q, first, last, cols = pl.pallas_call(
        first_kernel,
        grid=(CHUNKS,),
        in_specs=state_specs,
        out_specs=[GRID_SPEC, ROW_SPEC, ROW_SPEC, COL_SPEC],
        out_shape=[GRID_SHAPE, ROW_SHAPE, ROW_SHAPE, COL_SHAPE],
        compiler_params=params(),
        cost_estimate=cost(10**7, 9 * 10**6),
        name="first_substep",
    )(q, r, *edges)
    edges = halos(first, last, cols)

    moved, stats = pl.pallas_call(
        functools.partial(second_kernel, share),
        grid=(CHUNKS,),
        in_specs=state_specs + [whole((COLS, columns)), whole((ROWS, COLS))],
        out_specs=[GRID_SPEC, whole((COLS, 2 * FEATS))],
        out_shape=[GRID_SHAPE, jax.ShapeDtypeStruct((COLS, 2 * FEATS), jnp.float32)],
        scratch_shapes=[pltpu.VMEM((FEATS, columns), jnp.bfloat16) for _ in range(3)],
        compiler_params=params(),
        cost_estimate=cost(10**9, 9 * 10**6),
        name="second_substep",
    )(q, r, *edges, hot, batch)

    gathered = lax.all_to_all(stats, ("bx", "by"), split_axis=0, concat_axis=0, tiled=True)
    merged = pl.pallas_call(
        functools.partial(merge_kernel, float(share)),
        grid=(1,),
        in_specs=[whole((count, 2 * FEATS)), whole((1, FEATS))],
        out_specs=whole((count, 2 * FEATS)),
        out_shape=jax.ShapeDtypeStruct((count, 2 * FEATS), jnp.float32),
        compiler_params=params(),
        cost_estimate=cost(10**6, 10**6),
        name="merge_statistics",
    )(gathered, by_row(norm_gain)[None, :])
    known = lax.all_to_all(merged, ("bx", "by"), split_axis=0, concat_axis=0, tiled=True)

    def tile(values):
        return jnp.broadcast_to(values[..., None], (*values.shape, COLS))

    half = jnp.bfloat16(0.5)
    new = pl.pallas_call(
        network_outer,
        grid=(3,),
        in_specs=[
            pl.BlockSpec((8, FEATS, COLS), lambda c: (c, 0, 0)),
            pl.BlockSpec((8, COLS), lambda c: (c, 0)),
            whole((count, 2 * FEATS)),
            whole((FEATS, COLS)),
            whole((width, FEATS)),
            whole((3, width, width)),
            whole((FEATS, width)),
            whole((4, width, COLS)),
            whole((FEATS, COLS)),
        ],
        out_specs=pl.BlockSpec((FIELDS * LEVELS, 8, COLS), lambda c: (0, c, 0)),
        out_shape=jax.ShapeDtypeStruct((FIELDS * LEVELS, ROWS, COLS), jnp.float32),
        scratch_shapes=[pltpu.VMEM((FEATS, COLS), jnp.float32) for _ in range(2)],
        compiler_params=params(40),
        cost_estimate=cost(6 * 10**9, 9 * 10**6),
        name="network",
    )(
        moved,
        batch,
        known,
        tile(by_row(norm_shift)),
        by_row(weight_first.T).T * half,
        weight_hidden * half,
        by_row(weight_last),
        tile(bias_hidden * 0.5),
        tile(by_row(bias_last)),
    )
    return new.reshape(tracers.shape)


def solution(mesh):
    placed = (
        P(None, None, "bx", "by"),
        P(None, None, "bx", "by"),
        P(("bx", "by"), None),
        P(),
        P(),
        P(),
        P(),
        P(),
        P(),
        P(),
    )
    return jax.shard_map(
        body, mesh=mesh, in_specs=placed, out_specs=P(None, None, "bx", "by"), check_vma=False
    )
```

```python
import functools

import jax
import jax.numpy as jnp
from jax import lax
from jax.experimental import pallas as pl
from jax.experimental.pallas import tpu as pltpu
from jax.sharding import PartitionSpec as P

FIELDS = 4
LEVELS = 60
CHUNKS = 8
ROWS = 24
COLS = 128
FEATS = 256
HALF = ROWS // 2
MIB = 1 << 20
NT = (((1,), (1,)), ((), ()))
NN = (((1,), (0,)), ((), ()))


def params(limit=60):
    return pltpu.CompilerParams(
        dimension_semantics=("arbitrary",), vmem_limit_bytes=limit * MIB
    )


def lanes_of(shape):
    return lax.broadcasted_iota(jnp.int32, shape, 1)


def valid_rows(chunk):
    level = chunk * 8 + lax.broadcasted_iota(jnp.int32, (8, COLS), 0)
    return level < LEVELS


class ColumnPacker:
    def __init__(self):
        self.pair = lanes_of((8, COLS)) // 2
        self.halves = [jnp.zeros((8, COLS), jnp.float32) for _ in range(2)]

    def add(self, i, f, tile):
        m = 4 * (i % HALF) + f
        moved = pltpu.roll(tile, 2 * m + 1, axis=1)
        self.halves[i // HALF] = jnp.where(self.pair == m, moved, self.halves[i // HALF])

    def store(self, ref):
        for h in range(2):
            ref[:, COLS * h : COLS * (h + 1)] = self.halves[h]


def store_rows(parity_ref, tiles, near_ref, far_ref):
    even = jnp.full((32, COLS), parity_ref[0], jnp.int32) == 0
    near_ref[...] = jnp.where(even, tiles[ROWS - 1], tiles[0])
    far_ref[...] = jnp.where(even, tiles[0], tiles[ROWS - 1])


def pack_kernel(parity_ref, x_ref, q_ref, near_ref, far_ref, cols_ref):
    valid = valid_rows(pl.program_id(0))
    packer = ColumnPacker()
    for i in range(ROWS):
        for f in range(FIELDS):
            tile = jnp.where(valid, x_ref[f, pl.ds(i, 8, stride=ROWS), :], 0.0)
            q_ref[i, 8 * f : 8 * f + 8, :] = tile
            packer.add(i, f, tile)
    packer.store(cols_ref)
    store_rows(parity_ref, q_ref, near_ref, far_ref)


def advance_tiles(parity_ref, q_ref, rates_ref, near_ref, far_ref, core_ref, chip_ref, emit):
    valid = valid_rows(pl.program_id(0))
    lane = lanes_of((8, COLS))
    even = lane % 2 == 0
    even_x = jnp.full((8, COLS), parity_ref[0], jnp.int32) == 0
    even_y = jnp.full((8, COLS), parity_ref[1], jnp.int32) == 0
    ring = []
    for h in range(2):
        part = slice(COLS * h, COLS * (h + 1))
        right = jnp.where(even_y, core_ref[:, part], chip_ref[:, part])
        left = jnp.where(even_y, chip_ref[:, part], core_ref[:, part])
        ring.append(
            jnp.where(even, pltpu.roll(right, COLS - 1, axis=1), pltpu.roll(left, 1, axis=1))
        )
    for i in range(ROWS):
        rate = [rates_ref[k, pl.ds(i, 8, stride=ROWS), :] for k in range(4)]
        for f in range(FIELDS):
            rows = slice(8 * f, 8 * f + 8)
            m = 4 * (i % HALF) + f
            here = q_ref[i, rows, :]
            if i == 0:
                above = jnp.where(even_x, far_ref[rows, :], near_ref[rows, :])
            else:
                above = q_ref[i - 1, rows, :]
            if i == ROWS - 1:
                below = jnp.where(even_x, near_ref[rows, :], far_ref[rows, :])
            else:
                below = q_ref[i + 1, rows, :]
            edge = pltpu.roll(ring[i // HALF], COLS - (2 * m + 1), axis=1)
            after = jnp.where(lane == COLS - 1, edge, pltpu.roll(here, COLS - 1, axis=1))
            before = jnp.where(lane == 0, edge, pltpu.roll(here, 1, axis=1))
            new = (
                here
                + rate[0] * (below - here)
                + rate[1] * (above - here)
                + rate[2] * (after - here)
                + rate[3] * (before - here)
            )
            emit(i, f, jnp.where(valid, new, 0.0))


def first_kernel(
    parity_ref,
    q_ref,
    rates_ref,
    near_ref,
    far_ref,
    core_ref,
    chip_ref,
    out_ref,
    near_out_ref,
    far_out_ref,
    cols_ref,
):
    def emit(i, f, tile):
        out_ref[i, 8 * f : 8 * f + 8, :] = tile

    advance_tiles(parity_ref, q_ref, rates_ref, near_ref, far_ref, core_ref, chip_ref, emit)
    store_rows(parity_ref, out_ref, near_out_ref, far_out_ref)
    packer = ColumnPacker()
    for i in range(ROWS):
        for f in range(FIELDS):
            packer.add(i, f, out_ref[i, 8 * f : 8 * f + 8, :])
    packer.store(cols_ref)


def second_kernel(
    share,
    parity_ref,
    q_ref,
    rates_ref,
    near_ref,
    far_ref,
    core_ref,
    chip_ref,
    hot_ref,
    batch_ref,
    out_ref,
    stats_ref,
    x_ref,
    hi_ref,
    lo_ref,
):
    chunk = pl.program_id(0)
    kept = {}

    def emit(i, f, tile):
        out_ref[i, 8 * f : 8 * f + 8, :] = tile
        kept[f] = tile
        if f % 2 == 1:
            both = jnp.concatenate([kept[f - 1], tile], axis=0).astype(jnp.bfloat16)
            start = pl.multiple_of(32 * chunk + 8 * (f - 1), 16)
            x_ref[pl.ds(start, 16), COLS * i : COLS * (i + 1)] = both

    advance_tiles(parity_ref, q_ref, rates_ref, near_ref, far_ref, core_ref, chip_ref, emit)

    @pl.when(chunk == CHUNKS - 1)
    def _():
        hot = hot_ref[...]
        sums = lax.dot_general(x_ref[...], hot, NT, preferred_element_type=jnp.float32)
        mean = sums * (1.0 / share)
        for i in range(ROWS):
            part = slice(COLS * i, COLS * (i + 1))
            index = jnp.broadcast_to(batch_ref[i : i + 1, :], (FEATS, COLS))
            own = jnp.take_along_axis(mean, index, axis=1)
            away = x_ref[:, part].astype(jnp.float32) - own
            square = away * away
            high = square.astype(jnp.bfloat16)
            hi_ref[:, part] = high
            lo_ref[:, part] = (square - high.astype(jnp.float32)).astype(jnp.bfloat16)
        spread = lax.dot_general(
            hi_ref[...], hot, NT, preferred_element_type=jnp.float32
        ) + lax.dot_general(lo_ref[...], hot, NT, preferred_element_type=jnp.float32)
        store_parts(stats_ref, (mean[:COLS].T, mean[COLS:].T, spread[:COLS].T, spread[COLS:].T))


def store_parts(ref, parts):
    for k, part in enumerate(parts):
        ref[pl.ds(k, part.shape[0], stride=4), :] = part


def load_parts(ref):
    return [ref[pl.ds(k, ref.shape[0] // 4, stride=4), :] for k in range(4)]


def batch_kernel(order_ref, owner_ref, batch_ref, hot_ref):
    order = order_ref[...]
    shape = (32, order.shape[1])
    high = lax.broadcasted_iota(jnp.int32, shape, 0) == order // COLS
    left = jnp.where(high, owner_ref[...], 0.0).astype(jnp.bfloat16)
    shape = (COLS, order.shape[1])
    low = lax.broadcasted_iota(jnp.int32, shape, 0) == order % COLS
    right = jnp.where(low, 1.0, 0.0).astype(jnp.bfloat16)
    found = lax.dot_general(left, right, NT, preferred_element_type=jnp.float32)
    batch = found[:ROWS].astype(jnp.int32)
    batch_ref[...] = batch
    groups = lax.broadcasted_iota(jnp.int32, (COLS, COLS), 0)
    for i in range(ROWS):
        hot_ref[:, COLS * i : COLS * (i + 1)] = jnp.where(
            groups == batch[i : i + 1, :], 1.0, 0.0
        ).astype(jnp.bfloat16)


def merge_kernel(share, stats_ref, gain_ref, out_ref):
    count = stats_ref.shape[0] // 4
    parts = load_parts(stats_ref)
    merged = []
    for k in range(2):
        mean = jnp.sum(parts[k], axis=0, keepdims=True) * (1.0 / count)
        away = parts[k] - mean
        total = jnp.sum(parts[k + 2] + share * (away * away), axis=0, keepdims=True)
        gain = gain_ref[:, COLS * k : COLS * (k + 1)]
        merged.append((mean, lax.rsqrt(total * (1.0 / (count * share)) + 1e-05) * gain))
    values = (merged[0][0], merged[1][0], merged[0][1], merged[1][1])
    store_parts(out_ref, [jnp.broadcast_to(v, (count, COLS)) for v in values])


def network_kernel(
    moved_ref,
    batch_ref,
    stats_ref,
    shift_ref,
    first_ref,
    inner_ref,
    last_ref,
    bias_ref,
    final_ref,
    out_ref,
    mean_ref,
    scale_ref,
):
    step = pl.program_id(0)

    @pl.when(step == 0)
    def _():
        parts = load_parts(stats_ref)
        for k in range(2):
            mean_ref[COLS * k : COLS * (k + 1), :] = parts[k].T
            scale_ref[COLS * k : COLS * (k + 1), :] = parts[k + 2].T

    mean = mean_ref[...]
    scale = scale_ref[...]
    shift = shift_ref[...]

    def wide(tile):
        return jnp.concatenate([tile, tile], axis=1)

    def act(product, layer):
        t = product + wide(bias_ref[layer])
        return (t + t * jnp.tanh(t)).astype(jnp.bfloat16)

    for pair in range(4):
        normed = []
        for i in (2 * pair, 2 * pair + 1):
            index = jnp.broadcast_to(batch_ref[i : i + 1, :], (FEATS, COLS))
            x = moved_ref[i].astype(jnp.bfloat16).astype(jnp.float32)
            away = x - jnp.take_along_axis(mean, index, axis=1)
            tile = away * jnp.take_along_axis(scale, index, axis=1) + shift
            normed.append(tile.astype(jnp.bfloat16))
        hidden = jnp.concatenate(normed, axis=1)
        hidden = act(
            lax.dot_general(first_ref[...], hidden, NN, preferred_element_type=jnp.float32), 0
        )
        for layer in range(3):
            hidden = act(
                lax.dot_general(
                    inner_ref[layer], hidden, NN, preferred_element_type=jnp.float32
                ),
                layer + 1,
            )
        tendency = lax.dot_general(
            last_ref[...], hidden, NN, preferred_element_type=jnp.float32
        ) + wide(final_ref[...])
        tendency = tendency.astype(jnp.bfloat16).astype(jnp.float32)
        for k in range(2):
            i = 2 * pair + k
            new = moved_ref[i] + tendency[:, COLS * k : COLS * (k + 1)]
            for chunk in range(CHUNKS):
                rows = min(8, LEVELS - 8 * chunk)
                for f in range(FIELDS):
                    row = 32 * chunk + 8 * f
                    out_ref[pl.ds((LEVELS * f + 8 * chunk) * 8 + i, rows, stride=8), :] = new[
                        row : row + rows
                    ]


def network_outer(*refs):
    (*inputs, out_ref, mean_ref, scale_ref) = refs
    network_kernel(*inputs, out_ref.reshape(FIELDS * LEVELS * 8, COLS), mean_ref, scale_ref)


def whole(shape):
    return pl.BlockSpec(shape, lambda c: (0,) * len(shape))


SCALAR_SPEC = pl.BlockSpec(memory_space=pltpu.SMEM)
GRID_SPEC = pl.BlockSpec((ROWS, 32, COLS), lambda c: (0, c, 0))
NATIVE_SPEC = pl.BlockSpec((4, 8 * ROWS, COLS), lambda c: (0, c, 0))
ROW_SPEC = pl.BlockSpec((32, COLS), lambda c: (c, 0))
COL_SPEC = pl.BlockSpec((8, 2 * COLS), lambda c: (c, 0))
GRID_SHAPE = jax.ShapeDtypeStruct((ROWS, FEATS, COLS), jnp.float32)
ROW_SHAPE = jax.ShapeDtypeStruct((FEATS, COLS), jnp.float32)
COL_SHAPE = jax.ShapeDtypeStruct((64, 2 * COLS), jnp.float32)


def cost(flops, size):
    return pl.CostEstimate(flops=flops, bytes_accessed=size, transcendentals=0)


def swap(values, axis, first):
    count = lax.axis_size(axis)
    step = 0 if first else 1
    pairs = [((i + step) % count, (i + 1 + step) % count) for i in range(0, count, 2)]
    return lax.ppermute(values, axis, pairs + [(b, a) for a, b in pairs])


def halos(near, far, cols):
    return (
        swap(near, "bx", True),
        swap(far, "bx", False),
        swap(cols, "by", True),
        swap(cols, "by", False),
    )


def by_row(values):
    rest = values.shape[1:]
    values = values.reshape(FIELDS, LEVELS, *rest)
    values = jnp.pad(values, ((0, 0), (0, 64 - LEVELS)) + ((0, 0),) * len(rest))
    values = values.reshape(FIELDS, CHUNKS, 8, *rest).swapaxes(0, 1)
    return values.reshape(FEATS, *rest)


def body(
    tracers,
    rates,
    column_order,
    norm_gain,
    norm_shift,
    weight_first,
    weight_hidden,
    weight_last,
    bias_hidden,
    bias_last,
):
    count = lax.axis_size("bx") * lax.axis_size("by")
    columns = ROWS * COLS
    share = columns // count
    width = weight_first.shape[0]
    x = tracers.reshape(FIELDS, LEVELS * ROWS, COLS)
    r = rates.reshape(4, LEVELS * ROWS, COLS)
    parity = jnp.stack([lax.axis_index("bx"), lax.axis_index("by")]).astype(jnp.int32) % 2

    q, near, far, cols = pl.pallas_call(
        pack_kernel,
        grid=(CHUNKS,),
        in_specs=[SCALAR_SPEC, NATIVE_SPEC],
        out_specs=[GRID_SPEC, ROW_SPEC, ROW_SPEC, COL_SPEC],
        out_shape=[GRID_SHAPE, ROW_SHAPE, ROW_SHAPE, COL_SHAPE],
        compiler_params=params(),
        cost_estimate=cost(10**6, 6 * 10**6),
        name="pack_edges",
    )(parity, x)
    edges = halos(near, far, cols)

    owner = (jnp.arange(columns, dtype=jnp.int32) // share).astype(jnp.float32)[None, :]
    batch, hot = pl.pallas_call(
        batch_kernel,
        grid=(1,),
        in_specs=[whole((1, columns)), whole((1, columns))],
        out_specs=[whole((ROWS, COLS)), whole((COLS, columns))],
        out_shape=[
            jax.ShapeDtypeStruct((ROWS, COLS), jnp.int32),
            jax.ShapeDtypeStruct((COLS, columns), jnp.bfloat16),
        ],
        compiler_params=params(),
        cost_estimate=cost(10**9, 2 * 10**6),
        name="batch_ids",
    )(column_order, owner)

    state_specs = [SCALAR_SPEC, GRID_SPEC, NATIVE_SPEC, ROW_SPEC, ROW_SPEC, COL_SPEC, COL_SPEC]
    q, near, far, cols = pl.pallas_call(
        first_kernel,
        grid=(CHUNKS,),
        in_specs=state_specs,
        out_specs=[GRID_SPEC, ROW_SPEC, ROW_SPEC, COL_SPEC],
        out_shape=[GRID_SHAPE, ROW_SHAPE, ROW_SHAPE, COL_SHAPE],
        compiler_params=params(),
        cost_estimate=cost(10**7, 9 * 10**6),
        name="first_substep",
    )(parity, q, r, *edges)
    edges = halos(near, far, cols)

    moved, stats = pl.pallas_call(
        functools.partial(second_kernel, share),
        grid=(CHUNKS,),
        in_specs=state_specs + [whole((COLS, columns)), whole((ROWS, COLS))],
        out_specs=[GRID_SPEC, whole((4 * count, COLS))],
        out_shape=[GRID_SHAPE, jax.ShapeDtypeStruct((4 * count, COLS), jnp.float32)],
        scratch_shapes=[pltpu.VMEM((FEATS, columns), jnp.bfloat16) for _ in range(3)],
        compiler_params=params(),
        cost_estimate=cost(10**9, 9 * 10**6),
        name="second_substep",
    )(parity, q, r, *edges, hot, batch)

    gathered = lax.all_to_all(stats, ("bx", "by"), split_axis=0, concat_axis=0, tiled=True)
    merged = pl.pallas_call(
        functools.partial(merge_kernel, float(share)),
        grid=(1,),
        in_specs=[whole((4 * count, COLS)), whole((1, FEATS))],
        out_specs=whole((4 * count, COLS)),
        out_shape=jax.ShapeDtypeStruct((4 * count, COLS), jnp.float32),
        compiler_params=params(),
        cost_estimate=cost(10**6, 10**6),
        name="merge_statistics",
    )(gathered, by_row(norm_gain)[None, :])
    known = lax.all_to_all(merged, ("bx", "by"), split_axis=0, concat_axis=0, tiled=True)

    def tile(values):
        return jnp.broadcast_to(values[..., None], (*values.shape, COLS))

    half = jnp.bfloat16(0.5)
    new = pl.pallas_call(
        network_outer,
        grid=(3,),
        in_specs=[
            pl.BlockSpec((8, FEATS, COLS), lambda c: (c, 0, 0)),
            pl.BlockSpec((8, COLS), lambda c: (c, 0)),
            whole((4 * count, COLS)),
            whole((FEATS, COLS)),
            whole((width, FEATS)),
            whole((3, width, width)),
            whole((FEATS, width)),
            whole((4, width, COLS)),
            whole((FEATS, COLS)),
        ],
        out_specs=pl.BlockSpec((FIELDS * LEVELS, 8, COLS), lambda c: (0, c, 0)),
        out_shape=jax.ShapeDtypeStruct((FIELDS * LEVELS, ROWS, COLS), jnp.float32),
        scratch_shapes=[pltpu.VMEM((FEATS, COLS), jnp.float32) for _ in range(2)],
        compiler_params=params(40),
        cost_estimate=cost(6 * 10**9, 9 * 10**6),
        name="network",
    )(
        moved,
        batch,
        known,
        tile(by_row(norm_shift)),
        by_row(weight_first.T).T * half,
        weight_hidden * half,
        by_row(weight_last),
        tile(bias_hidden * 0.5),
        tile(by_row(bias_last)),
    )
    return new.reshape(tracers.shape)


def solution(mesh):
    placed = (
        P(None, None, "bx", "by"),
        P(None, None, "bx", "by"),
        P(("bx", "by"), None),
        P(),
        P(),
        P(),
        P(),
        P(),
        P(),
        P(),
    )
    return jax.shard_map(
        body, mesh=mesh, in_specs=placed, out_specs=P(None, None, "bx", "by"), check_vma=False
    )
```

```python
import functools

import jax
import jax.numpy as jnp
from jax import lax
from jax.experimental import pallas as pl
from jax.experimental.pallas import tpu as pltpu
from jax.sharding import PartitionSpec as P

FIELDS = 4
LEVELS = 60
CHUNKS = 8
ROWS = 24
COLS = 128
FEATS = 256
HALF = ROWS // 2
MIB = 1 << 20
NT = (((1,), (1,)), ((), ()))
NN = (((1,), (0,)), ((), ()))


def params(grid=False, limit=60):
    return pltpu.CompilerParams(
        dimension_semantics=("arbitrary",) if grid else None, vmem_limit_bytes=limit * MIB
    )


def lanes_of(shape):
    return lax.broadcasted_iota(jnp.int32, shape, 1)


def valid_rows(chunk):
    level = chunk * 8 + lax.broadcasted_iota(jnp.int32, (8, COLS), 0)
    return level < LEVELS


def level_copies(hbm_ref, vmem_ref, sem):
    copies = []
    for c in range(CHUNKS):
        rows = ROWS * min(8, LEVELS - 8 * c)
        copies.append(
            pltpu.make_async_copy(
                hbm_ref.at[:, pl.ds(8 * ROWS * c, rows), :],
                vmem_ref.at[c, :, pl.ds(0, rows), :],
                sem.at[c],
            )
        )
    return copies


def wait_for(chunk, *groups):
    for c in range(CHUNKS):

        @pl.when(chunk == c)
        def _(c=c):
            for copies in groups:
                copies[c].wait()


class ColumnPacker:
    def __init__(self):
        self.pair = lanes_of((8, COLS)) // 2
        self.halves = [jnp.zeros((8, COLS), jnp.float32) for _ in range(2)]

    def add(self, i, f, tile):
        m = 4 * (i % HALF) + f
        moved = pltpu.roll(tile, 2 * m + 1, axis=1)
        self.halves[i // HALF] = jnp.where(self.pair == m, moved, self.halves[i // HALF])

    def store(self, ref, row):
        for h in range(2):
            ref[pl.ds(row, 8), COLS * h : COLS * (h + 1)] = self.halves[h]


def pair_of(last, first):
    return jnp.where(
        lanes_of((8, COLS)) % 2 == 0,
        jnp.broadcast_to(last[:, COLS - 1 :], (8, COLS)),
        jnp.broadcast_to(first[:, :1], (8, COLS)),
    )


def swap_flag(parity_ref, axis, rows):
    return jnp.full((rows, COLS), parity_ref[axis], jnp.int32) == 0


def mixed(rate, here, below, above, after, before):
    return (
        here
        + rate[0] * (below - here)
        + rate[1] * (above - here)
        + rate[2] * (after - here)
        + rate[3] * (before - here)
    )


def first_kernel(
    parity_ref,
    x_hbm,
    r_hbm,
    part_hbm,
    near_ref,
    far_ref,
    cols_ref,
    x_ref,
    r_ref,
    part_ref,
    x_sem,
    r_sem,
    out_sem,
):
    x_copies = level_copies(x_hbm, x_ref, x_sem)
    r_copies = level_copies(r_hbm, r_ref, r_sem)
    for c in range(CHUNKS):
        x_copies[c].start()
        r_copies[c].start()
    lane = lanes_of((8, COLS))
    zero = jnp.zeros((8, COLS), jnp.float32)
    even = swap_flag(parity_ref, 0, 8)

    def one_chunk(c, carry):
        valid = valid_rows(c)
        wait_for(c, x_copies, r_copies)

        def cell(i, f):
            return jnp.where(valid, x_ref[c, f, pl.ds(i, 8, stride=ROWS), :], 0.0)

        def rate_of(i, k):
            return jnp.where(valid, r_ref[c, k, pl.ds(i, 8, stride=ROWS), :], 0.0)

        for i in range(ROWS):
            rate = [rate_of(i, k) for k in range(4)]
            for f in range(FIELDS):
                here = cell(i, f)
                part_ref[c, i, 8 * f : 8 * f + 8, :] = mixed(
                    rate,
                    here,
                    cell(i + 1, f) if i < ROWS - 1 else zero,
                    cell(i - 1, f) if i > 0 else zero,
                    jnp.where(lane == COLS - 1, 0.0, pltpu.roll(here, COLS - 1, axis=1)),
                    jnp.where(lane == 0, 0.0, pltpu.roll(here, 1, axis=1)),
                )
        pltpu.make_async_copy(part_ref.at[c], part_hbm.at[c], out_sem.at[c]).start()

        start = pl.multiple_of(EDGE_ROWS * c, 8)
        for f in range(2 * FIELDS + 1):
            if f < FIELDS:
                last, first = cell(ROWS - 1, f), cell(0, f)
            elif f < 2 * FIELDS:
                rows = slice(8 * (f - FIELDS), 8 * (f - FIELDS) + 8)
                last, first = part_ref[c, ROWS - 1, rows, :], part_ref[c, 0, rows, :]
            else:
                last, first = rate_of(ROWS - 1, 0), rate_of(0, 1)
            near_ref[pl.ds(start + 8 * f, 8), :] = jnp.where(even, last, first)
            far_ref[pl.ds(start + 8 * f, 8), :] = jnp.where(even, first, last)

        row = pl.multiple_of(8 * c, 8)
        packer = ColumnPacker()
        for i in range(ROWS):
            for f in range(FIELDS):
                packer.add(i, f, cell(i, f))
        packer.store(cols_ref, row)
        packer = ColumnPacker()
        for i in range(ROWS):
            for f in range(FIELDS):
                packer.add(i, f, part_ref[c, i, 8 * f : 8 * f + 8, :])
        packer.store(cols_ref, 64 + row)
        for h in range(2):
            acc = zero
            for i in range(HALF):
                pair = pair_of(rate_of(HALF * h + i, 2), rate_of(HALF * h + i, 3))
                acc = jnp.where(lane // 8 == i, pair, acc)
            outer = rate_of(0, 1) if h == 0 else rate_of(ROWS - 1, 0)
            acc = jnp.where(lane // 8 == HALF, pair_of(outer, outer), acc)
            cols_ref[pl.ds(128 + row, 8), COLS * h : COLS * (h + 1)] = acc
        return carry

    lax.fori_loop(0, CHUNKS, one_chunk, 0)
    for c in range(CHUNKS):
        pltpu.make_async_copy(part_ref.at[c], part_hbm.at[c], out_sem.at[c]).wait()


def merged_columns(even_y, core, chip):
    right = jnp.where(even_y, core, chip)
    left = jnp.where(even_y, chip, core)
    return jnp.where(
        lanes_of((8, COLS)) % 2 == 0,
        pltpu.roll(right, COLS - 1, axis=1),
        pltpu.roll(left, 1, axis=1),
    )


def corner_kernel(parity_ref, cols_ref, core_ref, chip_ref, near_ref, far_ref):
    even = swap_flag(parity_ref, 0, 8)
    even_y = swap_flag(parity_ref, 1, 8)
    lane = lanes_of((8, COLS))
    for c in range(CHUNKS):
        sent = []
        for h in range(2):
            part = slice(COLS * h, COLS * (h + 1))
            rows = slice(8 * c, 8 * c + 8)
            beside = merged_columns(even_y, core_ref[rows, part], chip_ref[rows, part])
            given = cols_ref[128 + 8 * c : 136 + 8 * c, part] * beside
            back = 8 * (HALF - 1) * h
            sent.append(
                jnp.where(
                    lane < 8,
                    pltpu.roll(beside, (COLS - back) % COLS, axis=1),
                    pltpu.roll(given, (COLS + 8 - back) % COLS, axis=1),
                )
            )
        first, last = sent
        near_ref[8 * c : 8 * c + 8, :] = jnp.where(even, last, first)
        far_ref[8 * c : 8 * c + 8, :] = jnp.where(even, first, last)


def second_kernel(
    share,
    parity_ref,
    part_hbm,
    r_hbm,
    own_near_ref,
    own_far_ref,
    near_ref,
    far_ref,
    cols_ref,
    core_ref,
    chip_ref,
    corner_near_ref,
    corner_far_ref,
    hot_hbm,
    batch_ref,
    moved_hbm,
    stats_ref,
    part_ref,
    r_ref,
    hot_ref,
    moved_ref,
    x_ref,
    hi_ref,
    lo_ref,
    part_sem,
    r_sem,
    out_sem,
    hot_sem,
):
    part_copies = [
        pltpu.make_async_copy(part_hbm.at[c], part_ref.at[c], part_sem.at[c])
        for c in range(CHUNKS)
    ]
    r_copies = level_copies(r_hbm, r_ref, r_sem)
    for c in range(CHUNKS):
        part_copies[c].start()
        r_copies[c].start()
    hot_copy = pltpu.make_async_copy(hot_hbm, hot_ref, hot_sem)
    hot_copy.start()
    lane = lanes_of((8, COLS))
    rim = (lane == 0) | (lane == COLS - 1)
    even = swap_flag(parity_ref, 0, 8)
    even_y = swap_flag(parity_ref, 1, 8)

    def one_chunk(c, carry):
        valid = valid_rows(c)
        row = pl.multiple_of(8 * c, 8)
        start = pl.multiple_of(EDGE_ROWS * c, 8)
        wait_for(c, part_copies, r_copies)

        def edge(near, far, f, below):
            a, b = near[pl.ds(start + 8 * f, 8), :], far[pl.ds(start + 8 * f, 8), :]
            return jnp.where(even, a, b) if below else jnp.where(even, b, a)

        def rate_of(i, k):
            return r_ref[c, k, pl.ds(i, 8, stride=ROWS), :]

        corner = [corner_near_ref[pl.ds(row, 8), :], corner_far_ref[pl.ds(row, 8), :]]
        corner = [jnp.where(even, corner[1], corner[0]), jnp.where(even, corner[0], corner[1])]
        rings, gains = [], []
        for h in range(2):
            lanes = slice(COLS * h, COLS * (h + 1))
            cells, parts, rates = (
                merged_columns(
                    even_y,
                    core_ref[pl.ds(64 * k + row, 8), lanes],
                    chip_ref[pl.ds(64 * k + row, 8), lanes],
                )
                for k in range(3)
            )
            diagonal = corner[h]
            if h == 1:
                diagonal = pltpu.roll(diagonal, 8 * (HALF - 1), axis=1)
            shift = COLS - 8 * HALF if h == 0 else COLS - 8
            spot = lane // 8 == (0 if h == 0 else HALF - 1)
            extra = jnp.where(spot, pltpu.roll(rates, shift, axis=1) * diagonal, 0.0)
            rings.append(parts + rates * cols_ref[pl.ds(row, 8), lanes] + extra)
            gains.append(cols_ref[pl.ds(128 + row, 8), lanes] * cells)

        outer = []
        for side, i in enumerate((0, ROWS - 1)):
            down = side == 1
            rate = edge(near_ref, far_ref, 2 * FIELDS, down)
            tiles = []
            for f in range(FIELDS):
                turned = pltpu.roll(corner[side], COLS - (9 + 2 * f), axis=1)
                tiles.append(
                    edge(near_ref, far_ref, FIELDS + f, down)
                    + rate * edge(own_near_ref, own_far_ref, f, down)
                    + jnp.where(rim, turned, 0.0)
                )
            outer.append(tiles)

        for i in range(ROWS):
            for f in range(FIELDS):
                m = 4 * (i % HALF) + f
                turned = pltpu.roll(gains[i // HALF], COLS - (2 * m + 1), axis=1)
                tile = part_ref[c, i, 8 * f : 8 * f + 8, :] + jnp.where(rim, turned, 0.0)
                if i == 0:
                    tile = tile + rate_of(0, 1) * edge(near_ref, far_ref, f, False)
                if i == ROWS - 1:
                    tile = tile + rate_of(ROWS - 1, 0) * edge(near_ref, far_ref, f, True)
                part_ref[c, i, 8 * f : 8 * f + 8, :] = tile

        for i in range(ROWS):
            rate = [rate_of(i, k) for k in range(4)]
            kept = []
            for f in range(FIELDS):
                rows = slice(8 * f, 8 * f + 8)
                m = 4 * (i % HALF) + f
                here = part_ref[c, i, rows, :]
                above = outer[0][f] if i == 0 else part_ref[c, i - 1, rows, :]
                below = outer[1][f] if i == ROWS - 1 else part_ref[c, i + 1, rows, :]
                turned = pltpu.roll(rings[i // HALF], COLS - (2 * m + 1), axis=1)
                after = jnp.where(lane == COLS - 1, turned, pltpu.roll(here, COLS - 1, axis=1))
                before = jnp.where(lane == 0, turned, pltpu.roll(here, 1, axis=1))
                tile = jnp.where(valid, mixed(rate, here, below, above, after, before), 0.0)
                moved_ref[c, i, rows, :] = tile
                kept.append(tile)
            for f in (0, 2):
                both = jnp.concatenate(kept[f : f + 2], axis=0).astype(jnp.bfloat16)
                x_ref[pl.ds(pl.multiple_of(32 * c + 8 * f, 16), 16), COLS * i : COLS * (i + 1)] = (
                    both
                )
        pltpu.make_async_copy(moved_ref.at[c], moved_hbm.at[c], out_sem.at[c]).start()
        return carry

    lax.fori_loop(0, CHUNKS, one_chunk, 0)
    hot_copy.wait()
    hot = hot_ref[...]
    sums = lax.dot_general(x_ref[...], hot, NT, preferred_element_type=jnp.float32)
    mean = sums * (1.0 / share)
    for i in range(ROWS):
        part = slice(COLS * i, COLS * (i + 1))
        index = jnp.broadcast_to(batch_ref[i : i + 1, :], (FEATS, COLS))
        own = jnp.take_along_axis(mean, index, axis=1)
        away = x_ref[:, part].astype(jnp.float32) - own
        square = away * away
        high = square.astype(jnp.bfloat16)
        hi_ref[:, part] = high
        lo_ref[:, part] = (square - high.astype(jnp.float32)).astype(jnp.bfloat16)
    spread = lax.dot_general(
        hi_ref[...], hot, NT, preferred_element_type=jnp.float32
    ) + lax.dot_general(lo_ref[...], hot, NT, preferred_element_type=jnp.float32)
    store_parts(stats_ref, (mean[:COLS].T, mean[COLS:].T, spread[:COLS].T, spread[COLS:].T))
    for c in range(CHUNKS):
        pltpu.make_async_copy(moved_ref.at[c], moved_hbm.at[c], out_sem.at[c]).wait()


def store_parts(ref, parts):
    for k, part in enumerate(parts):
        ref[pl.ds(k, part.shape[0], stride=4), :] = part


def load_parts(ref):
    return [ref[pl.ds(k, ref.shape[0] // 4, stride=4), :] for k in range(4)]


def batch_kernel(order_ref, owner_ref, batch_ref, hot_ref):
    order = order_ref[...]
    shape = (32, order.shape[1])
    high = lax.broadcasted_iota(jnp.int32, shape, 0) == order // COLS
    left = jnp.where(high, owner_ref[...], 0.0).astype(jnp.bfloat16)
    shape = (COLS, order.shape[1])
    low = lax.broadcasted_iota(jnp.int32, shape, 0) == order % COLS
    right = jnp.where(low, 1.0, 0.0).astype(jnp.bfloat16)
    found = lax.dot_general(left, right, NT, preferred_element_type=jnp.float32)
    batch = found[:ROWS].astype(jnp.int32)
    batch_ref[...] = batch
    groups = lax.broadcasted_iota(jnp.int32, (COLS, COLS), 0)
    for i in range(ROWS):
        hot_ref[:, COLS * i : COLS * (i + 1)] = jnp.where(
            groups == batch[i : i + 1, :], 1.0, 0.0
        ).astype(jnp.bfloat16)


def merge_kernel(share, stats_ref, gain_ref, out_ref):
    count = stats_ref.shape[0] // 4
    parts = load_parts(stats_ref)
    merged = []
    for k in range(2):
        mean = jnp.sum(parts[k], axis=0, keepdims=True) * (1.0 / count)
        away = parts[k] - mean
        total = jnp.sum(parts[k + 2] + share * (away * away), axis=0, keepdims=True)
        gain = gain_ref[:, COLS * k : COLS * (k + 1)]
        merged.append((mean, lax.rsqrt(total * (1.0 / (count * share)) + 1e-05) * gain))
    values = (merged[0][0], merged[1][0], merged[0][1], merged[1][1])
    store_parts(out_ref, [jnp.broadcast_to(v, (count, COLS)) for v in values])


def network_kernel(
    moved_ref,
    batch_ref,
    stats_ref,
    shift_ref,
    first_ref,
    inner_ref,
    last_ref,
    bias_ref,
    final_ref,
    out_block_ref,
    mean_ref,
    scale_ref,
):
    out_ref = out_block_ref.reshape(FIELDS * LEVELS * 8, COLS)

    @pl.when(pl.program_id(0) == 0)
    def _():
        parts = load_parts(stats_ref)
        for k in range(2):
            mean_ref[COLS * k : COLS * (k + 1), :] = parts[k].T
            scale_ref[COLS * k : COLS * (k + 1), :] = parts[k + 2].T

    mean = mean_ref[...]
    scale = scale_ref[...]
    shift = shift_ref[...]

    def dot(a, b):
        return lax.dot_general(a, b, NN, preferred_element_type=jnp.float32)

    def act(product, layer):
        t = product + bias_ref[layer : layer + 1, :]
        return (t + t * jnp.tanh(t)).astype(jnp.bfloat16)

    normed = []
    for i in range(8):
        index = jnp.broadcast_to(batch_ref[i : i + 1, :], (FEATS, COLS))
        x = moved_ref[:, i].reshape(FEATS, COLS).astype(jnp.bfloat16).astype(jnp.float32)
        away = x - jnp.take_along_axis(mean, index, axis=1)
        tile = away * jnp.take_along_axis(scale, index, axis=1) + shift
        normed.append(tile.T.astype(jnp.bfloat16))
    hidden = act(dot(jnp.concatenate(normed, axis=0), first_ref[...]), 0)
    for layer in range(3):
        hidden = act(dot(hidden, inner_ref[layer]), layer + 1)
    tendency = dot(hidden, last_ref[...]) + final_ref[...]
    tendency = tendency.astype(jnp.bfloat16).astype(jnp.float32)
    for i in range(8):
        change = tendency[COLS * i : COLS * (i + 1), :].T
        for chunk in range(CHUNKS):
            rows = min(8, LEVELS - 8 * chunk)
            for f in range(FIELDS):
                row = 32 * chunk + 8 * f
                new = moved_ref[chunk, i, 8 * f : 8 * f + rows, :] + change[row : row + rows]
                out_ref[pl.ds((LEVELS * f + 8 * chunk) * 8 + i, rows, stride=8), :] = new


def whole(shape):
    return pl.BlockSpec(shape, lambda c: (0,) * len(shape))


EDGE_ROWS = 8 * (2 * FIELDS + 1)
SCALAR_SPEC = pl.BlockSpec(memory_space=pltpu.SMEM)
VMEM_SPEC = pl.BlockSpec(memory_space=pltpu.VMEM)
HBM_SPEC = pl.BlockSpec(memory_space=pltpu.HBM)
GRID_SHAPE = (CHUNKS, ROWS, 32, COLS)
LEVEL_SHAPE = (CHUNKS, 4, 8 * ROWS, COLS)


def f32(*shape):
    return jax.ShapeDtypeStruct(shape, jnp.float32)


def cost(flops, size):
    return pl.CostEstimate(flops=flops, bytes_accessed=size, transcendentals=0)


def swap(values, axis, first):
    count = lax.axis_size(axis)
    step = 0 if first else 1
    pairs = [((i + step) % count, (i + 1 + step) % count) for i in range(0, count, 2)]
    return lax.ppermute(values, axis, pairs + [(b, a) for a, b in pairs])


def by_row(values):
    rest = values.shape[1:]
    values = values.reshape(FIELDS, LEVELS, *rest)
    values = jnp.pad(values, ((0, 0), (0, 64 - LEVELS)) + ((0, 0),) * len(rest))
    values = values.reshape(FIELDS, CHUNKS, 8, *rest).swapaxes(0, 1)
    return values.reshape(FEATS, *rest)


def body(
    tracers,
    rates,
    column_order,
    norm_gain,
    norm_shift,
    weight_first,
    weight_hidden,
    weight_last,
    bias_hidden,
    bias_last,
):
    count = lax.axis_size("bx") * lax.axis_size("by")
    columns = ROWS * COLS
    share = columns // count
    width = weight_first.shape[0]
    x = tracers.reshape(FIELDS, LEVELS * ROWS, COLS)
    r = rates.reshape(4, LEVELS * ROWS, COLS)
    parity = jnp.stack([lax.axis_index("bx"), lax.axis_index("by")]).astype(jnp.int32) % 2

    dma = pltpu.SemaphoreType.DMA
    part, near, far, cols = pl.pallas_call(
        first_kernel,
        in_specs=[SCALAR_SPEC, HBM_SPEC, HBM_SPEC],
        out_specs=[HBM_SPEC, VMEM_SPEC, VMEM_SPEC, VMEM_SPEC],
        out_shape=[
            f32(*GRID_SHAPE),
            f32(CHUNKS * EDGE_ROWS, COLS),
            f32(CHUNKS * EDGE_ROWS, COLS),
            f32(3 * 64, 2 * COLS),
        ],
        scratch_shapes=[
            pltpu.VMEM(LEVEL_SHAPE, jnp.float32),
            pltpu.VMEM(LEVEL_SHAPE, jnp.float32),
            pltpu.VMEM(GRID_SHAPE, jnp.float32),
            dma((CHUNKS,)),
            dma((CHUNKS,)),
            dma((CHUNKS,)),
        ],
        compiler_params=params(),
        cost_estimate=cost(10**7, 9 * 10**6),
        name="first_substep",
    )(parity, x, r)
    core = swap(cols, "by", True)
    chip = swap(cols, "by", False)
    near_in = swap(near, "bx", True)
    far_in = swap(far, "bx", False)
    corners = pl.pallas_call(
        corner_kernel,
        in_specs=[SCALAR_SPEC, VMEM_SPEC, VMEM_SPEC, VMEM_SPEC],
        out_specs=[VMEM_SPEC, VMEM_SPEC],
        out_shape=[f32(64, COLS), f32(64, COLS)],
        compiler_params=params(limit=32),
        cost_estimate=cost(10**5, 10**6),
        name="corners",
    )(parity, cols, core, chip)
    corner_near = swap(corners[0], "bx", True)
    corner_far = swap(corners[1], "bx", False)

    owner = (jnp.arange(columns, dtype=jnp.int32) // share).astype(jnp.float32)[None, :]
    batch, hot = pl.pallas_call(
        batch_kernel,
        in_specs=[VMEM_SPEC, VMEM_SPEC],
        out_specs=[VMEM_SPEC, VMEM_SPEC],
        out_shape=[
            jax.ShapeDtypeStruct((ROWS, COLS), jnp.int32),
            jax.ShapeDtypeStruct((COLS, columns), jnp.bfloat16),
        ],
        compiler_params=params(),
        cost_estimate=cost(10**9, 2 * 10**6),
        name="batch_ids",
    )(column_order, owner)

    moved, stats = pl.pallas_call(
        functools.partial(second_kernel, share),
        in_specs=[SCALAR_SPEC, HBM_SPEC, HBM_SPEC] + [VMEM_SPEC] * 9 + [HBM_SPEC, VMEM_SPEC],
        out_specs=[HBM_SPEC, VMEM_SPEC],
        out_shape=[f32(*GRID_SHAPE), f32(4 * count, COLS)],
        scratch_shapes=[
            pltpu.VMEM(GRID_SHAPE, jnp.float32),
            pltpu.VMEM(LEVEL_SHAPE, jnp.float32),
            pltpu.VMEM((COLS, columns), jnp.bfloat16),
            pltpu.VMEM(GRID_SHAPE, jnp.float32),
            pltpu.VMEM((FEATS, columns), jnp.bfloat16),
            pltpu.VMEM((FEATS, columns), jnp.bfloat16),
            pltpu.VMEM((FEATS, columns), jnp.bfloat16),
            dma((CHUNKS,)),
            dma((CHUNKS,)),
            dma((CHUNKS,)),
            dma,
        ],
        compiler_params=params(),
        cost_estimate=cost(10**9, 9 * 10**6),
        name="second_substep",
    )(
        parity,
        part,
        r,
        near,
        far,
        near_in,
        far_in,
        cols,
        core,
        chip,
        corner_near,
        corner_far,
        hot,
        batch,
    )

    gathered = lax.all_to_all(stats, ("bx", "by"), split_axis=0, concat_axis=0, tiled=True)
    merged = pl.pallas_call(
        functools.partial(merge_kernel, float(share)),
        in_specs=[VMEM_SPEC, VMEM_SPEC],
        out_specs=VMEM_SPEC,
        out_shape=jax.ShapeDtypeStruct((4 * count, COLS), jnp.float32),
        compiler_params=params(),
        cost_estimate=cost(10**6, 10**6),
        name="merge_statistics",
    )(gathered, by_row(norm_gain)[None, :])
    known = lax.all_to_all(merged, ("bx", "by"), split_axis=0, concat_axis=0, tiled=True)

    half = jnp.bfloat16(0.5)
    new = pl.pallas_call(
        network_kernel,
        grid=(3,),
        in_specs=[
            pl.BlockSpec((CHUNKS, 8, 32, COLS), lambda c: (0, c, 0, 0)),
            pl.BlockSpec((8, COLS), lambda c: (c, 0)),
            whole((4 * count, COLS)),
            whole((FEATS, COLS)),
            whole((FEATS, width)),
            whole((3, width, width)),
            whole((width, FEATS)),
            whole((4, width)),
            whole((1, FEATS)),
        ],
        out_specs=pl.BlockSpec((FIELDS * LEVELS, 8, COLS), lambda c: (0, c, 0)),
        out_shape=f32(FIELDS * LEVELS, ROWS, COLS),
        scratch_shapes=[pltpu.VMEM((FEATS, COLS), jnp.float32) for _ in range(2)],
        compiler_params=params(True),
        cost_estimate=cost(6 * 10**9, 9 * 10**6),
        name="network",
    )(
        moved,
        batch,
        known,
        jnp.broadcast_to(by_row(norm_shift)[:, None], (FEATS, COLS)),
        by_row(weight_first.T) * half,
        weight_hidden.swapaxes(1, 2) * half,
        by_row(weight_last).T,
        bias_hidden * 0.5,
        by_row(bias_last)[None, :],
    )
    return new.reshape(tracers.shape)


def solution(mesh):
    placed = (
        P(None, None, "bx", "by"),
        P(None, None, "bx", "by"),
        P(("bx", "by"), None),
        P(),
        P(),
        P(),
        P(),
        P(),
        P(),
        P(),
    )
    return jax.shard_map(
        body, mesh=mesh, in_specs=placed, out_specs=P(None, None, "bx", "by"), check_vma=False
    )
```

```python
import functools

import jax
import jax.numpy as jnp
from jax import lax
from jax.experimental import pallas as pl
from jax.experimental.pallas import tpu as pltpu
from jax.sharding import PartitionSpec as P

FIELDS = 4
LEVELS = 60
CHUNKS = 8
ROWS = 24
COLS = 128
FEATS = 256
HALF = ROWS // 2
MIB = 1 << 20
NT = (((1,), (1,)), ((), ()))
NN = (((1,), (0,)), ((), ()))


def params(limit):
    return pltpu.CompilerParams(vmem_limit_bytes=limit * MIB)


def lanes_of(shape):
    return lax.broadcasted_iota(jnp.int32, shape, 1)


def valid_rows(chunk):
    level = chunk * 8 + lax.broadcasted_iota(jnp.int32, (8, COLS), 0)
    return level < LEVELS


def level_copies(hbm_ref, vmem_ref, sem):
    copies = []
    for c in range(CHUNKS):
        rows = ROWS * min(8, LEVELS - 8 * c)
        copies.append(
            pltpu.make_async_copy(
                hbm_ref.at[:, pl.ds(8 * ROWS * c, rows), :],
                vmem_ref.at[c, :, pl.ds(0, rows), :],
                sem.at[c],
            )
        )
    return copies


def wait_for(chunk, *groups):
    for c in range(CHUNKS):

        @pl.when(chunk == c)
        def _(c=c):
            for copies in groups:
                copies[c].wait()


class ColumnPacker:
    def __init__(self):
        self.pair = lanes_of((8, COLS)) // 2
        self.halves = [jnp.zeros((8, COLS), jnp.float32) for _ in range(2)]

    def add(self, i, f, tile):
        m = 4 * (i % HALF) + f
        moved = pltpu.roll(tile, 2 * m + 1, axis=1)
        self.halves[i // HALF] = jnp.where(self.pair == m, moved, self.halves[i // HALF])

    def store(self, ref, row):
        for h in range(2):
            ref[pl.ds(row, 8), COLS * h : COLS * (h + 1)] = self.halves[h]


def pair_of(last, first):
    return jnp.where(
        lanes_of((8, COLS)) % 2 == 0,
        jnp.broadcast_to(last[:, COLS - 1 :], (8, COLS)),
        jnp.broadcast_to(first[:, :1], (8, COLS)),
    )


def is_even(axis):
    return jnp.full((8, COLS), lax.axis_index(axis) % 2, jnp.int32) == 0


def mixed(rate, here, below, above, after, before):
    return (
        here
        + rate[0] * (below - here)
        + rate[1] * (above - here)
        + rate[2] * (after - here)
        + rate[3] * (before - here)
    )


def first_kernel(
    x_hbm,
    r_hbm,
    part_hbm,
    near_out_ref,
    far_out_ref,
    cols_out_ref,
    x_ref,
    r_ref,
    part_ref,
    near_ref,
    far_ref,
    cols_ref,
    x_sem,
    r_sem,
    out_sem,
):
    x_copies = level_copies(x_hbm, x_ref, x_sem)
    r_copies = level_copies(r_hbm, r_ref, r_sem)
    for c in range(CHUNKS):
        x_copies[c].start()
        r_copies[c].start()
    lane = lanes_of((8, COLS))
    zero = jnp.zeros((8, COLS), jnp.float32)
    even = is_even("bx")

    def one_chunk(c, carry):
        valid = valid_rows(c)
        wait_for(c, x_copies, r_copies)

        def cell(i, f):
            return jnp.where(valid, x_ref[c, f, pl.ds(i, 8, stride=ROWS), :], 0.0)

        def rate_of(i, k):
            return jnp.where(valid, r_ref[c, k, pl.ds(i, 8, stride=ROWS), :], 0.0)

        for i in range(ROWS):
            rate = [rate_of(i, k) for k in range(4)]
            for f in range(FIELDS):
                here = cell(i, f)
                part_ref[c, i, 8 * f : 8 * f + 8, :] = mixed(
                    rate,
                    here,
                    cell(i + 1, f) if i < ROWS - 1 else zero,
                    cell(i - 1, f) if i > 0 else zero,
                    jnp.where(lane == COLS - 1, 0.0, pltpu.roll(here, COLS - 1, axis=1)),
                    jnp.where(lane == 0, 0.0, pltpu.roll(here, 1, axis=1)),
                )
        pltpu.make_async_copy(part_ref.at[c], part_hbm.at[c], out_sem.at[c]).start()

        start = pl.multiple_of(EDGE_ROWS * c, 8)
        for f in range(2 * FIELDS + 1):
            if f < FIELDS:
                last, first = cell(ROWS - 1, f), cell(0, f)
            elif f < 2 * FIELDS:
                rows = slice(8 * (f - FIELDS), 8 * (f - FIELDS) + 8)
                last, first = part_ref[c, ROWS - 1, rows, :], part_ref[c, 0, rows, :]
            else:
                last, first = rate_of(ROWS - 1, 0), rate_of(0, 1)
            near_ref[pl.ds(start + 8 * f, 8), :] = jnp.where(even, last, first)
            far_ref[pl.ds(start + 8 * f, 8), :] = jnp.where(even, first, last)

        row = pl.multiple_of(8 * c, 8)
        packer = ColumnPacker()
        for i in range(ROWS):
            for f in range(FIELDS):
                packer.add(i, f, cell(i, f))
        packer.store(cols_ref, row)
        packer = ColumnPacker()
        for i in range(ROWS):
            for f in range(FIELDS):
                packer.add(i, f, part_ref[c, i, 8 * f : 8 * f + 8, :])
        packer.store(cols_ref, 64 + row)
        for h in range(2):
            acc = zero
            for i in range(HALF):
                pair = pair_of(rate_of(HALF * h + i, 2), rate_of(HALF * h + i, 3))
                acc = jnp.where(lane // 8 == i, pair, acc)
            outer = rate_of(0, 1) if h == 0 else rate_of(ROWS - 1, 0)
            acc = jnp.where(lane // 8 == HALF, pair_of(outer, outer), acc)
            cols_ref[pl.ds(128 + row, 8), COLS * h : COLS * (h + 1)] = acc
        return carry

    lax.fori_loop(0, CHUNKS, one_chunk, 0)
    for out, kept in ((near_out_ref, near_ref), (far_out_ref, far_ref)):
        out[...] = kept[...].astype(jnp.bfloat16)
    cols_out_ref[...] = cols_ref[...].astype(jnp.bfloat16)
    for c in range(CHUNKS):
        pltpu.make_async_copy(part_ref.at[c], part_hbm.at[c], out_sem.at[c]).wait()


def merged_columns(even_y, core, chip):
    right = jnp.where(even_y, core, chip)
    left = jnp.where(even_y, chip, core)
    return jnp.where(
        lanes_of((8, COLS)) % 2 == 0,
        pltpu.roll(right, COLS - 1, axis=1),
        pltpu.roll(left, 1, axis=1),
    )


def corner_kernel(cols_ref, core_ref, chip_ref, near_in, far_in, near_ref, far_ref):
    even = is_even("bx")
    even_y = is_even("by")
    lane = lanes_of((8, COLS))
    cols = cols_ref[...].astype(jnp.float32)
    core = core_ref[...].astype(jnp.float32)
    chip = chip_ref[...].astype(jnp.float32)
    nears, fars = [], []
    for c in range(CHUNKS):
        sent = []
        for h in range(2):
            part = slice(COLS * h, COLS * (h + 1))
            rows = slice(8 * c, 8 * c + 8)
            beside = merged_columns(even_y, core[rows, part], chip[rows, part])
            given = cols[128 + 8 * c : 136 + 8 * c, part] * beside
            back = 8 * (HALF - 1) * h
            sent.append(
                jnp.where(
                    lane < 8,
                    pltpu.roll(beside, (COLS - back) % COLS, axis=1),
                    pltpu.roll(given, (COLS + 8 - back) % COLS, axis=1),
                )
            )
        first, last = sent
        nears.append(jnp.where(even, last, first))
        fars.append(jnp.where(even, first, last))
    for out, given, corner in ((near_ref, near_in, nears), (far_ref, far_in, fars)):
        out[:EDGES, :] = given[...]
        out[EDGES:, :] = jnp.concatenate(corner, axis=0).astype(jnp.bfloat16)


def second_kernel(
    share,
    part_hbm,
    r_hbm,
    own_near_in,
    own_far_in,
    near_in,
    far_in,
    cols_in,
    core_in,
    chip_in,
    hot_hbm,
    batch_ref,
    moved_hbm,
    stats_ref,
    part_ref,
    r_ref,
    hot_ref,
    moved_ref,
    x_ref,
    hi_ref,
    lo_ref,
    own_near_ref,
    own_far_ref,
    near_ref,
    far_ref,
    cols_ref,
    core_ref,
    chip_ref,
    part_sem,
    r_sem,
    out_sem,
    hot_sem,
):
    part_copies = [
        pltpu.make_async_copy(part_hbm.at[c], part_ref.at[c], part_sem.at[c])
        for c in range(CHUNKS)
    ]
    r_copies = level_copies(r_hbm, r_ref, r_sem)
    for c in range(CHUNKS):
        part_copies[c].start()
        r_copies[c].start()
    hot_copy = pltpu.make_async_copy(hot_hbm, hot_ref, hot_sem)
    hot_copy.start()
    for kept, given in (
        (own_near_ref, own_near_in),
        (own_far_ref, own_far_in),
        (near_ref, near_in),
        (far_ref, far_in),
        (cols_ref, cols_in),
        (core_ref, core_in),
        (chip_ref, chip_in),
    ):
        kept[...] = given[...].astype(jnp.float32)
    lane = lanes_of((8, COLS))
    rim = (lane == 0) | (lane == COLS - 1)
    even = is_even("bx")
    even_y = is_even("by")

    def one_chunk(c, carry):
        valid = valid_rows(c)
        row = pl.multiple_of(8 * c, 8)
        start = pl.multiple_of(EDGE_ROWS * c, 8)
        wait_for(c, part_copies, r_copies)

        def edge(near, far, f, below):
            a, b = near[pl.ds(start + 8 * f, 8), :], far[pl.ds(start + 8 * f, 8), :]
            return jnp.where(even, a, b) if below else jnp.where(even, b, a)

        def rate_of(i, k):
            return r_ref[c, k, pl.ds(i, 8, stride=ROWS), :]

        corner = [near_ref[pl.ds(EDGES + row, 8), :], far_ref[pl.ds(EDGES + row, 8), :]]
        corner = [jnp.where(even, corner[1], corner[0]), jnp.where(even, corner[0], corner[1])]
        rings, gains = [], []
        for h in range(2):
            lanes = slice(COLS * h, COLS * (h + 1))
            cells, parts, rates = (
                merged_columns(
                    even_y,
                    core_ref[pl.ds(64 * k + row, 8), lanes],
                    chip_ref[pl.ds(64 * k + row, 8), lanes],
                )
                for k in range(3)
            )
            diagonal = corner[h]
            if h == 1:
                diagonal = pltpu.roll(diagonal, 8 * (HALF - 1), axis=1)
            shift = COLS - 8 * HALF if h == 0 else COLS - 8
            spot = lane // 8 == (0 if h == 0 else HALF - 1)
            extra = jnp.where(spot, pltpu.roll(rates, shift, axis=1) * diagonal, 0.0)
            rings.append(parts + rates * cols_ref[pl.ds(row, 8), lanes] + extra)
            gains.append(cols_ref[pl.ds(128 + row, 8), lanes] * cells)

        outer = []
        for side, i in enumerate((0, ROWS - 1)):
            down = side == 1
            rate = edge(near_ref, far_ref, 2 * FIELDS, down)
            tiles = []
            for f in range(FIELDS):
                turned = pltpu.roll(corner[side], COLS - (9 + 2 * f), axis=1)
                tiles.append(
                    edge(near_ref, far_ref, FIELDS + f, down)
                    + rate * edge(own_near_ref, own_far_ref, f, down)
                    + jnp.where(rim, turned, 0.0)
                )
            outer.append(tiles)

        for i in range(ROWS):
            for f in range(FIELDS):
                m = 4 * (i % HALF) + f
                turned = pltpu.roll(gains[i // HALF], COLS - (2 * m + 1), axis=1)
                tile = part_ref[c, i, 8 * f : 8 * f + 8, :] + jnp.where(rim, turned, 0.0)
                if i == 0:
                    tile = tile + rate_of(0, 1) * edge(near_ref, far_ref, f, False)
                if i == ROWS - 1:
                    tile = tile + rate_of(ROWS - 1, 0) * edge(near_ref, far_ref, f, True)
                part_ref[c, i, 8 * f : 8 * f + 8, :] = tile

        for i in range(ROWS):
            rate = [rate_of(i, k) for k in range(4)]
            kept = []
            for f in range(FIELDS):
                rows = slice(8 * f, 8 * f + 8)
                m = 4 * (i % HALF) + f
                here = part_ref[c, i, rows, :]
                above = outer[0][f] if i == 0 else part_ref[c, i - 1, rows, :]
                below = outer[1][f] if i == ROWS - 1 else part_ref[c, i + 1, rows, :]
                turned = pltpu.roll(rings[i // HALF], COLS - (2 * m + 1), axis=1)
                after = jnp.where(lane == COLS - 1, turned, pltpu.roll(here, COLS - 1, axis=1))
                before = jnp.where(lane == 0, turned, pltpu.roll(here, 1, axis=1))
                tile = jnp.where(valid, mixed(rate, here, below, above, after, before), 0.0)
                moved_ref[c, i, rows, :] = tile
                kept.append(tile)
            for f in (0, 2):
                both = jnp.concatenate(kept[f : f + 2], axis=0).astype(jnp.bfloat16)
                x_ref[pl.ds(pl.multiple_of(32 * c + 8 * f, 16), 16), COLS * i : COLS * (i + 1)] = (
                    both
                )
        pltpu.make_async_copy(moved_ref.at[c], moved_hbm.at[c], out_sem.at[c]).start()
        return carry

    lax.fori_loop(0, CHUNKS, one_chunk, 0)
    hot_copy.wait()
    hot = hot_ref[...]
    sums = lax.dot_general(x_ref[...], hot, NT, preferred_element_type=jnp.float32)
    mean = sums * (1.0 / share)
    for i in range(ROWS):
        part = slice(COLS * i, COLS * (i + 1))
        index = jnp.broadcast_to(batch_ref[i : i + 1, :], (FEATS, COLS))
        own = jnp.take_along_axis(mean, index, axis=1)
        away = x_ref[:, part].astype(jnp.float32) - own
        square = away * away
        high = square.astype(jnp.bfloat16)
        hi_ref[:, part] = high
        lo_ref[:, part] = (square - high.astype(jnp.float32)).astype(jnp.bfloat16)
    spread = lax.dot_general(
        hi_ref[...], hot, NT, preferred_element_type=jnp.float32
    ) + lax.dot_general(lo_ref[...], hot, NT, preferred_element_type=jnp.float32)
    store_parts(stats_ref, (mean[:COLS].T, mean[COLS:].T, spread[:COLS].T, spread[COLS:].T))
    for c in range(CHUNKS):
        pltpu.make_async_copy(moved_ref.at[c], moved_hbm.at[c], out_sem.at[c]).wait()


def store_parts(ref, parts):
    for k, part in enumerate(parts):
        ref[pl.ds(k, part.shape[0], stride=4), :] = part


def load_parts(ref):
    return [ref[pl.ds(k, ref.shape[0] // 4, stride=4), :] for k in range(4)]


def batch_kernel(order_ref, owner_ref, batch_ref, hot_ref):
    order = order_ref[...]
    shape = (32, order.shape[1])
    high = lax.broadcasted_iota(jnp.int32, shape, 0) == order // COLS
    left = jnp.where(high, owner_ref[...], 0.0).astype(jnp.bfloat16)
    shape = (COLS, order.shape[1])
    low = lax.broadcasted_iota(jnp.int32, shape, 0) == order % COLS
    right = jnp.where(low, 1.0, 0.0).astype(jnp.bfloat16)
    found = lax.dot_general(left, right, NT, preferred_element_type=jnp.float32)
    batch = found[:ROWS].astype(jnp.int32)
    batch_ref[...] = batch
    groups = lax.broadcasted_iota(jnp.int32, (COLS, COLS), 0)
    for i in range(ROWS):
        hot_ref[:, COLS * i : COLS * (i + 1)] = jnp.where(
            groups == batch[i : i + 1, :], 1.0, 0.0
        ).astype(jnp.bfloat16)


def merge_kernel(share, stats_ref, gain_ref, out_ref):
    count = stats_ref.shape[0] // 4
    parts = load_parts(stats_ref)
    merged = []
    for k in range(2):
        mean = jnp.sum(parts[k], axis=0, keepdims=True) * (1.0 / count)
        away = parts[k] - mean
        total = jnp.sum(parts[k + 2] + share * (away * away), axis=0, keepdims=True)
        gain = gain_ref[:, COLS * k : COLS * (k + 1)]
        merged.append((mean, lax.rsqrt(total * (1.0 / (count * share)) + 1e-05) * gain))
    values = (merged[0][0], merged[1][0], merged[0][1], merged[1][1])
    store_parts(out_ref, [jnp.broadcast_to(v, (count, COLS)) for v in values])


def network_kernel(
    moved_hbm,
    batch_ref,
    stats_hbm,
    shift_ref,
    first_hbm,
    inner_hbm,
    last_hbm,
    bias_ref,
    final_ref,
    out_hbm,
    moved_ref,
    stats_ref,
    first_ref,
    inner_ref,
    last_ref,
    out_ref,
    mean_ref,
    scale_ref,
    even_ref,
    odd_ref,
    moved_sem,
    weight_sem,
    out_sem,
):
    blocks = ROWS // BLOCK
    moved_copies = [
        pltpu.make_async_copy(
            moved_hbm.at[:, pl.ds(BLOCK * b, BLOCK)],
            moved_ref.at[:, pl.ds(BLOCK * b, BLOCK)],
            moved_sem.at[b],
        )
        for b in range(blocks)
    ]
    stats_copy = pltpu.make_async_copy(stats_hbm, stats_ref, weight_sem.at[0])
    weight_copies = [
        pltpu.make_async_copy(given, kept, weight_sem.at[k + 1])
        for k, (given, kept) in enumerate(
            ((first_hbm, first_ref), (inner_hbm, inner_ref), (last_hbm, last_ref))
        )
    ]
    stats_copy.start()
    moved_copies[0].start()
    for copy in weight_copies + moved_copies[1:]:
        copy.start()
    stats_copy.wait()
    parts = load_parts(stats_ref)
    for k in range(2):
        mean_ref[COLS * k : COLS * (k + 1), :] = parts[k].T
        scale_ref[COLS * k : COLS * (k + 1), :] = parts[k + 2].T
    out_rows = out_ref.reshape(FIELDS * LEVELS * ROWS, COLS)

    def dot(a, b):
        return lax.dot_general(a, b, NN, preferred_element_type=jnp.float32)

    def act(product, layer):
        t = product + bias_ref[layer : layer + 1, :]
        return (t + t * jnp.tanh(t)).astype(jnp.bfloat16)

    def normalize(block, normed_ref):
        mean, scale = mean_ref[...], scale_ref[...]
        for k in range(BLOCK):
            i = BLOCK * block + k
            index = jnp.broadcast_to(batch_ref[pl.ds(i, 1), :], (FEATS, COLS))
            x = moved_ref[:, i].reshape(FEATS, COLS).astype(jnp.bfloat16).astype(jnp.float32)
            away = x - jnp.take_along_axis(mean, index, axis=1)
            tile = away * jnp.take_along_axis(scale, index, axis=1)
            normed_ref[COLS * k : COLS * (k + 1), :] = (tile.T + shift_ref[...]).astype(
                jnp.bfloat16
            )

    def layers(block, normed_ref):
        hidden = act(dot(normed_ref[...], first_ref[...]), 0)
        for layer in range(3):
            hidden = act(dot(hidden, inner_ref[layer]), layer + 1)
        tendency = dot(hidden, last_ref[...]) + final_ref[...]
        tendency = tendency.astype(jnp.bfloat16).astype(jnp.float32)
        for k in range(BLOCK):
            i = BLOCK * block + k
            change = tendency[COLS * k : COLS * (k + 1), :].T
            for chunk in range(CHUNKS):
                rows = min(8, LEVELS - 8 * chunk)
                for f in range(FIELDS):
                    row = 32 * chunk + 8 * f
                    new = moved_ref[chunk, i, 8 * f : 8 * f + rows, :] + change[row : row + rows]
                    start = (LEVELS * f + 8 * chunk) * ROWS + i
                    out_rows[pl.ds(start, rows, stride=ROWS), :] = new

    def out_copy(group):
        part = pl.ds(pl.multiple_of(8 * group, 8), 8)
        return pltpu.make_async_copy(
            out_ref.at[:, part, :], out_hbm.at[:, part, :], out_sem.at[group]
        )

    moved_copies[0].wait()
    normalize(0, even_ref)
    for copy in weight_copies + moved_copies[1:]:
        copy.wait()

    def two_blocks(group, carry):
        block = 2 * group
        normalize(block + 1, odd_ref)
        layers(block, even_ref)
        normalize(jnp.minimum(block + 2, blocks - 1), even_ref)
        layers(block + 1, odd_ref)
        out_copy(group).start()
        return carry

    lax.fori_loop(0, blocks // 2, two_blocks, 0)
    for group in range(blocks // 2):
        out_copy(group).wait()


BLOCK = 4
EDGE_ROWS = 8 * (2 * FIELDS + 1)
EDGES = CHUNKS * EDGE_ROWS
VMEM_SPEC = pl.BlockSpec(memory_space=pltpu.VMEM)
HBM_SPEC = pl.BlockSpec(memory_space=pltpu.HBM)
GRID_SHAPE = (CHUNKS, ROWS, 32, COLS)
LEVEL_SHAPE = (CHUNKS, 4, 8 * ROWS, COLS)


def f32(*shape):
    return jax.ShapeDtypeStruct(shape, jnp.float32)


def bf16(*shape):
    return jax.ShapeDtypeStruct(shape, jnp.bfloat16)


def cost(flops, size):
    return pl.CostEstimate(flops=flops, bytes_accessed=size, transcendentals=0)


def swap(values, axis, first):
    count = lax.axis_size(axis)
    step = 0 if first else 1
    pairs = [((i + step) % count, (i + 1 + step) % count) for i in range(0, count, 2)]
    return lax.ppermute(values, axis, pairs + [(b, a) for a, b in pairs])


def by_row(values):
    rest = values.shape[1:]
    values = values.reshape(FIELDS, LEVELS, *rest)
    values = jnp.pad(values, ((0, 0), (0, 64 - LEVELS)) + ((0, 0),) * len(rest))
    values = values.reshape(FIELDS, CHUNKS, 8, *rest).swapaxes(0, 1)
    return values.reshape(FEATS, *rest)


def body(
    tracers,
    rates,
    column_order,
    norm_gain,
    norm_shift,
    weight_first,
    weight_hidden,
    weight_last,
    bias_hidden,
    bias_last,
):
    count = lax.axis_size("bx") * lax.axis_size("by")
    columns = ROWS * COLS
    share = columns // count
    width = weight_first.shape[0]
    x = tracers.reshape(FIELDS, LEVELS * ROWS, COLS)
    r = rates.reshape(4, LEVELS * ROWS, COLS)

    dma = pltpu.SemaphoreType.DMA
    part, near, far, cols = pl.pallas_call(
        first_kernel,
        in_specs=[HBM_SPEC, HBM_SPEC],
        out_specs=[HBM_SPEC, VMEM_SPEC, VMEM_SPEC, VMEM_SPEC],
        out_shape=[
            f32(*GRID_SHAPE),
            bf16(EDGES, COLS),
            bf16(EDGES, COLS),
            bf16(3 * 64, 2 * COLS),
        ],
        scratch_shapes=[
            pltpu.VMEM(LEVEL_SHAPE, jnp.float32),
            pltpu.VMEM(LEVEL_SHAPE, jnp.float32),
            pltpu.VMEM(GRID_SHAPE, jnp.float32),
            pltpu.VMEM((EDGES, COLS), jnp.float32),
            pltpu.VMEM((EDGES, COLS), jnp.float32),
            pltpu.VMEM((3 * 64, 2 * COLS), jnp.float32),
            dma((CHUNKS,)),
            dma((CHUNKS,)),
            dma((CHUNKS,)),
        ],
        compiler_params=params(62),
        cost_estimate=cost(10**7, 9 * 10**6),
        name="first_substep",
    )(x, r)
    core = swap(cols, "by", True)
    chip = swap(cols, "by", False)
    near, far = pl.pallas_call(
        corner_kernel,
        in_specs=[VMEM_SPEC] * 5,
        out_specs=[VMEM_SPEC, VMEM_SPEC],
        out_shape=[bf16(EDGES + 64, COLS), bf16(EDGES + 64, COLS)],
        compiler_params=params(62),
        cost_estimate=cost(10**5, 10**6),
        name="corners",
    )(cols, core, chip, near, far)
    near_in = swap(near, "bx", True)
    far_in = swap(far, "bx", False)

    owner = (jnp.arange(columns, dtype=jnp.int32) // share).astype(jnp.float32)[None, :]
    batch, hot = pl.pallas_call(
        batch_kernel,
        in_specs=[VMEM_SPEC, VMEM_SPEC],
        out_specs=[VMEM_SPEC, VMEM_SPEC],
        out_shape=[
            jax.ShapeDtypeStruct((ROWS, COLS), jnp.int32),
            jax.ShapeDtypeStruct((COLS, columns), jnp.bfloat16),
        ],
        compiler_params=params(62),
        cost_estimate=cost(10**9, 2 * 10**6),
        name="batch_ids",
    )(column_order, owner)

    moved, stats = pl.pallas_call(
        functools.partial(second_kernel, share),
        in_specs=[HBM_SPEC, HBM_SPEC] + [VMEM_SPEC] * 7 + [HBM_SPEC, VMEM_SPEC],
        out_specs=[HBM_SPEC, VMEM_SPEC],
        out_shape=[f32(*GRID_SHAPE), f32(4 * count, COLS)],
        scratch_shapes=[
            pltpu.VMEM(GRID_SHAPE, jnp.float32),
            pltpu.VMEM(LEVEL_SHAPE, jnp.float32),
            pltpu.VMEM((COLS, columns), jnp.bfloat16),
            pltpu.VMEM(GRID_SHAPE, jnp.float32),
            pltpu.VMEM((FEATS, columns), jnp.bfloat16),
            pltpu.VMEM((FEATS, columns), jnp.bfloat16),
            pltpu.VMEM((FEATS, columns), jnp.bfloat16),
            *[pltpu.VMEM((EDGES + 64, COLS), jnp.float32) for _ in range(4)],
            *[pltpu.VMEM((3 * 64, 2 * COLS), jnp.float32) for _ in range(3)],
            dma((CHUNKS,)),
            dma((CHUNKS,)),
            dma((CHUNKS,)),
            dma,
        ],
        compiler_params=params(62),
        cost_estimate=cost(10**9, 9 * 10**6),
        name="second_substep",
    )(
        part,
        r,
        near,
        far,
        near_in,
        far_in,
        cols,
        core,
        chip,
        hot,
        batch,
    )

    stats, *raw = lax.optimization_barrier(
        (
            stats,
            norm_gain,
            norm_shift,
            weight_first,
            weight_hidden,
            weight_last,
            bias_hidden,
            bias_last,
        )
    )
    norm_gain, norm_shift, weight_first, weight_hidden, weight_last, bias_hidden, bias_last = raw
    gathered = lax.all_to_all(stats, ("bx", "by"), split_axis=0, concat_axis=0, tiled=True)
    merged = pl.pallas_call(
        functools.partial(merge_kernel, float(share)),
        in_specs=[VMEM_SPEC, VMEM_SPEC],
        out_specs=VMEM_SPEC,
        out_shape=jax.ShapeDtypeStruct((4 * count, COLS), jnp.float32),
        compiler_params=params(16),
        cost_estimate=cost(10**6, 10**6),
        name="merge_statistics",
    )(gathered, by_row(norm_gain)[None, :])
    known = lax.all_to_all(merged, ("bx", "by"), split_axis=0, concat_axis=0, tiled=True)

    half = jnp.bfloat16(0.5)
    new = pl.pallas_call(
        network_kernel,
        in_specs=[
            HBM_SPEC,
            VMEM_SPEC,
            HBM_SPEC,
            VMEM_SPEC,
            HBM_SPEC,
            HBM_SPEC,
            HBM_SPEC,
            VMEM_SPEC,
            VMEM_SPEC,
        ],
        out_specs=HBM_SPEC,
        out_shape=f32(FIELDS * LEVELS, ROWS, COLS),
        scratch_shapes=[
            pltpu.VMEM(GRID_SHAPE, jnp.float32),
            pltpu.VMEM((4 * count, COLS), jnp.float32),
            pltpu.VMEM((FEATS, width), jnp.bfloat16),
            pltpu.VMEM((3, width, width), jnp.bfloat16),
            pltpu.VMEM((width, FEATS), jnp.bfloat16),
            pltpu.VMEM((FIELDS * LEVELS, ROWS, COLS), jnp.float32),
            pltpu.VMEM((FEATS, COLS), jnp.float32),
            pltpu.VMEM((FEATS, COLS), jnp.float32),
            pltpu.VMEM((BLOCK * COLS, FEATS), jnp.bfloat16),
            pltpu.VMEM((BLOCK * COLS, FEATS), jnp.bfloat16),
            dma((ROWS // BLOCK,)),
            dma((4,)),
            dma((3,)),
        ],
        compiler_params=params(62),
        cost_estimate=cost(6 * 10**9, 9 * 10**6),
        name="network",
    )(
        moved,
        batch,
        known,
        by_row(norm_shift)[None, :],
        by_row(weight_first.T) * half,
        weight_hidden.swapaxes(1, 2) * half,
        by_row(weight_last).T,
        bias_hidden * 0.5,
        by_row(bias_last)[None, :],
    )
    return new.reshape(tracers.shape)


def solution(mesh):
    placed = (
        P(None, None, "bx", "by"),
        P(None, None, "bx", "by"),
        P(("bx", "by"), None),
        P(),
        P(),
        P(),
        P(),
        P(),
        P(),
        P(),
    )
    return jax.shard_map(
        body, mesh=mesh, in_specs=placed, out_specs=P(None, None, "bx", "by"), check_vma=False
    )
```

```python
import functools

import jax
import jax.numpy as jnp
from jax import lax
from jax.experimental import pallas as pl
from jax.experimental.pallas import tpu as pltpu
from jax.sharding import PartitionSpec as P

FIELDS = 4
LEVELS = 60
CHUNKS = 8
ROWS = 24
COLS = 128
FEATS = 256
HALF = ROWS // 2
MIB = 1 << 20
NT = (((1,), (1,)), ((), ()))
NN = (((1,), (0,)), ((), ()))


def params(limit):
    return pltpu.CompilerParams(vmem_limit_bytes=limit * MIB)


def lanes_of(shape):
    return lax.broadcasted_iota(jnp.int32, shape, 1)


def valid_rows(chunk):
    level = chunk * 8 + lax.broadcasted_iota(jnp.int32, (8, COLS), 0)
    return level < LEVELS


def level_copies(hbm_ref, vmem_ref, sem):
    copies = []
    for c in range(CHUNKS):
        rows = ROWS * min(8, LEVELS - 8 * c)
        copies.append(
            pltpu.make_async_copy(
                hbm_ref.at[:, pl.ds(8 * ROWS * c, rows), :],
                vmem_ref.at[c, :, pl.ds(0, rows), :],
                sem.at[c],
            )
        )
    return copies


def copies_of(given, kept, sem, first=0):
    return [
        pltpu.make_async_copy(a, b, sem.at[first + k])
        for k, (a, b) in enumerate(zip(given, kept, strict=True))
    ]


def wait_for(chunk, *groups):
    for c in range(CHUNKS):

        @pl.when(chunk == c)
        def _(c=c):
            for copies in groups:
                copies[c].wait()


class ColumnPacker:
    def __init__(self):
        self.pair = lanes_of((8, COLS)) // 2
        self.halves = [jnp.zeros((8, COLS), jnp.float32) for _ in range(2)]

    def add(self, i, f, tile):
        m = 4 * (i % HALF) + f
        moved = pltpu.roll(tile, 2 * m + 1, axis=1)
        self.halves[i // HALF] = jnp.where(self.pair == m, moved, self.halves[i // HALF])

    def store(self, ref, row):
        for h in range(2):
            ref[pl.ds(row, 8), COLS * h : COLS * (h + 1)] = self.halves[h]


def pair_of(last, first):
    return jnp.where(
        lanes_of((8, COLS)) % 2 == 0,
        jnp.broadcast_to(last[:, COLS - 1 :], (8, COLS)),
        jnp.broadcast_to(first[:, :1], (8, COLS)),
    )


def is_even(axis):
    return jnp.full((8, COLS), lax.axis_index(axis) % 2, jnp.int32) == 0


def mixed(rate, here, below, above, after, before):
    return (
        here
        + rate[0] * (below - here)
        + rate[1] * (above - here)
        + rate[2] * (after - here)
        + rate[3] * (before - here)
    )


def first_kernel(
    x_hbm,
    r_hbm,
    part_hbm,
    near_hbm,
    far_hbm,
    cols_hbm,
    x_ref,
    r_ref,
    part_ref,
    near_ref,
    far_ref,
    cols_ref,
    near_out_ref,
    far_out_ref,
    cols_out_ref,
    x_sem,
    r_sem,
    out_sem,
    edge_sem,
):
    x_copies = level_copies(x_hbm, x_ref, x_sem)
    r_copies = level_copies(r_hbm, r_ref, r_sem)
    for c in range(CHUNKS):
        x_copies[c].start()
        r_copies[c].start()
    lane = lanes_of((8, COLS))
    zero = jnp.zeros((8, COLS), jnp.float32)
    even = is_even("bx")

    def one_chunk(c, carry):
        valid = valid_rows(c)
        wait_for(c, x_copies, r_copies)

        def cell(i, f):
            return jnp.where(valid, x_ref[c, f, pl.ds(i, 8, stride=ROWS), :], 0.0)

        def rate_of(i, k):
            return jnp.where(valid, r_ref[c, k, pl.ds(i, 8, stride=ROWS), :], 0.0)

        for i in range(ROWS):
            rate = [rate_of(i, k) for k in range(4)]
            for f in range(FIELDS):
                here = cell(i, f)
                part_ref[c, i, 8 * f : 8 * f + 8, :] = mixed(
                    rate,
                    here,
                    cell(i + 1, f) if i < ROWS - 1 else zero,
                    cell(i - 1, f) if i > 0 else zero,
                    jnp.where(lane == COLS - 1, 0.0, pltpu.roll(here, COLS - 1, axis=1)),
                    jnp.where(lane == 0, 0.0, pltpu.roll(here, 1, axis=1)),
                )
        pltpu.make_async_copy(part_ref.at[c], part_hbm.at[c], out_sem.at[c]).start()

        start = pl.multiple_of(EDGE_ROWS * c, 8)
        for f in range(2 * FIELDS + 1):
            if f < FIELDS:
                last, first = cell(ROWS - 1, f), cell(0, f)
            elif f < 2 * FIELDS:
                rows = slice(8 * (f - FIELDS), 8 * (f - FIELDS) + 8)
                last, first = part_ref[c, ROWS - 1, rows, :], part_ref[c, 0, rows, :]
            else:
                last, first = rate_of(ROWS - 1, 0), rate_of(0, 1)
            near_ref[pl.ds(start + 8 * f, 8), :] = jnp.where(even, last, first)
            far_ref[pl.ds(start + 8 * f, 8), :] = jnp.where(even, first, last)

        row = pl.multiple_of(8 * c, 8)
        packer = ColumnPacker()
        for i in range(ROWS):
            for f in range(FIELDS):
                packer.add(i, f, cell(i, f))
        packer.store(cols_ref, row)
        packer = ColumnPacker()
        for i in range(ROWS):
            for f in range(FIELDS):
                packer.add(i, f, part_ref[c, i, 8 * f : 8 * f + 8, :])
        packer.store(cols_ref, 64 + row)
        for h in range(2):
            acc = zero
            for i in range(HALF):
                pair = pair_of(rate_of(HALF * h + i, 2), rate_of(HALF * h + i, 3))
                acc = jnp.where(lane // 8 == i, pair, acc)
            outer = rate_of(0, 1) if h == 0 else rate_of(ROWS - 1, 0)
            acc = jnp.where(lane // 8 == HALF, pair_of(outer, outer), acc)
            cols_ref[pl.ds(128 + row, 8), COLS * h : COLS * (h + 1)] = acc
        return carry

    lax.fori_loop(0, CHUNKS, one_chunk, 0)
    for out, kept in ((near_out_ref, near_ref), (far_out_ref, far_ref)):
        out[...] = kept[...].astype(jnp.bfloat16)
    cols_out_ref[...] = cols_ref[...].astype(jnp.bfloat16)
    copies = copies_of(
        (cols_out_ref, near_out_ref, far_out_ref),
        (cols_hbm, near_hbm.at[pl.ds(0, EDGES), :], far_hbm.at[pl.ds(0, EDGES), :]),
        edge_sem,
    )
    for copy in copies:
        copy.start()
    for c in range(CHUNKS):
        pltpu.make_async_copy(part_ref.at[c], part_hbm.at[c], out_sem.at[c]).wait()
    for copy in copies:
        copy.wait()


def merged_columns(even_y, core, chip):
    right = jnp.where(even_y, core, chip)
    left = jnp.where(even_y, chip, core)
    return jnp.where(
        lanes_of((8, COLS)) % 2 == 0,
        pltpu.roll(right, COLS - 1, axis=1),
        pltpu.roll(left, 1, axis=1),
    )


def corner_kernel(
    cols_hbm,
    core_ref,
    chip_ref,
    near_in,
    far_in,
    near_hbm,
    far_hbm,
    rates_ref,
    near_ref,
    far_ref,
    sem,
):
    del near_in, far_in
    copy = pltpu.make_async_copy(cols_hbm.at[pl.ds(128, 64), :], rates_ref, sem.at[2])
    copy.start()
    copy.wait()
    even = is_even("bx")
    even_y = is_even("by")
    lane = lanes_of((8, COLS))
    rates = rates_ref[...].astype(jnp.float32)
    core = core_ref[:64, :].astype(jnp.float32)
    chip = chip_ref[:64, :].astype(jnp.float32)
    nears, fars = [], []
    for c in range(CHUNKS):
        sent = []
        for h in range(2):
            part = slice(COLS * h, COLS * (h + 1))
            rows = slice(8 * c, 8 * c + 8)
            beside = merged_columns(even_y, core[rows, part], chip[rows, part])
            given = rates[rows, part] * beside
            back = 8 * (HALF - 1) * h
            sent.append(
                jnp.where(
                    lane < 8,
                    pltpu.roll(beside, (COLS - back) % COLS, axis=1),
                    pltpu.roll(given, (COLS + 8 - back) % COLS, axis=1),
                )
            )
        first, last = sent
        nears.append(jnp.where(even, last, first))
        fars.append(jnp.where(even, first, last))
    near_ref[...] = jnp.concatenate(nears, axis=0).astype(jnp.bfloat16)
    far_ref[...] = jnp.concatenate(fars, axis=0).astype(jnp.bfloat16)
    arrays = (near_hbm.at[pl.ds(EDGES, 64), :], far_hbm.at[pl.ds(EDGES, 64), :])
    copies = copies_of((near_ref, far_ref), arrays, sem)
    for copy in copies:
        copy.start()
    for copy in copies:
        copy.wait()


def second_kernel(
    share,
    part_hbm,
    r_hbm,
    own_near_in,
    own_far_in,
    near_in,
    far_in,
    cols_in,
    core_in,
    chip_in,
    hot_hbm,
    moved_hbm,
    stats_hbm,
    part_ref,
    r_ref,
    hot_ref,
    moved_ref,
    x_ref,
    hi_ref,
    lo_ref,
    own_near_ref,
    own_far_ref,
    near_ref,
    far_ref,
    cols_ref,
    core_ref,
    chip_ref,
    own_near_16,
    own_far_16,
    near_16,
    far_16,
    cols_16,
    core_16,
    chip_16,
    stats_ref,
    part_sem,
    r_sem,
    out_sem,
    hot_sem,
    edge_sem,
):
    edges_in = (own_near_in, own_far_in, near_in, far_in, cols_in, core_in, chip_in)
    edges_16 = (own_near_16, own_far_16, near_16, far_16, cols_16, core_16, chip_16)
    edges = (own_near_ref, own_far_ref, near_ref, far_ref, cols_ref, core_ref, chip_ref)
    edge_copies = copies_of(edges_in, edges_16, edge_sem)
    for copy in edge_copies:
        copy.start()
    part_copies = [
        pltpu.make_async_copy(part_hbm.at[c], part_ref.at[c], part_sem.at[c])
        for c in range(CHUNKS)
    ]
    r_copies = level_copies(r_hbm, r_ref, r_sem)
    for c in range(CHUNKS):
        part_copies[c].start()
        r_copies[c].start()
    hot_copy = pltpu.make_async_copy(hot_hbm, hot_ref, hot_sem)
    hot_copy.start()
    for copy, kept, given in zip(edge_copies, edges, edges_16, strict=True):
        copy.wait()
        kept[...] = given[...].astype(jnp.float32)
    lane = lanes_of((8, COLS))
    rim = (lane == 0) | (lane == COLS - 1)
    even = is_even("bx")
    even_y = is_even("by")

    def one_chunk(c, carry):
        valid = valid_rows(c)
        row = pl.multiple_of(8 * c, 8)
        start = pl.multiple_of(EDGE_ROWS * c, 8)
        wait_for(c, part_copies, r_copies)

        def edge(near, far, f, below):
            a, b = near[pl.ds(start + 8 * f, 8), :], far[pl.ds(start + 8 * f, 8), :]
            return jnp.where(even, a, b) if below else jnp.where(even, b, a)

        def rate_of(i, k):
            return r_ref[c, k, pl.ds(i, 8, stride=ROWS), :]

        corner = [near_ref[pl.ds(EDGES + row, 8), :], far_ref[pl.ds(EDGES + row, 8), :]]
        corner = [jnp.where(even, corner[1], corner[0]), jnp.where(even, corner[0], corner[1])]
        rings, gains = [], []
        for h in range(2):
            lanes = slice(COLS * h, COLS * (h + 1))
            cells, parts, rates = (
                merged_columns(
                    even_y,
                    core_ref[pl.ds(64 * k + row, 8), lanes],
                    chip_ref[pl.ds(64 * k + row, 8), lanes],
                )
                for k in range(3)
            )
            diagonal = corner[h]
            if h == 1:
                diagonal = pltpu.roll(diagonal, 8 * (HALF - 1), axis=1)
            shift = COLS - 8 * HALF if h == 0 else COLS - 8
            spot = lane // 8 == (0 if h == 0 else HALF - 1)
            extra = jnp.where(spot, pltpu.roll(rates, shift, axis=1) * diagonal, 0.0)
            rings.append(parts + rates * cols_ref[pl.ds(row, 8), lanes] + extra)
            gains.append(cols_ref[pl.ds(128 + row, 8), lanes] * cells)

        outer = []
        for side, i in enumerate((0, ROWS - 1)):
            down = side == 1
            rate = edge(near_ref, far_ref, 2 * FIELDS, down)
            tiles = []
            for f in range(FIELDS):
                turned = pltpu.roll(corner[side], COLS - (9 + 2 * f), axis=1)
                tiles.append(
                    edge(near_ref, far_ref, FIELDS + f, down)
                    + rate * edge(own_near_ref, own_far_ref, f, down)
                    + jnp.where(rim, turned, 0.0)
                )
            outer.append(tiles)

        for i in range(ROWS):
            for f in range(FIELDS):
                m = 4 * (i % HALF) + f
                turned = pltpu.roll(gains[i // HALF], COLS - (2 * m + 1), axis=1)
                tile = part_ref[c, i, 8 * f : 8 * f + 8, :] + jnp.where(rim, turned, 0.0)
                if i == 0:
                    tile = tile + rate_of(0, 1) * edge(near_ref, far_ref, f, False)
                if i == ROWS - 1:
                    tile = tile + rate_of(ROWS - 1, 0) * edge(near_ref, far_ref, f, True)
                part_ref[c, i, 8 * f : 8 * f + 8, :] = tile

        for i in range(ROWS):
            rate = [rate_of(i, k) for k in range(4)]
            kept = []
            for f in range(FIELDS):
                rows = slice(8 * f, 8 * f + 8)
                m = 4 * (i % HALF) + f
                here = part_ref[c, i, rows, :]
                above = outer[0][f] if i == 0 else part_ref[c, i - 1, rows, :]
                below = outer[1][f] if i == ROWS - 1 else part_ref[c, i + 1, rows, :]
                turned = pltpu.roll(rings[i // HALF], COLS - (2 * m + 1), axis=1)
                after = jnp.where(lane == COLS - 1, turned, pltpu.roll(here, COLS - 1, axis=1))
                before = jnp.where(lane == 0, turned, pltpu.roll(here, 1, axis=1))
                tile = jnp.where(valid, mixed(rate, here, below, above, after, before), 0.0)
                moved_ref[c, i, rows, :] = tile
                kept.append(tile)
            for f in (0, 2):
                both = jnp.concatenate(kept[f : f + 2], axis=0).astype(jnp.bfloat16)
                x_ref[pl.ds(pl.multiple_of(32 * c + 8 * f, 16), 16), COLS * i : COLS * (i + 1)] = (
                    both
                )
        pltpu.make_async_copy(moved_ref.at[c], moved_hbm.at[c], out_sem.at[c]).start()
        return carry

    lax.fori_loop(0, CHUNKS, one_chunk, 0)
    hot_copy.wait()
    hot = hot_ref[...]
    sums = lax.dot_general(x_ref[...], hot, NT, preferred_element_type=jnp.float32)
    mean = sums * (1.0 / share)
    near_mean = mean.astype(jnp.bfloat16)
    for i in range(0, ROWS, 4):
        part = slice(COLS * i, COLS * (i + 4))
        centre = lax.dot_general(
            near_mean, hot_ref[:, part], NN, preferred_element_type=jnp.float32
        )
        away = x_ref[:, part].astype(jnp.float32) - centre
        square = away * away
        high = square.astype(jnp.bfloat16)
        hi_ref[:, part] = high
        lo_ref[:, part] = (square - high.astype(jnp.float32)).astype(jnp.bfloat16)
    spread = lax.dot_general(
        hi_ref[...], hot, NT, preferred_element_type=jnp.float32
    ) + lax.dot_general(lo_ref[...], hot, NT, preferred_element_type=jnp.float32)
    offset = mean - near_mean.astype(jnp.float32)
    spread = spread - share * (offset * offset)
    store_parts(stats_ref, (mean[:COLS].T, mean[COLS:].T, spread[:COLS].T, spread[COLS:].T))
    stats_copy = pltpu.make_async_copy(stats_ref, stats_hbm, hot_sem)
    stats_copy.start()
    for c in range(CHUNKS):
        pltpu.make_async_copy(moved_ref.at[c], moved_hbm.at[c], out_sem.at[c]).wait()
    stats_copy.wait()


def store_parts(ref, parts):
    for k, part in enumerate(parts):
        ref[pl.ds(k, part.shape[0], stride=4), :] = part


def load_parts(ref):
    return [ref[pl.ds(k, ref.shape[0] // 4, stride=4), :] for k in range(4)]


def batch_kernel(order_ref, owner_ref, batch_ref, hot_ref):
    order = order_ref[...]
    shape = (32, order.shape[1])
    high = lax.broadcasted_iota(jnp.int32, shape, 0) == order // COLS
    left = jnp.where(high, owner_ref[...], 0.0).astype(jnp.bfloat16)
    shape = (COLS, order.shape[1])
    low = lax.broadcasted_iota(jnp.int32, shape, 0) == order % COLS
    right = jnp.where(low, 1.0, 0.0).astype(jnp.bfloat16)
    found = lax.dot_general(left, right, NT, preferred_element_type=jnp.float32)
    batch = found[:ROWS].astype(jnp.int32)
    batch_ref[...] = batch
    groups = lax.broadcasted_iota(jnp.int32, (COLS, COLS), 0)
    for i in range(ROWS):
        hot_ref[:, COLS * i : COLS * (i + 1)] = jnp.where(
            groups == batch[i : i + 1, :], 1.0, 0.0
        ).astype(jnp.bfloat16)


def merge_kernel(share, stats_ref, gain_ref, out_ref):
    count = stats_ref.shape[0] // 4
    parts = load_parts(stats_ref)
    merged = []
    for k in range(2):
        mean = jnp.sum(parts[k], axis=0, keepdims=True) * (1.0 / count)
        away = parts[k] - mean
        total = jnp.sum(parts[k + 2] + share * (away * away), axis=0, keepdims=True)
        gain = gain_ref[:, COLS * k : COLS * (k + 1)]
        merged.append((mean, lax.rsqrt(total * (1.0 / (count * share)) + 1e-05) * gain))
    values = (merged[0][0], merged[1][0], merged[0][1], merged[1][1])
    store_parts(out_ref, [jnp.broadcast_to(v, (count, COLS)) for v in values])


def network_kernel(
    moved_hbm,
    batch_hbm,
    stats_hbm,
    shift_hbm,
    first_hbm,
    inner_hbm,
    last_hbm,
    bias_hbm,
    final_hbm,
    out_hbm,
    moved_ref,
    batch_ref,
    stats_ref,
    shift_ref,
    first_ref,
    inner_ref,
    last_ref,
    bias_ref,
    final_ref,
    out_ref,
    mean_ref,
    scale_ref,
    even_ref,
    odd_ref,
    moved_sem,
    weight_sem,
    out_sem,
):
    blocks = ROWS // BLOCK
    moved_copies = [
        pltpu.make_async_copy(
            moved_hbm.at[:, pl.ds(BLOCK * b, BLOCK)],
            moved_ref.at[:, pl.ds(BLOCK * b, BLOCK)],
            moved_sem.at[b],
        )
        for b in range(blocks)
    ]
    early_copies = copies_of(
        (stats_hbm, batch_hbm, shift_hbm), (stats_ref, batch_ref, shift_ref), weight_sem
    )
    weight_copies = copies_of(
        (first_hbm, bias_hbm, inner_hbm, last_hbm, final_hbm),
        (first_ref, bias_ref, inner_ref, last_ref, final_ref),
        weight_sem,
        3,
    )
    for copy in early_copies + moved_copies[:2] + weight_copies + moved_copies[2:]:
        copy.start()
    for copy in early_copies:
        copy.wait()
    parts = load_parts(stats_ref)
    for k in range(2):
        mean_ref[COLS * k : COLS * (k + 1), :] = parts[k].T
        scale_ref[COLS * k : COLS * (k + 1), :] = parts[k + 2].T
    out_rows = out_ref.reshape(FIELDS * LEVELS * ROWS, COLS)

    def dot(a, b):
        return lax.dot_general(a, b, NN, preferred_element_type=jnp.float32)

    def act(product, layer):
        t = product + bias_ref[layer : layer + 1, :]
        return (t + t * jnp.tanh(t)).astype(jnp.bfloat16)

    def normalize(block, normed_ref):
        mean, scale = mean_ref[...], scale_ref[...]
        for k in range(BLOCK):
            i = BLOCK * block + k
            index = jnp.broadcast_to(batch_ref[pl.ds(i, 1), :], (FEATS, COLS))
            x = moved_ref[:, i].reshape(FEATS, COLS).astype(jnp.bfloat16).astype(jnp.float32)
            away = x - jnp.take_along_axis(mean, index, axis=1)
            tile = away * jnp.take_along_axis(scale, index, axis=1)
            normed_ref[COLS * k : COLS * (k + 1), :] = (tile.T + shift_ref[...]).astype(
                jnp.bfloat16
            )

    def layers(block, normed_ref):
        hidden = act(dot(normed_ref[...], first_ref[...]), 0)
        for layer in range(3):
            hidden = act(dot(hidden, inner_ref[layer]), layer + 1)
        tendency = dot(hidden, last_ref[...]) + final_ref[...]
        tendency = tendency.astype(jnp.bfloat16).astype(jnp.float32)
        for k in range(BLOCK):
            i = BLOCK * block + k
            change = tendency[COLS * k : COLS * (k + 1), :].T
            for chunk in range(CHUNKS):
                rows = min(8, LEVELS - 8 * chunk)
                for f in range(FIELDS):
                    row = 32 * chunk + 8 * f
                    new = moved_ref[chunk, i, 8 * f : 8 * f + rows, :] + change[row : row + rows]
                    start = (LEVELS * f + 8 * chunk) * ROWS + i
                    out_rows[pl.ds(start, rows, stride=ROWS), :] = new

    def out_copy(group):
        part = pl.ds(pl.multiple_of(8 * group, 8), 8)
        return pltpu.make_async_copy(
            out_ref.at[:, part, :], out_hbm.at[:, part, :], out_sem.at[group]
        )

    moved_copies[0].wait()
    normalize(0, even_ref)
    for copy in weight_copies:
        copy.wait()

    def two_blocks(group, carry):
        block = 2 * group
        for b in range(1, blocks):

            @pl.when(block == (b - 1) // 2 * 2)
            def _(b=b):
                moved_copies[b].wait()

        normalize(block + 1, odd_ref)
        layers(block, even_ref)
        normalize(jnp.minimum(block + 2, blocks - 1), even_ref)
        layers(block + 1, odd_ref)
        out_copy(group).start()
        return carry

    lax.fori_loop(0, blocks // 2, two_blocks, 0)
    for group in range(blocks // 2):
        out_copy(group).wait()


BLOCK = 4
EDGE_ROWS = 8 * (2 * FIELDS + 1)
EDGES = CHUNKS * EDGE_ROWS
VMEM_SPEC = pl.BlockSpec(memory_space=pltpu.VMEM)
HBM_SPEC = pl.BlockSpec(memory_space=pltpu.HBM)
GRID_SHAPE = (CHUNKS, ROWS, 32, COLS)
LEVEL_SHAPE = (CHUNKS, 4, 8 * ROWS, COLS)


def f32(*shape):
    return jax.ShapeDtypeStruct(shape, jnp.float32)


def bf16(*shape):
    return jax.ShapeDtypeStruct(shape, jnp.bfloat16)


def cost(flops, size):
    return pl.CostEstimate(flops=flops, bytes_accessed=size, transcendentals=0)


def swap(values, axis, first):
    count = lax.axis_size(axis)
    step = 0 if first else 1
    pairs = [((i + step) % count, (i + 1 + step) % count) for i in range(0, count, 2)]
    return lax.ppermute(values, axis, pairs + [(b, a) for a, b in pairs])


def by_row(values):
    rest = values.shape[1:]
    values = values.reshape(FIELDS, LEVELS, *rest)
    values = jnp.pad(values, ((0, 0), (0, 64 - LEVELS)) + ((0, 0),) * len(rest))
    values = values.reshape(FIELDS, CHUNKS, 8, *rest).swapaxes(0, 1)
    return values.reshape(FEATS, *rest)


def body(
    tracers,
    rates,
    column_order,
    norm_gain,
    norm_shift,
    weight_first,
    weight_hidden,
    weight_last,
    bias_hidden,
    bias_last,
):
    count = lax.axis_size("bx") * lax.axis_size("by")
    columns = ROWS * COLS
    share = columns // count
    width = weight_first.shape[0]
    x = tracers.reshape(FIELDS, LEVELS * ROWS, COLS)
    r = rates.reshape(4, LEVELS * ROWS, COLS)

    dma = pltpu.SemaphoreType.DMA
    part, near, far, cols = pl.pallas_call(
        first_kernel,
        in_specs=[HBM_SPEC, HBM_SPEC],
        out_specs=[HBM_SPEC] * 4,
        out_shape=[
            f32(*GRID_SHAPE),
            bf16(EDGES + 64, COLS),
            bf16(EDGES + 64, COLS),
            bf16(3 * 64, 2 * COLS),
        ],
        scratch_shapes=[
            pltpu.VMEM(LEVEL_SHAPE, jnp.float32),
            pltpu.VMEM(LEVEL_SHAPE, jnp.float32),
            pltpu.VMEM(GRID_SHAPE, jnp.float32),
            pltpu.VMEM((EDGES, COLS), jnp.float32),
            pltpu.VMEM((EDGES, COLS), jnp.float32),
            pltpu.VMEM((3 * 64, 2 * COLS), jnp.float32),
            pltpu.VMEM((EDGES, COLS), jnp.bfloat16),
            pltpu.VMEM((EDGES, COLS), jnp.bfloat16),
            pltpu.VMEM((3 * 64, 2 * COLS), jnp.bfloat16),
            dma((CHUNKS,)),
            dma((CHUNKS,)),
            dma((CHUNKS,)),
            dma((3,)),
        ],
        compiler_params=params(62),
        cost_estimate=cost(10**7, 9 * 10**6),
        name="first_substep",
    )(x, r)
    core = swap(cols, "by", True)
    chip = swap(cols, "by", False)
    near, far = pl.pallas_call(
        corner_kernel,
        in_specs=[HBM_SPEC, VMEM_SPEC, VMEM_SPEC, HBM_SPEC, HBM_SPEC],
        out_specs=[HBM_SPEC] * 2,
        out_shape=[bf16(EDGES + 64, COLS), bf16(EDGES + 64, COLS)],
        scratch_shapes=[
            pltpu.VMEM((64, 2 * COLS), jnp.bfloat16),
            pltpu.VMEM((64, COLS), jnp.bfloat16),
            pltpu.VMEM((64, COLS), jnp.bfloat16),
            dma((3,)),
        ],
        input_output_aliases={3: 0, 4: 1},
        compiler_params=params(16),
        cost_estimate=cost(10**5, 10**6),
        name="corners",
    )(cols, core, chip, near, far)
    near_in = swap(near, "bx", True)
    far_in = swap(far, "bx", False)

    owner = (jnp.arange(columns, dtype=jnp.int32) // share).astype(jnp.float32)[None, :]
    batch, hot = pl.pallas_call(
        batch_kernel,
        in_specs=[VMEM_SPEC, VMEM_SPEC],
        out_specs=[VMEM_SPEC, VMEM_SPEC],
        out_shape=[
            jax.ShapeDtypeStruct((ROWS, COLS), jnp.int32),
            jax.ShapeDtypeStruct((COLS, columns), jnp.bfloat16),
        ],
        compiler_params=params(62),
        cost_estimate=cost(10**9, 2 * 10**6),
        name="batch_ids",
    )(column_order, owner)

    moved, stats = pl.pallas_call(
        functools.partial(second_kernel, share),
        in_specs=[HBM_SPEC] * 10,
        out_specs=[HBM_SPEC] * 2,
        out_shape=[f32(*GRID_SHAPE), f32(4 * count, COLS)],
        scratch_shapes=[
            pltpu.VMEM(GRID_SHAPE, jnp.float32),
            pltpu.VMEM(LEVEL_SHAPE, jnp.float32),
            pltpu.VMEM((COLS, columns), jnp.bfloat16),
            pltpu.VMEM(GRID_SHAPE, jnp.float32),
            pltpu.VMEM((FEATS, columns), jnp.bfloat16),
            pltpu.VMEM((FEATS, columns), jnp.bfloat16),
            pltpu.VMEM((FEATS, columns), jnp.bfloat16),
            *[pltpu.VMEM((EDGES + 64, COLS), jnp.float32) for _ in range(4)],
            *[pltpu.VMEM((3 * 64, 2 * COLS), jnp.float32) for _ in range(3)],
            *[pltpu.VMEM((EDGES + 64, COLS), jnp.bfloat16) for _ in range(4)],
            *[pltpu.VMEM((3 * 64, 2 * COLS), jnp.bfloat16) for _ in range(3)],
            pltpu.VMEM((4 * count, COLS), jnp.float32),
            dma((CHUNKS,)),
            dma((CHUNKS,)),
            dma((CHUNKS,)),
            dma,
            dma((7,)),
        ],
        compiler_params=params(62),
        cost_estimate=cost(10**9, 9 * 10**6),
        name="second_substep",
    )(
        part,
        r,
        near,
        far,
        near_in,
        far_in,
        cols,
        core,
        chip,
        hot,
    )

    stats, *raw = lax.optimization_barrier(
        (
            stats,
            norm_gain,
            norm_shift,
            weight_first,
            weight_hidden,
            weight_last,
            bias_hidden,
            bias_last,
        )
    )
    norm_gain, norm_shift, weight_first, weight_hidden, weight_last, bias_hidden, bias_last = raw
    gathered = lax.all_to_all(stats, ("bx", "by"), split_axis=0, concat_axis=0, tiled=True)
    merged = pl.pallas_call(
        functools.partial(merge_kernel, float(share)),
        in_specs=[VMEM_SPEC, VMEM_SPEC],
        out_specs=VMEM_SPEC,
        out_shape=jax.ShapeDtypeStruct((4 * count, COLS), jnp.float32),
        compiler_params=params(16),
        cost_estimate=cost(10**6, 10**6),
        name="merge_statistics",
    )(gathered, by_row(norm_gain)[None, :])
    known = lax.all_to_all(merged, ("bx", "by"), split_axis=0, concat_axis=0, tiled=True)

    half = jnp.bfloat16(0.5)
    new = pl.pallas_call(
        network_kernel,
        in_specs=[HBM_SPEC] * 9,
        out_specs=HBM_SPEC,
        out_shape=f32(FIELDS * LEVELS, ROWS, COLS),
        scratch_shapes=[
            pltpu.VMEM(GRID_SHAPE, jnp.float32),
            pltpu.VMEM((ROWS, COLS), jnp.int32),
            pltpu.VMEM((4 * count, COLS), jnp.float32),
            pltpu.VMEM((1, FEATS), jnp.float32),
            pltpu.VMEM((FEATS, width), jnp.bfloat16),
            pltpu.VMEM((3, width, width), jnp.bfloat16),
            pltpu.VMEM((width, FEATS), jnp.bfloat16),
            pltpu.VMEM((4, width), jnp.float32),
            pltpu.VMEM((1, FEATS), jnp.float32),
            pltpu.VMEM((FIELDS * LEVELS, ROWS, COLS), jnp.float32),
            pltpu.VMEM((FEATS, COLS), jnp.float32),
            pltpu.VMEM((FEATS, COLS), jnp.float32),
            pltpu.VMEM((BLOCK * COLS, FEATS), jnp.bfloat16),
            pltpu.VMEM((BLOCK * COLS, FEATS), jnp.bfloat16),
            dma((ROWS // BLOCK,)),
            dma((8,)),
            dma((3,)),
        ],
        compiler_params=params(62),
        cost_estimate=cost(6 * 10**9, 9 * 10**6),
        name="network",
    )(
        moved,
        batch,
        known,
        by_row(norm_shift)[None, :],
        by_row(weight_first.T) * half,
        weight_hidden.swapaxes(1, 2) * half,
        by_row(weight_last).T,
        bias_hidden * 0.5,
        by_row(bias_last)[None, :],
    )
    return new.reshape(tracers.shape)


def solution(mesh):
    placed = (
        P(None, None, "bx", "by"),
        P(None, None, "bx", "by"),
        P(("bx", "by"), None),
        P(),
        P(),
        P(),
        P(),
        P(),
        P(),
        P(),
    )
    return jax.shard_map(
        body, mesh=mesh, in_specs=placed, out_specs=P(None, None, "bx", "by"), check_vma=False
    )
```

```python
import functools

import jax
import jax.numpy as jnp
from jax import lax
from jax.experimental import pallas as pl
from jax.experimental.pallas import tpu as pltpu
from jax.sharding import PartitionSpec as P

FIELDS = 4
LEVELS = 60
CHUNKS = 8
ROWS = 24
COLS = 128
FEATS = 256
HALF = ROWS // 2
MIB = 1 << 20
NT = (((1,), (1,)), ((), ()))
NN = (((1,), (0,)), ((), ()))


def params(limit):
    return pltpu.CompilerParams(vmem_limit_bytes=limit * MIB)


def lanes_of(shape):
    return lax.broadcasted_iota(jnp.int32, shape, 1)


def valid_rows(chunk):
    level = chunk * 8 + lax.broadcasted_iota(jnp.int32, (8, COLS), 0)
    return level < LEVELS


def level_copies(hbm_ref, vmem_ref, sem):
    copies = []
    for c in range(CHUNKS):
        rows = ROWS * min(8, LEVELS - 8 * c)
        copies.append(
            pltpu.make_async_copy(
                hbm_ref.at[:, pl.ds(8 * ROWS * c, rows), :],
                vmem_ref.at[c, :, pl.ds(0, rows), :],
                sem.at[c],
            )
        )
    return copies


def copies_of(given, kept, sem, first=0):
    return [
        pltpu.make_async_copy(a, b, sem.at[first + k])
        for k, (a, b) in enumerate(zip(given, kept, strict=True))
    ]


def wait_for(chunk, *groups):
    for c in range(CHUNKS):

        @pl.when(chunk == c)
        def _(c=c):
            for copies in groups:
                copies[c].wait()


class ColumnPacker:
    def __init__(self):
        self.pair = lanes_of((8, COLS)) // 2
        self.halves = [jnp.zeros((8, COLS), jnp.float32) for _ in range(2)]

    def add(self, i, f, tile):
        m = 4 * (i % HALF) + f
        moved = pltpu.roll(tile, 2 * m + 1, axis=1)
        self.halves[i // HALF] = jnp.where(self.pair == m, moved, self.halves[i // HALF])

    def store(self, ref, row, valid):
        for h in range(2):
            ref[pl.ds(row, 8), COLS * h : COLS * (h + 1)] = jnp.where(valid, self.halves[h], 0.0)


def pair_of(last, first):
    return jnp.where(
        lanes_of((8, COLS)) % 2 == 0,
        jnp.broadcast_to(last[:, COLS - 1 :], (8, COLS)),
        jnp.broadcast_to(first[:, :1], (8, COLS)),
    )


def is_even(axis):
    return jnp.full((8, COLS), lax.axis_index(axis) % 2, jnp.int32) == 0


def mixed(rate, here, below, above, after, before):
    return (
        here
        + rate[0] * (below - here)
        + rate[1] * (above - here)
        + rate[2] * (after - here)
        + rate[3] * (before - here)
    )


def first_kernel(
    x_hbm,
    r_hbm,
    part_hbm,
    near_hbm,
    far_hbm,
    cols_hbm,
    x_ref,
    r_ref,
    part_ref,
    near_ref,
    far_ref,
    cols_ref,
    near_out_ref,
    far_out_ref,
    cols_out_ref,
    x_sem,
    r_sem,
    out_sem,
    edge_sem,
):
    x_copies = level_copies(x_hbm, x_ref, x_sem)
    r_copies = level_copies(r_hbm, r_ref, r_sem)
    for c in range(CHUNKS):
        x_copies[c].start()
        r_copies[c].start()
    lane = lanes_of((8, COLS))
    zero = jnp.zeros((8, COLS), jnp.float32)
    even = is_even("bx")
    odd = jnp.logical_not(even)

    def one_chunk(c, carry):
        valid = valid_rows(c)
        wait_for(c, x_copies, r_copies)

        def cell(i, f):
            return x_ref[c, f, pl.ds(i, 8, stride=ROWS), :]

        def rate_of(i, k):
            return r_ref[c, k, pl.ds(i, 8, stride=ROWS), :]

        for i in range(ROWS):
            rate = [rate_of(i, k) for k in range(4)]
            for f in range(FIELDS):
                here = cell(i, f)
                new = mixed(
                    rate,
                    here,
                    cell(i + 1, f) if i < ROWS - 1 else zero,
                    cell(i - 1, f) if i > 0 else zero,
                    jnp.where(lane == COLS - 1, 0.0, pltpu.roll(here, COLS - 1, axis=1)),
                    jnp.where(lane == 0, 0.0, pltpu.roll(here, 1, axis=1)),
                )
                part_ref[c, i, 8 * f : 8 * f + 8, :] = jnp.where(valid, new, 0.0)
        pltpu.make_async_copy(part_ref.at[c], part_hbm.at[c], out_sem.at[c]).start()

        start = pl.multiple_of(EDGE_ROWS * c, 8)
        for f in range(2 * FIELDS + 1):
            if f < FIELDS:
                last, first = cell(ROWS - 1, f), cell(0, f)
            elif f < 2 * FIELDS:
                rows = slice(8 * (f - FIELDS), 8 * (f - FIELDS) + 8)
                last, first = part_ref[c, ROWS - 1, rows, :], part_ref[c, 0, rows, :]
            else:
                last, first = rate_of(ROWS - 1, 0), rate_of(0, 1)
            near_ref[pl.ds(start + 8 * f, 8), :] = jnp.where(valid & even, last, 0.0) + jnp.where(
                valid & odd, first, 0.0
            )
            far_ref[pl.ds(start + 8 * f, 8), :] = jnp.where(valid & even, first, 0.0) + jnp.where(
                valid & odd, last, 0.0
            )

        row = pl.multiple_of(8 * c, 8)
        last = pair_of(rate_of(ROWS - 1, 2), rate_of(ROWS - 1, 3))
        first = pair_of(rate_of(0, 2), rate_of(0, 3))
        spot = valid & (lane // 8 == 1)
        near_ref[pl.ds(EDGES + row, 8), :] = jnp.where(spot, jnp.where(even, last, first), 0.0)
        far_ref[pl.ds(EDGES + row, 8), :] = jnp.where(spot, jnp.where(even, first, last), 0.0)
        packer = ColumnPacker()
        for i in range(ROWS):
            for f in range(FIELDS):
                packer.add(i, f, cell(i, f))
        packer.store(cols_ref, row, valid)
        packer = ColumnPacker()
        for i in range(ROWS):
            for f in range(FIELDS):
                packer.add(i, f, part_ref[c, i, 8 * f : 8 * f + 8, :])
        packer.store(cols_ref, 64 + row, valid)
        for h in range(2):
            acc = zero
            for i in range(HALF):
                pair = pair_of(rate_of(HALF * h + i, 2), rate_of(HALF * h + i, 3))
                acc = jnp.where(lane // 8 == i, pair, acc)
            outer = rate_of(0, 1) if h == 0 else rate_of(ROWS - 1, 0)
            acc = jnp.where(lane // 8 == HALF, pair_of(outer, outer), acc)
            cols_ref[pl.ds(128 + row, 8), COLS * h : COLS * (h + 1)] = jnp.where(valid, acc, 0.0)
        return carry

    lax.fori_loop(0, CHUNKS, one_chunk, 0)
    for out, kept in ((near_out_ref, near_ref), (far_out_ref, far_ref)):
        out[...] = kept[...].astype(jnp.bfloat16)
    cols_out_ref[...] = cols_ref[...].astype(jnp.bfloat16)
    copies = copies_of(
        (cols_out_ref, near_out_ref, far_out_ref),
        (cols_hbm, near_hbm, far_hbm),
        edge_sem,
    )
    for copy in copies:
        copy.start()
    for c in range(CHUNKS):
        pltpu.make_async_copy(part_ref.at[c], part_hbm.at[c], out_sem.at[c]).wait()
    for copy in copies:
        copy.wait()


def merged_columns(even_y, core, chip):
    right = jnp.where(even_y, core, chip)
    left = jnp.where(even_y, chip, core)
    return jnp.where(
        lanes_of((8, COLS)) % 2 == 0,
        pltpu.roll(right, COLS - 1, axis=1),
        pltpu.roll(left, 1, axis=1),
    )


def corner_kernel(
    core_ref, chip_ref, near_in, far_in, near_hbm, far_hbm, near_ref, far_ref, sem
):
    corners_in = [given.at[pl.ds(EDGES, 64), :] for given in (near_in, far_in)]
    copies = copies_of(corners_in, (near_ref, far_ref), sem)
    for copy in copies:
        copy.start()
    even = is_even("bx")
    even_y = is_even("by")
    lane = lanes_of((8, COLS))
    core = core_ref[:64, :].astype(jnp.float32)
    chip = chip_ref[:64, :].astype(jnp.float32)
    for copy in copies:
        copy.wait()
    near_rates = near_ref[...].astype(jnp.float32)
    far_rates = far_ref[...].astype(jnp.float32)
    nears, fars = [], []
    for c in range(CHUNKS):
        rows = slice(8 * c, 8 * c + 8)
        cells, again = [], []
        for h in range(2):
            part = slice(COLS * h, COLS * (h + 1))
            beside = merged_columns(even_y, core[rows, part], chip[rows, part])
            back = 8 * (HALF - 1) * h
            cells.append(pltpu.roll(beside, (COLS - back) % COLS, axis=1))
            again.append(pltpu.roll(beside, (COLS + 8 - back) % COLS, axis=1))
        near = jnp.where(even, again[1], again[0]) * near_rates[rows]
        far = jnp.where(even, again[0], again[1]) * far_rates[rows]
        nears.append(jnp.where(lane < 8, jnp.where(even, cells[1], cells[0]), near))
        fars.append(jnp.where(lane < 8, jnp.where(even, cells[0], cells[1]), far))
    near_ref[...] = jnp.concatenate(nears, axis=0).astype(jnp.bfloat16)
    far_ref[...] = jnp.concatenate(fars, axis=0).astype(jnp.bfloat16)
    corners_out = [out.at[pl.ds(EDGES, 64), :] for out in (near_hbm, far_hbm)]
    copies = copies_of((near_ref, far_ref), corners_out, sem)
    for copy in copies:
        copy.start()
    for copy in copies:
        copy.wait()


def second_kernel(
    share,
    part_hbm,
    r_hbm,
    own_near_in,
    own_far_in,
    near_in,
    far_in,
    cols_in,
    core_in,
    chip_in,
    hot_hbm,
    hot_t_hbm,
    moved_hbm,
    stats_hbm,
    part_ref,
    r_ref,
    hot_ref,
    hot_t_ref,
    moved_ref,
    x_ref,
    hi_ref,
    lo_ref,
    own_near_ref,
    own_far_ref,
    near_ref,
    far_ref,
    cols_ref,
    core_ref,
    chip_ref,
    own_near_16,
    own_far_16,
    near_16,
    far_16,
    cols_16,
    core_16,
    chip_16,
    stats_ref,
    part_sem,
    r_sem,
    out_sem,
    hot_sem,
    edge_sem,
):
    edges_in = (own_near_in, own_far_in, near_in, far_in, cols_in, core_in, chip_in)
    edges_16 = (own_near_16, own_far_16, near_16, far_16, cols_16, core_16, chip_16)
    edges = (own_near_ref, own_far_ref, near_ref, far_ref, cols_ref, core_ref, chip_ref)
    edge_copies = copies_of(edges_in, edges_16, edge_sem)
    for copy in edge_copies:
        copy.start()
    part_copies = [
        pltpu.make_async_copy(part_hbm.at[c], part_ref.at[c], part_sem.at[c])
        for c in range(CHUNKS)
    ]
    r_copies = level_copies(r_hbm, r_ref, r_sem)
    for c in range(CHUNKS):
        part_copies[c].start()
        r_copies[c].start()
    hot_copies = copies_of((hot_hbm, hot_t_hbm), (hot_ref, hot_t_ref), hot_sem)
    for copy in hot_copies:
        copy.start()
    for copy, kept, given in zip(edge_copies, edges, edges_16, strict=True):
        copy.wait()
        kept[...] = given[...].astype(jnp.float32)
    lane = lanes_of((8, COLS))
    rim = (lane == 0) | (lane == COLS - 1)
    even = is_even("bx")
    even_y = is_even("by")

    def one_chunk(c, carry):
        valid = valid_rows(c)
        row = pl.multiple_of(8 * c, 8)
        start = pl.multiple_of(EDGE_ROWS * c, 8)
        wait_for(c, part_copies, r_copies)

        def edge(near, far, f, below):
            a, b = near[pl.ds(start + 8 * f, 8), :], far[pl.ds(start + 8 * f, 8), :]
            return jnp.where(even, a, b) if below else jnp.where(even, b, a)

        def rate_of(i, k):
            return r_ref[c, k, pl.ds(i, 8, stride=ROWS), :]

        corner = [near_ref[pl.ds(EDGES + row, 8), :], far_ref[pl.ds(EDGES + row, 8), :]]
        corner = [jnp.where(even, corner[1], corner[0]), jnp.where(even, corner[0], corner[1])]
        rings, gains = [], []
        for h in range(2):
            lanes = slice(COLS * h, COLS * (h + 1))
            cells, parts, rates = (
                merged_columns(
                    even_y,
                    core_ref[pl.ds(64 * k + row, 8), lanes],
                    chip_ref[pl.ds(64 * k + row, 8), lanes],
                )
                for k in range(3)
            )
            diagonal = corner[h]
            if h == 1:
                diagonal = pltpu.roll(diagonal, 8 * (HALF - 1), axis=1)
            shift = COLS - 8 * HALF if h == 0 else COLS - 8
            spot = lane // 8 == (0 if h == 0 else HALF - 1)
            extra = jnp.where(spot, pltpu.roll(rates, shift, axis=1) * diagonal, 0.0)
            rings.append(parts + rates * cols_ref[pl.ds(row, 8), lanes] + extra)
            gains.append(cols_ref[pl.ds(128 + row, 8), lanes] * cells)

        outer = []
        for side, i in enumerate((0, ROWS - 1)):
            down = side == 1
            rate = edge(near_ref, far_ref, 2 * FIELDS, down)
            tiles = []
            for f in range(FIELDS):
                turned = pltpu.roll(corner[side], COLS - (9 + 2 * f), axis=1)
                tiles.append(
                    edge(near_ref, far_ref, FIELDS + f, down)
                    + rate * edge(own_near_ref, own_far_ref, f, down)
                    + jnp.where(rim, turned, 0.0)
                )
            outer.append(tiles)

        for i in range(ROWS):
            for f in range(FIELDS):
                m = 4 * (i % HALF) + f
                turned = pltpu.roll(gains[i // HALF], COLS - (2 * m + 1), axis=1)
                tile = part_ref[c, i, 8 * f : 8 * f + 8, :] + jnp.where(rim, turned, 0.0)
                if i == 0:
                    tile = tile + rate_of(0, 1) * edge(near_ref, far_ref, f, False)
                if i == ROWS - 1:
                    tile = tile + rate_of(ROWS - 1, 0) * edge(near_ref, far_ref, f, True)
                part_ref[c, i, 8 * f : 8 * f + 8, :] = tile

        for i in range(ROWS):
            rate = [rate_of(i, k) for k in range(4)]
            kept = []
            for f in range(FIELDS):
                rows = slice(8 * f, 8 * f + 8)
                m = 4 * (i % HALF) + f
                here = part_ref[c, i, rows, :]
                above = outer[0][f] if i == 0 else part_ref[c, i - 1, rows, :]
                below = outer[1][f] if i == ROWS - 1 else part_ref[c, i + 1, rows, :]
                turned = pltpu.roll(rings[i // HALF], COLS - (2 * m + 1), axis=1)
                after = jnp.where(lane == COLS - 1, turned, pltpu.roll(here, COLS - 1, axis=1))
                before = jnp.where(lane == 0, turned, pltpu.roll(here, 1, axis=1))
                tile = jnp.where(valid, mixed(rate, here, below, above, after, before), 0.0)
                moved_ref[c, i, rows, :] = tile
                kept.append(tile)
            for f in (0, 2):
                both = jnp.concatenate(kept[f : f + 2], axis=0).astype(jnp.bfloat16)
                x_ref[pl.ds(pl.multiple_of(32 * c + 8 * f, 16), 16), COLS * i : COLS * (i + 1)] = (
                    both
                )
        pltpu.make_async_copy(moved_ref.at[c], moved_hbm.at[c], out_sem.at[c]).start()
        return carry

    lax.fori_loop(0, CHUNKS, one_chunk, 0)
    for copy in hot_copies:
        copy.wait()
    hot_t = hot_t_ref[...]
    sums = lax.dot_general(x_ref[...], hot_t, NN, preferred_element_type=jnp.float32)
    mean = sums * (1.0 / share)
    near_mean = mean.astype(jnp.bfloat16)
    for i in range(0, ROWS, 4):
        part = slice(COLS * i, COLS * (i + 4))
        centre = lax.dot_general(
            near_mean, hot_ref[:, part], NN, preferred_element_type=jnp.float32
        )
        away = x_ref[:, part].astype(jnp.float32) - centre
        square = away * away
        high = square.astype(jnp.bfloat16)
        hi_ref[:, part] = high
        lo_ref[:, part] = (square - high.astype(jnp.float32)).astype(jnp.bfloat16)
    spread = lax.dot_general(
        hi_ref[...], hot_t, NN, preferred_element_type=jnp.float32
    ) + lax.dot_general(lo_ref[...], hot_t, NN, preferred_element_type=jnp.float32)
    offset = mean - near_mean.astype(jnp.float32)
    spread = spread - share * (offset * offset)
    store_parts(stats_ref, (mean[:COLS].T, mean[COLS:].T, spread[:COLS].T, spread[COLS:].T))
    stats_copy = pltpu.make_async_copy(stats_ref, stats_hbm, hot_sem.at[0])
    stats_copy.start()
    for c in range(CHUNKS):
        pltpu.make_async_copy(moved_ref.at[c], moved_hbm.at[c], out_sem.at[c]).wait()
    stats_copy.wait()


def store_parts(ref, parts):
    for k, part in enumerate(parts):
        ref[pl.ds(k, part.shape[0], stride=4), :] = part


def load_parts(ref):
    return [ref[pl.ds(k, ref.shape[0] // 4, stride=4), :] for k in range(4)]


def batch_kernel(order_ref, owner_ref, batch_ref, hot_ref, hot_t_ref):
    order = order_ref[...]
    shape = (32, order.shape[1])
    high = lax.broadcasted_iota(jnp.int32, shape, 0) == order // COLS
    left = jnp.where(high, owner_ref[...], 0.0).astype(jnp.bfloat16)
    shape = (COLS, order.shape[1])
    low = lax.broadcasted_iota(jnp.int32, shape, 0) == order % COLS
    right = jnp.where(low, 1.0, 0.0).astype(jnp.bfloat16)
    found = lax.dot_general(left, right, NT, preferred_element_type=jnp.float32)
    batch = found[:ROWS].astype(jnp.int32)
    batch_ref[...] = batch
    groups = lax.broadcasted_iota(jnp.int32, (COLS, COLS), 0)
    for i in range(ROWS):
        tile = jnp.where(groups == batch[i : i + 1, :], 1.0, 0.0)
        hot_ref[:, COLS * i : COLS * (i + 1)] = tile.astype(jnp.bfloat16)
        hot_t_ref[COLS * i : COLS * (i + 1), :] = tile.T.astype(jnp.bfloat16)


def merge_kernel(share, stats_ref, gain_ref, out_ref):
    count = stats_ref.shape[0] // 4
    parts = load_parts(stats_ref)
    merged = []
    for k in range(2):
        mean = jnp.sum(parts[k], axis=0, keepdims=True) * (1.0 / count)
        away = parts[k] - mean
        total = jnp.sum(parts[k + 2] + share * (away * away), axis=0, keepdims=True)
        gain = gain_ref[:, COLS * k : COLS * (k + 1)]
        merged.append((mean, lax.rsqrt(total * (1.0 / (count * share)) + 1e-05) * gain))
    values = (merged[0][0], merged[1][0], merged[0][1], merged[1][1])
    store_parts(out_ref, [jnp.broadcast_to(v, (count, COLS)) for v in values])


def network_kernel(
    moved_hbm,
    batch_hbm,
    stats_hbm,
    shift_hbm,
    first_hbm,
    inner_hbm,
    last_hbm,
    bias_hbm,
    final_hbm,
    out_hbm,
    moved_ref,
    batch_ref,
    stats_ref,
    shift_ref,
    first_ref,
    inner_ref,
    last_ref,
    bias_ref,
    final_ref,
    out_ref,
    mean_ref,
    scale_ref,
    even_ref,
    odd_ref,
    moved_sem,
    weight_sem,
    out_sem,
):
    blocks = ROWS // BLOCK
    moved_copies = [
        pltpu.make_async_copy(
            moved_hbm.at[:, pl.ds(BLOCK * b, BLOCK)],
            moved_ref.at[:, pl.ds(BLOCK * b, BLOCK)],
            moved_sem.at[b],
        )
        for b in range(blocks)
    ]
    early_copies = copies_of(
        (stats_hbm, batch_hbm, shift_hbm), (stats_ref, batch_ref, shift_ref), weight_sem
    )
    weight_copies = copies_of(
        (first_hbm, bias_hbm, inner_hbm, last_hbm, final_hbm),
        (first_ref, bias_ref, inner_ref, last_ref, final_ref),
        weight_sem,
        3,
    )
    for copy in early_copies + moved_copies[:2] + weight_copies + moved_copies[2:]:
        copy.start()
    for copy in early_copies:
        copy.wait()
    parts = load_parts(stats_ref)
    for k in range(2):
        mean_ref[COLS * k : COLS * (k + 1), :] = parts[k].T
        scale_ref[COLS * k : COLS * (k + 1), :] = parts[k + 2].T
    out_rows = out_ref.reshape(FIELDS * LEVELS * ROWS, COLS)

    def dot(a, b):
        return lax.dot_general(a, b, NN, preferred_element_type=jnp.float32)

    def act(product, layer):
        t = product + bias_ref[layer : layer + 1, :]
        return (t + t * jnp.tanh(t)).astype(jnp.bfloat16)

    def normalize(block, normed_ref):
        mean, scale = mean_ref[...], scale_ref[...]
        for k in range(BLOCK):
            i = BLOCK * block + k
            index = jnp.broadcast_to(batch_ref[pl.ds(i, 1), :], (FEATS, COLS))
            x = moved_ref[:, i].reshape(FEATS, COLS).astype(jnp.bfloat16).astype(jnp.float32)
            away = x - jnp.take_along_axis(mean, index, axis=1)
            tile = away * jnp.take_along_axis(scale, index, axis=1)
            normed_ref[COLS * k : COLS * (k + 1), :] = (tile.T + shift_ref[...]).astype(
                jnp.bfloat16
            )

    def layers(block, normed_ref):
        hidden = act(dot(normed_ref[...], first_ref[...]), 0)
        for layer in range(3):
            hidden = act(dot(hidden, inner_ref[layer]), layer + 1)
        tendency = dot(hidden, last_ref[...]) + final_ref[...]
        tendency = tendency.astype(jnp.bfloat16).astype(jnp.float32)
        for k in range(BLOCK):
            i = BLOCK * block + k
            change = tendency[COLS * k : COLS * (k + 1), :].T
            for chunk in range(CHUNKS):
                rows = min(8, LEVELS - 8 * chunk)
                for f in range(FIELDS):
                    row = 32 * chunk + 8 * f
                    new = moved_ref[chunk, i, 8 * f : 8 * f + rows, :] + change[row : row + rows]
                    start = (LEVELS * f + 8 * chunk) * ROWS + i
                    out_rows[pl.ds(start, rows, stride=ROWS), :] = new

    def out_copy(group):
        part = pl.ds(pl.multiple_of(8 * group, 8), 8)
        return pltpu.make_async_copy(
            out_ref.at[:, part, :], out_hbm.at[:, part, :], out_sem.at[group]
        )

    moved_copies[0].wait()
    normalize(0, even_ref)
    for copy in weight_copies:
        copy.wait()

    def two_blocks(group, carry):
        block = 2 * group
        for b in range(1, blocks):

            @pl.when(block == (b - 1) // 2 * 2)
            def _(b=b):
                moved_copies[b].wait()

        normalize(block + 1, odd_ref)
        layers(block, even_ref)
        normalize(jnp.minimum(block + 2, blocks - 1), even_ref)
        layers(block + 1, odd_ref)
        out_copy(group).start()
        return carry

    lax.fori_loop(0, blocks // 2, two_blocks, 0)
    for group in range(blocks // 2):
        out_copy(group).wait()


BLOCK = 4
EDGE_ROWS = 8 * (2 * FIELDS + 1)
EDGES = CHUNKS * EDGE_ROWS
VMEM_SPEC = pl.BlockSpec(memory_space=pltpu.VMEM)
HBM_SPEC = pl.BlockSpec(memory_space=pltpu.HBM)
GRID_SHAPE = (CHUNKS, ROWS, 32, COLS)
LEVEL_SHAPE = (CHUNKS, 4, 8 * ROWS, COLS)


def f32(*shape):
    return jax.ShapeDtypeStruct(shape, jnp.float32)


def bf16(*shape):
    return jax.ShapeDtypeStruct(shape, jnp.bfloat16)


def cost(flops, size):
    return pl.CostEstimate(flops=flops, bytes_accessed=size, transcendentals=0)


def swap(values, axis, first):
    count = lax.axis_size(axis)
    step = 0 if first else 1
    pairs = [((i + step) % count, (i + 1 + step) % count) for i in range(0, count, 2)]
    return lax.ppermute(values, axis, pairs + [(b, a) for a, b in pairs])


def by_row(values):
    rest = values.shape[1:]
    values = values.reshape(FIELDS, LEVELS, *rest)
    values = jnp.pad(values, ((0, 0), (0, 64 - LEVELS)) + ((0, 0),) * len(rest))
    values = values.reshape(FIELDS, CHUNKS, 8, *rest).swapaxes(0, 1)
    return values.reshape(FEATS, *rest)


def body(
    tracers,
    rates,
    column_order,
    norm_gain,
    norm_shift,
    weight_first,
    weight_hidden,
    weight_last,
    bias_hidden,
    bias_last,
):
    count = lax.axis_size("bx") * lax.axis_size("by")
    columns = ROWS * COLS
    share = columns // count
    width = weight_first.shape[0]
    x = tracers.reshape(FIELDS, LEVELS * ROWS, COLS)
    r = rates.reshape(4, LEVELS * ROWS, COLS)

    dma = pltpu.SemaphoreType.DMA
    part, near, far, cols = pl.pallas_call(
        first_kernel,
        in_specs=[HBM_SPEC, HBM_SPEC],
        out_specs=[HBM_SPEC] * 4,
        out_shape=[
            f32(*GRID_SHAPE),
            bf16(EDGES + 64, COLS),
            bf16(EDGES + 64, COLS),
            bf16(3 * 64, 2 * COLS),
        ],
        scratch_shapes=[
            pltpu.VMEM(LEVEL_SHAPE, jnp.float32),
            pltpu.VMEM(LEVEL_SHAPE, jnp.float32),
            pltpu.VMEM(GRID_SHAPE, jnp.float32),
            pltpu.VMEM((EDGES + 64, COLS), jnp.float32),
            pltpu.VMEM((EDGES + 64, COLS), jnp.float32),
            pltpu.VMEM((3 * 64, 2 * COLS), jnp.float32),
            pltpu.VMEM((EDGES + 64, COLS), jnp.bfloat16),
            pltpu.VMEM((EDGES + 64, COLS), jnp.bfloat16),
            pltpu.VMEM((3 * 64, 2 * COLS), jnp.bfloat16),
            dma((CHUNKS,)),
            dma((CHUNKS,)),
            dma((CHUNKS,)),
            dma((3,)),
        ],
        compiler_params=params(62),
        cost_estimate=cost(10**7, 9 * 10**6),
        name="first_substep",
    )(x, r)
    core = swap(cols, "by", True)
    chip = swap(cols, "by", False)
    near, far = pl.pallas_call(
        corner_kernel,
        in_specs=[VMEM_SPEC, VMEM_SPEC, HBM_SPEC, HBM_SPEC],
        out_specs=[HBM_SPEC] * 2,
        out_shape=[bf16(EDGES + 64, COLS), bf16(EDGES + 64, COLS)],
        scratch_shapes=[
            pltpu.VMEM((64, COLS), jnp.bfloat16),
            pltpu.VMEM((64, COLS), jnp.bfloat16),
            dma((2,)),
        ],
        input_output_aliases={2: 0, 3: 1},
        compiler_params=params(16),
        cost_estimate=cost(10**5, 10**6),
        name="corners",
    )(core, chip, near, far)
    near_in = swap(near, "bx", True)
    far_in = swap(far, "bx", False)

    owner = (jnp.arange(columns, dtype=jnp.int32) // share).astype(jnp.float32)[None, :]
    batch, hot, hot_t = pl.pallas_call(
        batch_kernel,
        in_specs=[VMEM_SPEC, VMEM_SPEC],
        out_specs=[VMEM_SPEC, VMEM_SPEC, VMEM_SPEC],
        out_shape=[
            jax.ShapeDtypeStruct((ROWS, COLS), jnp.int32),
            jax.ShapeDtypeStruct((COLS, columns), jnp.bfloat16),
            jax.ShapeDtypeStruct((columns, COLS), jnp.bfloat16),
        ],
        compiler_params=params(62),
        cost_estimate=cost(10**9, 2 * 10**6),
        name="batch_ids",
    )(column_order, owner)

    moved, stats = pl.pallas_call(
        functools.partial(second_kernel, share),
        in_specs=[HBM_SPEC] * 11,
        out_specs=[HBM_SPEC] * 2,
        out_shape=[f32(*GRID_SHAPE), f32(4 * count, COLS)],
        scratch_shapes=[
            pltpu.VMEM(GRID_SHAPE, jnp.float32),
            pltpu.VMEM(LEVEL_SHAPE, jnp.float32),
            pltpu.VMEM((COLS, columns), jnp.bfloat16),
            pltpu.VMEM((columns, COLS), jnp.bfloat16),
            pltpu.VMEM(GRID_SHAPE, jnp.float32),
            pltpu.VMEM((FEATS, columns), jnp.bfloat16),
            pltpu.VMEM((FEATS, columns), jnp.bfloat16),
            pltpu.VMEM((FEATS, columns), jnp.bfloat16),
            *[pltpu.VMEM((EDGES + 64, COLS), jnp.float32) for _ in range(4)],
            *[pltpu.VMEM((3 * 64, 2 * COLS), jnp.float32) for _ in range(3)],
            *[pltpu.VMEM((EDGES + 64, COLS), jnp.bfloat16) for _ in range(4)],
            *[pltpu.VMEM((3 * 64, 2 * COLS), jnp.bfloat16) for _ in range(3)],
            pltpu.VMEM((4 * count, COLS), jnp.float32),
            dma((CHUNKS,)),
            dma((CHUNKS,)),
            dma((CHUNKS,)),
            dma((2,)),
            dma((7,)),
        ],
        compiler_params=params(62),
        cost_estimate=cost(10**9, 9 * 10**6),
        name="second_substep",
    )(
        part,
        r,
        near,
        far,
        near_in,
        far_in,
        cols,
        core,
        chip,
        hot,
        hot_t,
    )

    stats, *raw = lax.optimization_barrier(
        (
            stats,
            norm_gain,
            norm_shift,
            weight_first,
            weight_hidden,
            weight_last,
            bias_hidden,
            bias_last,
        )
    )
    norm_gain, norm_shift, weight_first, weight_hidden, weight_last, bias_hidden, bias_last = raw
    gathered = lax.all_to_all(stats, ("bx", "by"), split_axis=0, concat_axis=0, tiled=True)
    merged = pl.pallas_call(
        functools.partial(merge_kernel, float(share)),
        in_specs=[VMEM_SPEC, VMEM_SPEC],
        out_specs=VMEM_SPEC,
        out_shape=jax.ShapeDtypeStruct((4 * count, COLS), jnp.float32),
        compiler_params=params(16),
        cost_estimate=cost(10**6, 10**6),
        name="merge_statistics",
    )(gathered, by_row(norm_gain)[None, :])
    known = lax.all_to_all(merged, ("bx", "by"), split_axis=0, concat_axis=0, tiled=True)

    half = jnp.bfloat16(0.5)
    new = pl.pallas_call(
        network_kernel,
        in_specs=[HBM_SPEC] * 9,
        out_specs=HBM_SPEC,
        out_shape=f32(FIELDS * LEVELS, ROWS, COLS),
        scratch_shapes=[
            pltpu.VMEM(GRID_SHAPE, jnp.float32),
            pltpu.VMEM((ROWS, COLS), jnp.int32),
            pltpu.VMEM((4 * count, COLS), jnp.float32),
            pltpu.VMEM((1, FEATS), jnp.float32),
            pltpu.VMEM((FEATS, width), jnp.bfloat16),
            pltpu.VMEM((3, width, width), jnp.bfloat16),
            pltpu.VMEM((width, FEATS), jnp.bfloat16),
            pltpu.VMEM((4, width), jnp.float32),
            pltpu.VMEM((1, FEATS), jnp.float32),
            pltpu.VMEM((FIELDS * LEVELS, ROWS, COLS), jnp.float32),
            pltpu.VMEM((FEATS, COLS), jnp.float32),
            pltpu.VMEM((FEATS, COLS), jnp.float32),
            pltpu.VMEM((BLOCK * COLS, FEATS), jnp.bfloat16),
            pltpu.VMEM((BLOCK * COLS, FEATS), jnp.bfloat16),
            dma((ROWS // BLOCK,)),
            dma((8,)),
            dma((3,)),
        ],
        compiler_params=params(62),
        cost_estimate=cost(6 * 10**9, 9 * 10**6),
        name="network",
    )(
        moved,
        batch,
        known,
        by_row(norm_shift)[None, :],
        by_row(weight_first.T) * half,
        weight_hidden.swapaxes(1, 2) * half,
        by_row(weight_last).T,
        bias_hidden * 0.5,
        by_row(bias_last)[None, :],
    )
    return new.reshape(tracers.shape)


def solution(mesh):
    placed = (
        P(None, None, "bx", "by"),
        P(None, None, "bx", "by"),
        P(("bx", "by"), None),
        P(),
        P(),
        P(),
        P(),
        P(),
        P(),
        P(),
    )
    return jax.shard_map(
        body, mesh=mesh, in_specs=placed, out_specs=P(None, None, "bx", "by"), check_vma=False
    )
```

```python
import functools

import jax
import jax.numpy as jnp
from jax import lax
from jax.experimental import pallas as pl
from jax.experimental.pallas import tpu as pltpu
from jax.sharding import PartitionSpec as P

FIELDS = 4
LEVELS = 60
CHUNKS = 8
ROWS = 24
COLS = 128
FEATS = 256
HALF = ROWS // 2
MIB = 1 << 20
NT = (((1,), (1,)), ((), ()))
NN = (((1,), (0,)), ((), ()))


def params(limit):
    return pltpu.CompilerParams(vmem_limit_bytes=limit * MIB)


def lanes_of(shape):
    return lax.broadcasted_iota(jnp.int32, shape, 1)


def valid_rows(chunk):
    level = chunk * 8 + lax.broadcasted_iota(jnp.int32, (8, COLS), 0)
    return level < LEVELS


def level_copies(hbm_ref, vmem_ref, sem):
    copies = []
    for c in range(CHUNKS):
        rows = ROWS * min(8, LEVELS - 8 * c)
        copies.append(
            pltpu.make_async_copy(
                hbm_ref.at[:, pl.ds(8 * ROWS * c, rows), :],
                vmem_ref.at[c, :, pl.ds(0, rows), :],
                sem.at[c],
            )
        )
    return copies


def copies_of(given, kept, sem, first=0):
    return [
        pltpu.make_async_copy(a, b, sem.at[first + k])
        for k, (a, b) in enumerate(zip(given, kept, strict=True))
    ]


def wait_for(chunk, *groups):
    for c in range(CHUNKS):

        @pl.when(chunk == c)
        def _(c=c):
            for copies in groups:
                copies[c].wait()


class ColumnPacker:
    def __init__(self):
        self.pair = lanes_of((8, COLS)) // 2
        self.halves = [jnp.zeros((8, COLS), jnp.float32) for _ in range(2)]

    def add(self, i, f, tile):
        m = 4 * (i % HALF) + f
        moved = pltpu.roll(tile, 2 * m + 1, axis=1)
        self.halves[i // HALF] = jnp.where(self.pair == m, moved, self.halves[i // HALF])

    def store(self, ref, row, valid):
        for h in range(2):
            ref[pl.ds(row, 8), COLS * h : COLS * (h + 1)] = jnp.where(valid, self.halves[h], 0.0)


def pair_of(last, first):
    return jnp.where(
        lanes_of((8, COLS)) % 2 == 0,
        jnp.broadcast_to(last[:, COLS - 1 :], (8, COLS)),
        jnp.broadcast_to(first[:, :1], (8, COLS)),
    )


def is_even(axis):
    return jnp.full((8, COLS), lax.axis_index(axis) % 2, jnp.int32) == 0


def mixed(rate, here, below, above, after, before):
    return (
        here
        + rate[0] * (below - here)
        + rate[1] * (above - here)
        + rate[2] * (after - here)
        + rate[3] * (before - here)
    )


def first_kernel(
    x_hbm,
    r_hbm,
    part_hbm,
    near_hbm,
    far_hbm,
    cols_hbm,
    x_ref,
    r_ref,
    part_ref,
    near_ref,
    far_ref,
    cols_ref,
    near_out_ref,
    far_out_ref,
    cols_out_ref,
    x_sem,
    r_sem,
    out_sem,
    edge_sem,
):
    x_copies = level_copies(x_hbm, x_ref, x_sem)
    r_copies = level_copies(r_hbm, r_ref, r_sem)
    for c in range(CHUNKS):
        x_copies[c].start()
        r_copies[c].start()
    lane = lanes_of((8, COLS))
    zero = jnp.zeros((8, COLS), jnp.float32)
    even = is_even("bx")
    odd = jnp.logical_not(even)

    def one_chunk(c, carry):
        valid = valid_rows(c)
        wait_for(c, x_copies, r_copies)

        def cell(i, f):
            return x_ref[c, f, pl.ds(i, 8, stride=ROWS), :]

        def rate_of(i, k):
            return r_ref[c, k, pl.ds(i, 8, stride=ROWS), :]

        for i in range(ROWS):
            rate = [rate_of(i, k) for k in range(4)]
            for f in range(FIELDS):
                here = cell(i, f)
                new = mixed(
                    rate,
                    here,
                    cell(i + 1, f) if i < ROWS - 1 else zero,
                    cell(i - 1, f) if i > 0 else zero,
                    jnp.where(lane == COLS - 1, 0.0, pltpu.roll(here, COLS - 1, axis=1)),
                    jnp.where(lane == 0, 0.0, pltpu.roll(here, 1, axis=1)),
                )
                part_ref[c, i, 8 * f : 8 * f + 8, :] = jnp.where(valid, new, 0.0)
        pltpu.make_async_copy(part_ref.at[c], part_hbm.at[c], out_sem.at[c]).start()

        start = pl.multiple_of(EDGE_ROWS * c, 8)
        for f in range(2 * FIELDS + 1):
            if f < FIELDS:
                last, first = cell(ROWS - 1, f), cell(0, f)
            elif f < 2 * FIELDS:
                rows = slice(8 * (f - FIELDS), 8 * (f - FIELDS) + 8)
                last, first = part_ref[c, ROWS - 1, rows, :], part_ref[c, 0, rows, :]
            else:
                last, first = rate_of(ROWS - 1, 0), rate_of(0, 1)
            near_ref[pl.ds(start + 8 * f, 8), :] = jnp.where(valid & even, last, 0.0) + jnp.where(
                valid & odd, first, 0.0
            )
            far_ref[pl.ds(start + 8 * f, 8), :] = jnp.where(valid & even, first, 0.0) + jnp.where(
                valid & odd, last, 0.0
            )

        row = pl.multiple_of(8 * c, 8)
        last = pair_of(rate_of(ROWS - 1, 2), rate_of(ROWS - 1, 3))
        first = pair_of(rate_of(0, 2), rate_of(0, 3))
        spot = valid & (lane // 8 == 1)
        near_ref[pl.ds(EDGES + row, 8), :] = jnp.where(spot, jnp.where(even, last, first), 0.0)
        far_ref[pl.ds(EDGES + row, 8), :] = jnp.where(spot, jnp.where(even, first, last), 0.0)
        packer = ColumnPacker()
        for i in range(ROWS):
            for f in range(FIELDS):
                packer.add(i, f, cell(i, f))
        packer.store(cols_ref, row, valid)
        packer = ColumnPacker()
        for i in range(ROWS):
            for f in range(FIELDS):
                packer.add(i, f, part_ref[c, i, 8 * f : 8 * f + 8, :])
        packer.store(cols_ref, 64 + row, valid)
        for h in range(2):
            acc = zero
            for i in range(HALF):
                pair = pair_of(rate_of(HALF * h + i, 2), rate_of(HALF * h + i, 3))
                acc = jnp.where(lane // 8 == i, pair, acc)
            outer = rate_of(0, 1) if h == 0 else rate_of(ROWS - 1, 0)
            acc = jnp.where(lane // 8 == HALF, pair_of(outer, outer), acc)
            cols_ref[pl.ds(128 + row, 8), COLS * h : COLS * (h + 1)] = jnp.where(valid, acc, 0.0)
        return carry

    lax.fori_loop(0, CHUNKS, one_chunk, 0, unroll=2)
    for out, kept in ((near_out_ref, near_ref), (far_out_ref, far_ref)):
        out[...] = kept[...].astype(jnp.bfloat16)
    cols_out_ref[...] = cols_ref[...].astype(jnp.bfloat16)
    copies = copies_of(
        (cols_out_ref, near_out_ref, far_out_ref),
        (cols_hbm, near_hbm, far_hbm),
        edge_sem,
    )
    for copy in copies:
        copy.start()
    for c in range(CHUNKS):
        pltpu.make_async_copy(part_ref.at[c], part_hbm.at[c], out_sem.at[c]).wait()
    for copy in copies:
        copy.wait()


def merged_columns(even_y, core, chip):
    right = jnp.where(even_y, core, chip)
    left = jnp.where(even_y, chip, core)
    return jnp.where(
        lanes_of((8, COLS)) % 2 == 0,
        pltpu.roll(right, COLS - 1, axis=1),
        pltpu.roll(left, 1, axis=1),
    )


def corner_kernel(
    core_ref, chip_ref, near_in, far_in, near_hbm, far_hbm, near_ref, far_ref, sem
):
    corners_in = [given.at[pl.ds(EDGES, 64), :] for given in (near_in, far_in)]
    copies = copies_of(corners_in, (near_ref, far_ref), sem)
    for copy in copies:
        copy.start()
    even = is_even("bx")
    even_y = is_even("by")
    lane = lanes_of((8, COLS))
    core = core_ref[:64, :].astype(jnp.float32)
    chip = chip_ref[:64, :].astype(jnp.float32)
    for copy in copies:
        copy.wait()
    near_rates = near_ref[...].astype(jnp.float32)
    far_rates = far_ref[...].astype(jnp.float32)
    nears, fars = [], []
    for c in range(CHUNKS):
        rows = slice(8 * c, 8 * c + 8)
        cells, again = [], []
        for h in range(2):
            part = slice(COLS * h, COLS * (h + 1))
            beside = merged_columns(even_y, core[rows, part], chip[rows, part])
            back = 8 * (HALF - 1) * h
            cells.append(pltpu.roll(beside, (COLS - back) % COLS, axis=1))
            again.append(pltpu.roll(beside, (COLS + 8 - back) % COLS, axis=1))
        near = jnp.where(even, again[1], again[0]) * near_rates[rows]
        far = jnp.where(even, again[0], again[1]) * far_rates[rows]
        nears.append(jnp.where(lane < 8, jnp.where(even, cells[1], cells[0]), near))
        fars.append(jnp.where(lane < 8, jnp.where(even, cells[0], cells[1]), far))
    near_ref[...] = jnp.concatenate(nears, axis=0).astype(jnp.bfloat16)
    far_ref[...] = jnp.concatenate(fars, axis=0).astype(jnp.bfloat16)
    corners_out = [out.at[pl.ds(EDGES, 64), :] for out in (near_hbm, far_hbm)]
    copies = copies_of((near_ref, far_ref), corners_out, sem)
    for copy in copies:
        copy.start()
    for copy in copies:
        copy.wait()


def second_kernel(
    share,
    part_hbm,
    r_hbm,
    own_near_in,
    own_far_in,
    near_in,
    far_in,
    cols_in,
    core_in,
    chip_in,
    hot_hbm,
    hot_t_hbm,
    moved_hbm,
    stats_hbm,
    part_ref,
    r_ref,
    hot_ref,
    hot_t_ref,
    moved_ref,
    x_ref,
    hi_ref,
    lo_ref,
    own_near_ref,
    own_far_ref,
    near_ref,
    far_ref,
    cols_ref,
    core_ref,
    chip_ref,
    own_near_16,
    own_far_16,
    near_16,
    far_16,
    cols_16,
    core_16,
    chip_16,
    stats_ref,
    part_sem,
    r_sem,
    out_sem,
    hot_sem,
    edge_sem,
):
    edges_in = (own_near_in, own_far_in, near_in, far_in, cols_in, core_in, chip_in)
    edges_16 = (own_near_16, own_far_16, near_16, far_16, cols_16, core_16, chip_16)
    edges = (own_near_ref, own_far_ref, near_ref, far_ref, cols_ref, core_ref, chip_ref)
    edge_copies = copies_of(edges_in, edges_16, edge_sem)
    for copy in edge_copies:
        copy.start()
    part_copies = [
        pltpu.make_async_copy(part_hbm.at[c], part_ref.at[c], part_sem.at[c])
        for c in range(CHUNKS)
    ]
    r_copies = level_copies(r_hbm, r_ref, r_sem)
    for c in range(CHUNKS):
        part_copies[c].start()
        r_copies[c].start()
    hot_copies = copies_of((hot_hbm, hot_t_hbm), (hot_ref, hot_t_ref), hot_sem)
    for copy in hot_copies:
        copy.start()
    for copy, kept, given in zip(edge_copies, edges, edges_16, strict=True):
        copy.wait()
        kept[...] = given[...].astype(jnp.float32)
    lane = lanes_of((8, COLS))
    rim = (lane == 0) | (lane == COLS - 1)
    even = is_even("bx")
    even_y = is_even("by")

    def one_chunk(c, carry):
        valid = valid_rows(c)
        row = pl.multiple_of(8 * c, 8)
        start = pl.multiple_of(EDGE_ROWS * c, 8)
        wait_for(c, part_copies, r_copies)

        def edge(near, far, f, below):
            a, b = near[pl.ds(start + 8 * f, 8), :], far[pl.ds(start + 8 * f, 8), :]
            return jnp.where(even, a, b) if below else jnp.where(even, b, a)

        def rate_of(i, k):
            return r_ref[c, k, pl.ds(i, 8, stride=ROWS), :]

        corner = [near_ref[pl.ds(EDGES + row, 8), :], far_ref[pl.ds(EDGES + row, 8), :]]
        corner = [jnp.where(even, corner[1], corner[0]), jnp.where(even, corner[0], corner[1])]
        rings, gains = [], []
        for h in range(2):
            lanes = slice(COLS * h, COLS * (h + 1))
            cells, parts, rates = (
                merged_columns(
                    even_y,
                    core_ref[pl.ds(64 * k + row, 8), lanes],
                    chip_ref[pl.ds(64 * k + row, 8), lanes],
                )
                for k in range(3)
            )
            diagonal = corner[h]
            if h == 1:
                diagonal = pltpu.roll(diagonal, 8 * (HALF - 1), axis=1)
            shift = COLS - 8 * HALF if h == 0 else COLS - 8
            spot = lane // 8 == (0 if h == 0 else HALF - 1)
            extra = jnp.where(spot, pltpu.roll(rates, shift, axis=1) * diagonal, 0.0)
            rings.append(parts + rates * cols_ref[pl.ds(row, 8), lanes] + extra)
            gains.append(cols_ref[pl.ds(128 + row, 8), lanes] * cells)

        outer = []
        for side, i in enumerate((0, ROWS - 1)):
            down = side == 1
            rate = edge(near_ref, far_ref, 2 * FIELDS, down)
            tiles = []
            for f in range(FIELDS):
                turned = pltpu.roll(corner[side], COLS - (9 + 2 * f), axis=1)
                tiles.append(
                    edge(near_ref, far_ref, FIELDS + f, down)
                    + rate * edge(own_near_ref, own_far_ref, f, down)
                    + jnp.where(rim, turned, 0.0)
                )
            outer.append(tiles)

        for i in range(ROWS):
            for f in range(FIELDS):
                m = 4 * (i % HALF) + f
                turned = pltpu.roll(gains[i // HALF], COLS - (2 * m + 1), axis=1)
                tile = part_ref[c, i, 8 * f : 8 * f + 8, :] + jnp.where(rim, turned, 0.0)
                if i == 0:
                    tile = tile + rate_of(0, 1) * edge(near_ref, far_ref, f, False)
                if i == ROWS - 1:
                    tile = tile + rate_of(ROWS - 1, 0) * edge(near_ref, far_ref, f, True)
                part_ref[c, i, 8 * f : 8 * f + 8, :] = tile

        for i in range(ROWS):
            rate = [rate_of(i, k) for k in range(4)]
            kept = []
            for f in range(FIELDS):
                rows = slice(8 * f, 8 * f + 8)
                m = 4 * (i % HALF) + f
                here = part_ref[c, i, rows, :]
                above = outer[0][f] if i == 0 else part_ref[c, i - 1, rows, :]
                below = outer[1][f] if i == ROWS - 1 else part_ref[c, i + 1, rows, :]
                turned = pltpu.roll(rings[i // HALF], COLS - (2 * m + 1), axis=1)
                after = jnp.where(lane == COLS - 1, turned, pltpu.roll(here, COLS - 1, axis=1))
                before = jnp.where(lane == 0, turned, pltpu.roll(here, 1, axis=1))
                tile = jnp.where(valid, mixed(rate, here, below, above, after, before), 0.0)
                moved_ref[c, i, rows, :] = tile
                kept.append(tile)
            for f in (0, 2):
                both = jnp.concatenate(kept[f : f + 2], axis=0).astype(jnp.bfloat16)
                x_ref[pl.ds(pl.multiple_of(32 * c + 8 * f, 16), 16), COLS * i : COLS * (i + 1)] = (
                    both
                )
        pltpu.make_async_copy(moved_ref.at[c], moved_hbm.at[c], out_sem.at[c]).start()
        return carry

    lax.fori_loop(0, CHUNKS, one_chunk, 0)
    for copy in hot_copies:
        copy.wait()
    hot_t = hot_t_ref[...]
    sums = lax.dot_general(x_ref[...], hot_t, NN, preferred_element_type=jnp.float32)
    mean = sums * (1.0 / share)
    near_mean = mean.astype(jnp.bfloat16)
    for i in range(0, ROWS, 4):
        part = slice(COLS * i, COLS * (i + 4))
        centre = lax.dot_general(
            near_mean, hot_ref[:, part], NN, preferred_element_type=jnp.float32
        )
        away = x_ref[:, part].astype(jnp.float32) - centre
        square = away * away
        high = square.astype(jnp.bfloat16)
        hi_ref[:, part] = high
        lo_ref[:, part] = (square - high.astype(jnp.float32)).astype(jnp.bfloat16)
    spread = lax.dot_general(
        hi_ref[...], hot_t, NN, preferred_element_type=jnp.float32
    ) + lax.dot_general(lo_ref[...], hot_t, NN, preferred_element_type=jnp.float32)
    offset = mean - near_mean.astype(jnp.float32)
    spread = spread - share * (offset * offset)
    store_parts(stats_ref, (mean[:COLS].T, mean[COLS:].T, spread[:COLS].T, spread[COLS:].T))
    stats_copy = pltpu.make_async_copy(stats_ref, stats_hbm, hot_sem.at[0])
    stats_copy.start()
    for c in range(CHUNKS):
        pltpu.make_async_copy(moved_ref.at[c], moved_hbm.at[c], out_sem.at[c]).wait()
    stats_copy.wait()


def store_parts(ref, parts):
    for k, part in enumerate(parts):
        ref[pl.ds(k, part.shape[0], stride=4), :] = part


def load_parts(ref):
    return [ref[pl.ds(k, ref.shape[0] // 4, stride=4), :] for k in range(4)]


def batch_kernel(order_ref, owner_ref, batch_ref, hot_ref, hot_t_ref):
    order = order_ref[...]
    shape = (32, order.shape[1])
    high = lax.broadcasted_iota(jnp.int32, shape, 0) == order // COLS
    left = jnp.where(high, owner_ref[...], 0.0).astype(jnp.bfloat16)
    shape = (COLS, order.shape[1])
    low = lax.broadcasted_iota(jnp.int32, shape, 0) == order % COLS
    right = jnp.where(low, 1.0, 0.0).astype(jnp.bfloat16)
    found = lax.dot_general(left, right, NT, preferred_element_type=jnp.float32)
    batch = found[:ROWS].astype(jnp.int32)
    batch_ref[...] = batch
    groups = lax.broadcasted_iota(jnp.int32, (COLS, COLS), 0)
    for i in range(ROWS):
        tile = jnp.where(groups == batch[i : i + 1, :], 1.0, 0.0)
        hot_ref[:, COLS * i : COLS * (i + 1)] = tile.astype(jnp.bfloat16)
        hot_t_ref[COLS * i : COLS * (i + 1), :] = tile.T.astype(jnp.bfloat16)


def merge_kernel(share, stats_ref, gain_ref, out_ref):
    count = stats_ref.shape[0] // 4
    parts = load_parts(stats_ref)
    merged = []
    for k in range(2):
        mean = jnp.sum(parts[k], axis=0, keepdims=True) * (1.0 / count)
        away = parts[k] - mean
        total = jnp.sum(parts[k + 2] + share * (away * away), axis=0, keepdims=True)
        gain = gain_ref[:, COLS * k : COLS * (k + 1)]
        merged.append((mean, lax.rsqrt(total * (1.0 / (count * share)) + 1e-05) * gain))
    values = (merged[0][0], merged[1][0], merged[0][1], merged[1][1])
    store_parts(out_ref, [jnp.broadcast_to(v, (count, COLS)) for v in values])


def network_kernel(
    moved_hbm,
    batch_hbm,
    stats_hbm,
    shift_hbm,
    first_hbm,
    inner_hbm,
    last_hbm,
    bias_hbm,
    final_hbm,
    out_hbm,
    moved_ref,
    batch_ref,
    stats_ref,
    shift_ref,
    first_ref,
    inner_ref,
    last_ref,
    bias_ref,
    final_ref,
    out_ref,
    mean_ref,
    scale_ref,
    even_ref,
    odd_ref,
    moved_sem,
    weight_sem,
    out_sem,
):
    blocks = ROWS // BLOCK
    moved_copies = [
        pltpu.make_async_copy(
            moved_hbm.at[:, pl.ds(BLOCK * b, BLOCK)],
            moved_ref.at[:, pl.ds(BLOCK * b, BLOCK)],
            moved_sem.at[b],
        )
        for b in range(blocks)
    ]
    early_copies = copies_of(
        (stats_hbm, batch_hbm, shift_hbm), (stats_ref, batch_ref, shift_ref), weight_sem
    )
    weight_copies = copies_of(
        (first_hbm, bias_hbm, inner_hbm, last_hbm, final_hbm),
        (first_ref, bias_ref, inner_ref, last_ref, final_ref),
        weight_sem,
        3,
    )
    for copy in early_copies + moved_copies[:2] + weight_copies + moved_copies[2:]:
        copy.start()
    for copy in early_copies:
        copy.wait()
    parts = load_parts(stats_ref)
    for k in range(2):
        mean_ref[COLS * k : COLS * (k + 1), :] = parts[k].T
        scale_ref[COLS * k : COLS * (k + 1), :] = parts[k + 2].T
    out_rows = out_ref.reshape(FIELDS * LEVELS * ROWS, COLS)

    def dot(a, b):
        return lax.dot_general(a, b, NN, preferred_element_type=jnp.float32)

    def act(product, layer):
        t = product + bias_ref[layer : layer + 1, :]
        return (t + t * jnp.tanh(t)).astype(jnp.bfloat16)

    def normalize(block, normed_ref):
        mean, scale = mean_ref[...], scale_ref[...]
        for k in range(BLOCK):
            i = BLOCK * block + k
            index = jnp.broadcast_to(batch_ref[pl.ds(i, 1), :], (FEATS, COLS))
            x = moved_ref[:, i].reshape(FEATS, COLS).astype(jnp.bfloat16).astype(jnp.float32)
            away = x - jnp.take_along_axis(mean, index, axis=1)
            tile = away * jnp.take_along_axis(scale, index, axis=1)
            normed_ref[COLS * k : COLS * (k + 1), :] = (tile.T + shift_ref[...]).astype(
                jnp.bfloat16
            )

    def layers(block, normed_ref):
        hidden = act(dot(normed_ref[...], first_ref[...]), 0)
        for layer in range(3):
            hidden = act(dot(hidden, inner_ref[layer]), layer + 1)
        tendency = dot(hidden, last_ref[...]) + final_ref[...]
        tendency = tendency.astype(jnp.bfloat16).astype(jnp.float32)
        for k in range(BLOCK):
            i = BLOCK * block + k
            change = tendency[COLS * k : COLS * (k + 1), :].T
            for chunk in range(CHUNKS):
                rows = min(8, LEVELS - 8 * chunk)
                for f in range(FIELDS):
                    row = 32 * chunk + 8 * f
                    new = moved_ref[chunk, i, 8 * f : 8 * f + rows, :] + change[row : row + rows]
                    start = (LEVELS * f + 8 * chunk) * ROWS + i
                    out_rows[pl.ds(start, rows, stride=ROWS), :] = new

    def out_copy(group):
        part = pl.ds(pl.multiple_of(8 * group, 8), 8)
        return pltpu.make_async_copy(
            out_ref.at[:, part, :], out_hbm.at[:, part, :], out_sem.at[group]
        )

    moved_copies[0].wait()
    normalize(0, even_ref)
    for copy in weight_copies:
        copy.wait()

    def two_blocks(group, carry):
        block = 2 * group
        for b in range(1, blocks):

            @pl.when(block == (b - 1) // 2 * 2)
            def _(b=b):
                moved_copies[b].wait()

        normalize(block + 1, odd_ref)
        layers(block, even_ref)
        normalize(jnp.minimum(block + 2, blocks - 1), even_ref)
        layers(block + 1, odd_ref)
        out_copy(group).start()
        return carry

    lax.fori_loop(0, blocks // 2, two_blocks, 0)
    for group in range(blocks // 2):
        out_copy(group).wait()


BLOCK = 4
EDGE_ROWS = 8 * (2 * FIELDS + 1)
EDGES = CHUNKS * EDGE_ROWS
VMEM_SPEC = pl.BlockSpec(memory_space=pltpu.VMEM)
HBM_SPEC = pl.BlockSpec(memory_space=pltpu.HBM)
GRID_SHAPE = (CHUNKS, ROWS, 32, COLS)
LEVEL_SHAPE = (CHUNKS, 4, 8 * ROWS, COLS)


def f32(*shape):
    return jax.ShapeDtypeStruct(shape, jnp.float32)


def bf16(*shape):
    return jax.ShapeDtypeStruct(shape, jnp.bfloat16)


def cost(flops, size):
    return pl.CostEstimate(flops=flops, bytes_accessed=size, transcendentals=0)


def swap(values, axis, first):
    count = lax.axis_size(axis)
    step = 0 if first else 1
    pairs = [((i + step) % count, (i + 1 + step) % count) for i in range(0, count, 2)]
    return lax.ppermute(values, axis, pairs + [(b, a) for a, b in pairs])


def by_row(values):
    rest = values.shape[1:]
    values = values.reshape(FIELDS, LEVELS, *rest)
    values = jnp.pad(values, ((0, 0), (0, 64 - LEVELS)) + ((0, 0),) * len(rest))
    values = values.reshape(FIELDS, CHUNKS, 8, *rest).swapaxes(0, 1)
    return values.reshape(FEATS, *rest)


def body(
    tracers,
    rates,
    column_order,
    norm_gain,
    norm_shift,
    weight_first,
    weight_hidden,
    weight_last,
    bias_hidden,
    bias_last,
):
    count = lax.axis_size("bx") * lax.axis_size("by")
    columns = ROWS * COLS
    share = columns // count
    width = weight_first.shape[0]
    x = tracers.reshape(FIELDS, LEVELS * ROWS, COLS)
    r = rates.reshape(4, LEVELS * ROWS, COLS)

    dma = pltpu.SemaphoreType.DMA
    part, near, far, cols = pl.pallas_call(
        first_kernel,
        in_specs=[HBM_SPEC, HBM_SPEC],
        out_specs=[HBM_SPEC] * 4,
        out_shape=[
            f32(*GRID_SHAPE),
            bf16(EDGES + 64, COLS),
            bf16(EDGES + 64, COLS),
            bf16(3 * 64, 2 * COLS),
        ],
        scratch_shapes=[
            pltpu.VMEM(LEVEL_SHAPE, jnp.float32),
            pltpu.VMEM(LEVEL_SHAPE, jnp.float32),
            pltpu.VMEM(GRID_SHAPE, jnp.float32),
            pltpu.VMEM((EDGES + 64, COLS), jnp.float32),
            pltpu.VMEM((EDGES + 64, COLS), jnp.float32),
            pltpu.VMEM((3 * 64, 2 * COLS), jnp.float32),
            pltpu.VMEM((EDGES + 64, COLS), jnp.bfloat16),
            pltpu.VMEM((EDGES + 64, COLS), jnp.bfloat16),
            pltpu.VMEM((3 * 64, 2 * COLS), jnp.bfloat16),
            dma((CHUNKS,)),
            dma((CHUNKS,)),
            dma((CHUNKS,)),
            dma((3,)),
        ],
        compiler_params=params(62),
        cost_estimate=cost(10**7, 9 * 10**6),
        name="first_substep",
    )(x, r)
    core = swap(cols, "by", True)
    chip = swap(cols, "by", False)
    near, far = pl.pallas_call(
        corner_kernel,
        in_specs=[VMEM_SPEC, VMEM_SPEC, HBM_SPEC, HBM_SPEC],
        out_specs=[HBM_SPEC] * 2,
        out_shape=[bf16(EDGES + 64, COLS), bf16(EDGES + 64, COLS)],
        scratch_shapes=[
            pltpu.VMEM((64, COLS), jnp.bfloat16),
            pltpu.VMEM((64, COLS), jnp.bfloat16),
            dma((2,)),
        ],
        input_output_aliases={2: 0, 3: 1},
        compiler_params=params(16),
        cost_estimate=cost(10**5, 10**6),
        name="corners",
    )(core, chip, near, far)
    near_in = swap(near, "bx", True)
    far_in = swap(far, "bx", False)

    owner = (jnp.arange(columns, dtype=jnp.int32) // share).astype(jnp.float32)[None, :]
    batch, hot, hot_t = pl.pallas_call(
        batch_kernel,
        in_specs=[VMEM_SPEC, VMEM_SPEC],
        out_specs=[VMEM_SPEC, VMEM_SPEC, VMEM_SPEC],
        out_shape=[
            jax.ShapeDtypeStruct((ROWS, COLS), jnp.int32),
            jax.ShapeDtypeStruct((COLS, columns), jnp.bfloat16),
            jax.ShapeDtypeStruct((columns, COLS), jnp.bfloat16),
        ],
        compiler_params=params(62),
        cost_estimate=cost(10**9, 2 * 10**6),
        name="batch_ids",
    )(column_order, owner)

    moved, stats = pl.pallas_call(
        functools.partial(second_kernel, share),
        in_specs=[HBM_SPEC] * 11,
        out_specs=[HBM_SPEC] * 2,
        out_shape=[f32(*GRID_SHAPE), f32(4 * count, COLS)],
        scratch_shapes=[
            pltpu.VMEM(GRID_SHAPE, jnp.float32),
            pltpu.VMEM(LEVEL_SHAPE, jnp.float32),
            pltpu.VMEM((COLS, columns), jnp.bfloat16),
            pltpu.VMEM((columns, COLS), jnp.bfloat16),
            pltpu.VMEM(GRID_SHAPE, jnp.float32),
            pltpu.VMEM((FEATS, columns), jnp.bfloat16),
            pltpu.VMEM((FEATS, columns), jnp.bfloat16),
            pltpu.VMEM((FEATS, columns), jnp.bfloat16),
            *[pltpu.VMEM((EDGES + 64, COLS), jnp.float32) for _ in range(4)],
            *[pltpu.VMEM((3 * 64, 2 * COLS), jnp.float32) for _ in range(3)],
            *[pltpu.VMEM((EDGES + 64, COLS), jnp.bfloat16) for _ in range(4)],
            *[pltpu.VMEM((3 * 64, 2 * COLS), jnp.bfloat16) for _ in range(3)],
            pltpu.VMEM((4 * count, COLS), jnp.float32),
            dma((CHUNKS,)),
            dma((CHUNKS,)),
            dma((CHUNKS,)),
            dma((2,)),
            dma((7,)),
        ],
        compiler_params=params(62),
        cost_estimate=cost(10**9, 9 * 10**6),
        name="second_substep",
    )(
        part,
        r,
        near,
        far,
        near_in,
        far_in,
        cols,
        core,
        chip,
        hot,
        hot_t,
    )

    stats, *raw = lax.optimization_barrier(
        (
            stats,
            norm_gain,
            norm_shift,
            weight_first,
            weight_hidden,
            weight_last,
            bias_hidden,
            bias_last,
        )
    )
    norm_gain, norm_shift, weight_first, weight_hidden, weight_last, bias_hidden, bias_last = raw
    gathered = lax.all_to_all(stats, ("bx", "by"), split_axis=0, concat_axis=0, tiled=True)
    merged = pl.pallas_call(
        functools.partial(merge_kernel, float(share)),
        in_specs=[VMEM_SPEC, VMEM_SPEC],
        out_specs=VMEM_SPEC,
        out_shape=jax.ShapeDtypeStruct((4 * count, COLS), jnp.float32),
        compiler_params=params(16),
        cost_estimate=cost(10**6, 10**6),
        name="merge_statistics",
    )(gathered, by_row(norm_gain)[None, :])
    known = lax.all_to_all(merged, ("bx", "by"), split_axis=0, concat_axis=0, tiled=True)

    half = jnp.bfloat16(0.5)
    new = pl.pallas_call(
        network_kernel,
        in_specs=[HBM_SPEC] * 9,
        out_specs=HBM_SPEC,
        out_shape=f32(FIELDS * LEVELS, ROWS, COLS),
        scratch_shapes=[
            pltpu.VMEM(GRID_SHAPE, jnp.float32),
            pltpu.VMEM((ROWS, COLS), jnp.int32),
            pltpu.VMEM((4 * count, COLS), jnp.float32),
            pltpu.VMEM((1, FEATS), jnp.float32),
            pltpu.VMEM((FEATS, width), jnp.bfloat16),
            pltpu.VMEM((3, width, width), jnp.bfloat16),
            pltpu.VMEM((width, FEATS), jnp.bfloat16),
            pltpu.VMEM((4, width), jnp.float32),
            pltpu.VMEM((1, FEATS), jnp.float32),
            pltpu.VMEM((FIELDS * LEVELS, ROWS, COLS), jnp.float32),
            pltpu.VMEM((FEATS, COLS), jnp.float32),
            pltpu.VMEM((FEATS, COLS), jnp.float32),
            pltpu.VMEM((BLOCK * COLS, FEATS), jnp.bfloat16),
            pltpu.VMEM((BLOCK * COLS, FEATS), jnp.bfloat16),
            dma((ROWS // BLOCK,)),
            dma((8,)),
            dma((3,)),
        ],
        compiler_params=params(62),
        cost_estimate=cost(6 * 10**9, 9 * 10**6),
        name="network",
    )(
        moved,
        batch,
        known,
        by_row(norm_shift)[None, :],
        by_row(weight_first.T) * half,
        weight_hidden.swapaxes(1, 2) * half,
        by_row(weight_last).T,
        bias_hidden * 0.5,
        by_row(bias_last)[None, :],
    )
    return new.reshape(tracers.shape)


def solution(mesh):
    placed = (
        P(None, None, "bx", "by"),
        P(None, None, "bx", "by"),
        P(("bx", "by"), None),
        P(),
        P(),
        P(),
        P(),
        P(),
        P(),
        P(),
    )
    return jax.shard_map(
        body, mesh=mesh, in_specs=placed, out_specs=P(None, None, "bx", "by"), check_vma=False
    )
```
